128 devices in a mesh: dp: 2 (over core), ctx: 64 (over x, z, y).
Axes of the slice: x: 4, y: 4, z: 4, core: 2. Of those that a mesh axis runs over, the one named last changes fastest.
Arguments:
- text_values: bfloat16 [32768, 4096], P(('dp', 'ctx')), parts along dimension 0, may hold values from -6 to 6
- text_gate: bfloat16 [32768, 4096], P(('dp', 'ctx')), parts along dimension 0, may hold values from -6 to 6
- text_proj: bfloat16 [32768, 1024], P(('dp', 'ctx')), parts along dimension 0, may hold values from -6 to 6
- text_step: bfloat16 [32768, 64], P(('dp', 'ctx')), parts along dimension 0
- tile_values: bfloat16 [8192, 4096], P(('dp', 'ctx')), parts along dimension 0, may hold values from -6 to 6
- tile_gate: bfloat16 [8192, 4096], P(('dp', 'ctx')), parts along dimension 0, may hold values from -6 to 6
- tile_proj: bfloat16 [8192, 1024], P(('dp', 'ctx')), parts along dimension 0, may hold values from -6 to 6
- tile_step: bfloat16 [8192, 64], P(('dp', 'ctx')), parts along dimension 0
- tile_position: int32 [8192], P('dp'), parts along dimension 0, may hold values from 0 to 16383, as said below
- tile_count: int32 [128], P('dp'), parts along dimension 0, may hold values from 32 to 64
- conv_weight: float32 [4, 5120], replicated, may hold values from -3 to 3
- conv_bias: float32 [5120], replicated, may hold values from -3 to 3
- step_bias: float32 [64], replicated, may hold values from -0.5 to 0.5
- decay_log: float32 [64], replicated
- skip_gain: float32 [64], replicated, may hold values from 0.5 to 1.5
- norm_gain: float32 [4096], replicated, may hold values from 0.5 to 1.5
Outputs:
- mixer_out: bfloat16 [32768, 4096], P(('dp', 'ctx')), parts along dimension 0
The draws below stay inside these ranges and needn't reach their ends.
There are 2 independent parts, one for each index of `dp`. The reference program is written for one: setup_inputs(seed, part) draws one part's arguments, and reference() takes and returns one part's arrays. A program takes and returns all parts, laid end to end along the dimension named above; an argument that names none is the same for every part. Nothing has to cross between parts.
Inputs may be any that keep to these rules, and one draw needn't show every extreme that they name: `tile_position`: positions of the tile rows are distinct over all rows. The 64 rows of one encoder device go in order, 2 at a time, to 32 different devices, so at most 2 rows of one encoder device land on one device's 256 positions; the rows that land on one device fill one run of consecutive positions, ordered by source device.
All inputs are finite; a program needn't handle non-finite values.
Results may differ from the reference program's by a relative error of at most 0.0095.
Values may be sent and summed in bfloat16 or wider, within the bound.
No kernel may reach another device: no remote copies, remote signals or barrier semaphores. Data moves between devices by JAX's collectives and lax.ppermute only.
A program may use at most 320 MiB of HBM per device.

```python
import jax
import jax.numpy as jnp
from jax import lax

H = 64
P_SIZE = 64
N = 64
G = 8
SPAN = 128
KCONV = 4
CAP = 2
TOK_DEV = 256
E = 4096
STREAM_SLOTS = 16384
TILE_DEV = 64
TILES = 4096


def loguniform_draw(key, shape, low, high):
    return jnp.exp(jax.random.uniform(key, shape, jnp.float32, jnp.log(low), jnp.log(high)))


def inverse_softplus(quantized_grades):
    return quantized_grades + jnp.log(-jnp.expm1(-quantized_grades))


def draw_text_step(key, part):
    key = jax.random.fold_in(key, 11)
    key_rough, key_device, key_spots, key_strength = jax.random.split(key, 4)
    rough_guess = loguniform_draw(key_rough, (STREAM_SLOTS, H), 0.6, 1.6)
    worker_fraction = jnp.repeat(loguniform_draw(key_device, (STREAM_SLOTS // TOK_DEV, 1), 0.6, 1.6), TOK_DEV, axis=0)
    picked_indices = jax.random.randint(key_spots, (3,), 0, STREAM_SLOTS)
    input_magnitude = jax.random.uniform(key_strength, (STREAM_SLOTS, 1), jnp.float32, 1.0, 2.0) * (0.02 * STREAM_SLOTS)
    spike_magnitude = jnp.any(jnp.arange(STREAM_SLOTS)[:, None] == picked_indices[None, :], axis=1)[:, None]
    quantized_grades = jnp.where(spike_magnitude, input_magnitude, 0.02 * rough_guess * worker_fraction)
    return inverse_softplus(quantized_grades).astype(jnp.bfloat16)


def draw_tile_step(key, part):
    key = jax.random.fold_in(key, 12)
    quantized_grades = 0.02 * loguniform_draw(key, (TILES, H), 0.6, 1.6)
    return inverse_softplus(quantized_grades).astype(jnp.bfloat16)


def draw_decay_log(key, part):
    key = jax.random.fold_in(key, 13)
    key_pick, key_slow, key_fast = jax.random.split(key, 3)
    share = 0.5
    fast_heads = jax.random.uniform(key_pick, (H,), jnp.float32) < share
    slow_rate = 1.0 / (STREAM_SLOTS * 0.02 * loguniform_draw(key_slow, (H,), 4.0, 10.0))
    fast_rate = 1.0 / (0.02 * loguniform_draw(key_fast, (H,), 25.0, 50.0))
    return jnp.log(jnp.where(fast_heads, fast_rate, slow_rate)).astype(jnp.float32)


def draw_tile_position(key, part):
    key = jax.random.fold_in(key, 21)
    devices = STREAM_SLOTS // TOK_DEV
    groups = TILE_DEV // CAP
    key_star, key_perm, key_offset = jax.random.split(key, 3)
    chosen = jax.random.randint(key_star, (), 0, devices)
    orders = jax.vmap(lambda one_key: jax.random.permutation(one_key, devices))(jax.random.split(key_perm, devices))
    scored = jnp.where(orders == chosen, -1, jnp.arange(devices)[None, :])
    moved = jnp.argsort(scored, axis=1, stable=True)
    targets = jnp.take_along_axis(orders, moved[:, :groups], axis=1)
    member = jnp.any(targets[:, :, None] == jnp.arange(devices)[None, None, :], axis=1).astype(jnp.int32)
    before = jnp.cumsum(member, axis=0) - member
    received = jnp.sum(member, axis=0) * CAP
    start = jax.random.randint(key_offset, (devices,), 0, TOK_DEV - received + 1)
    rank_here = jnp.take_along_axis(before, targets, axis=1)
    local_row = start[targets] + CAP * rank_here
    position = targets[:, :, None] * TOK_DEV + local_row[:, :, None] + jnp.arange(CAP)[None, None, :]
    return position.reshape(TILES).astype(jnp.int32)


def draw_tile_count(key, part):
    key = jax.random.fold_in(key, 22)
    devices = STREAM_SLOTS // TOK_DEV
    key_counts, key_full = jax.random.split(key)
    counts = jax.random.randint(key_counts, (devices,), TILE_DEV // 2, TILE_DEV + 1)
    full_device = jax.random.randint(key_full, (), 0, devices)
    return jnp.where(jnp.arange(devices) == full_device, TILE_DEV, counts).astype(jnp.int32)


def shard_levels(rng, dims, shards, low, largest):
    def one(dim, parts):
        heights = jax.random.uniform(jax.random.fold_in(jax.random.fold_in(rng, 6), dim), (parts,), jnp.float32, low / len(shards), largest / len(shards))
        return jnp.repeat(jnp.exp(heights), dims[dim] // parts).reshape((-1,) + (1,) * (len(dims) - dim - 1))

    gain = one(*shards[0])
    for cut in shards[1:]:
        gain = gain * one(*cut)
    return gain


def scatter_about(stream_key, dims, deviation, limit, cuts=(), held_as=jnp.bfloat16):
    loudness = shard_levels(stream_key, dims, cuts, -0.22, 0.18) if cuts else 1.0
    drawn = jax.random.normal(stream_key, dims, jnp.float32) * deviation * loudness
    return jnp.minimum(jnp.maximum(drawn, -limit), limit).astype(held_as)


def setup_inputs(seed: int = 0, part: int = 0) -> dict:
    seeds = jax.random.split(jax.random.key(seed), 17)
    own_keys = jax.random.split(jax.random.fold_in(seeds[16], part), 17)
    return {
        "text_values": scatter_about(own_keys[0], (STREAM_SLOTS, E), 1.0, 6.0, ((0, 64),)),
        "text_gate": scatter_about(own_keys[1], (STREAM_SLOTS, E), 1.0, 6.0, ((0, 64),)),
        "text_proj": scatter_about(own_keys[2], (STREAM_SLOTS, 2 * G * N), 1.0, 6.0, ((0, 64),)),
        "text_step": draw_text_step(jax.random.fold_in(jax.random.fold_in(seeds[16], part), 71), part),
        "tile_values": scatter_about(own_keys[4], (TILES, E), 1.0, 6.0, ((0, 64),)),
        "tile_gate": scatter_about(own_keys[5], (TILES, E), 1.0, 6.0, ((0, 64),)),
        "tile_proj": scatter_about(own_keys[6], (TILES, 2 * G * N), 1.0, 6.0, ((0, 64),)),
        "tile_step": draw_tile_step(jax.random.fold_in(jax.random.fold_in(seeds[16], part), 71), part),
        "tile_position": draw_tile_position(jax.random.fold_in(jax.random.fold_in(seeds[16], part), 71), part),
        "tile_count": draw_tile_count(jax.random.fold_in(jax.random.fold_in(seeds[16], part), 71), part),
        "conv_weight": scatter_about(seeds[10], (KCONV, E + 2 * G * N), KCONV ** -0.5, 3.0, (), jnp.float32),
        "conv_bias": scatter_about(seeds[11], (E + 2 * G * N,), 0.5, 3.0, (), jnp.float32),
        "step_bias": jnp.clip(jax.random.uniform(seeds[12], (H,), jnp.float32, -0.5, 0.5), -0.5, 0.5),
        "decay_log": draw_decay_log(jax.random.fold_in(seeds[16], 71), part),
        "skip_gain": jnp.clip(jax.random.uniform(seeds[14], (H,), jnp.float32, 0.5, 1.5), 0.5, 1.5),
        "norm_gain": jnp.clip(1.0 + 0.1 * jax.random.normal(seeds[15], (E,), jnp.float32), 0.5, 1.5),
    }


highest = lax.Precision.HIGHEST

def causal_conv(row_data, lead_rows, weights, bias_row):
    extended = jnp.concatenate([lead_rows, row_data], axis=0).astype(jnp.float32)
    length = row_data.shape[0]
    running_sum = jnp.zeros((length, row_data.shape[1]), jnp.float32) + bias_row[None, :]
    for offset in range(KCONV):
        running_sum = running_sum + weights[offset][None, :] * extended[offset:offset + length]
    return jax.nn.silu(running_sum).astype(jnp.bfloat16)

def gated_norm(mixed, gate_rows, gain_row):
    gated = mixed * jax.nn.silu(gate_rows.astype(jnp.float32))
    length = gated.shape[0]
    grouped = gated.reshape(length, G, E // G)
    scale = lax.rsqrt(lax.optimization_barrier(jnp.mean(grouped * grouped, axis=-1, keepdims=True)) + 1e-05)
    return ((grouped * scale).reshape(length, E) * gain_row[None, :]).astype(jnp.bfloat16)

def reference(text_values, text_gate, text_proj, text_step, tile_values, tile_gate, tile_proj, tile_step, tile_position, tile_count, conv_weight, conv_bias, step_bias, decay_log, skip_gain, norm_gain):
    row_index = jnp.arange(TILES, dtype=jnp.int32)
    source = row_index // TILE_DEV
    real_row = row_index % TILE_DEV < tile_count[source]
    target = jnp.where(real_row, tile_position, STREAM_SLOTS).astype(jnp.int32)
    values_in = text_values.at[target].set(tile_values, mode='drop')
    gate_in = text_gate.at[target].set(tile_gate, mode='drop')
    proj_in = text_proj.at[target].set(tile_proj, mode='drop')
    step_in = text_step.at[target].set(tile_step, mode='drop')
    values_conv = causal_conv(values_in, jnp.zeros((KCONV - 1, E), jnp.bfloat16), conv_weight[:, :E], conv_bias[:E])
    proj_conv = causal_conv(proj_in, jnp.zeros((KCONV - 1, 2 * G * N), jnp.bfloat16), conv_weight[:, E:], conv_bias[E:])
    step_size = jax.nn.softplus(step_in.astype(jnp.float32) + step_bias[None, :])
    log_decay = step_size * (-jnp.exp(decay_log))[None, :]
    blocks = STREAM_SLOTS // SPAN
    value_blocks = values_conv.reshape(blocks, SPAN, H, P_SIZE)
    input_blocks = proj_conv[:, :G * N].reshape(blocks, SPAN, G, N)
    output_blocks = proj_conv[:, G * N:].reshape(blocks, SPAN, G, N)
    step_blocks = step_size.reshape(blocks, SPAN, H)
    decay_blocks = log_decay.reshape(blocks, SPAN, H)
    causal = jnp.arange(SPAN)[:, None] >= jnp.arange(SPAN)[None, :]

    def advance(state, current):
        value_blk, input_blk, output_blk, step_blk, decay_blk = current
        values_f = value_blk.astype(jnp.float32)
        input_f = input_blk.astype(jnp.float32)
        output_f = output_blk.astype(jnp.float32)
        cum_decay = jnp.cumsum(decay_blk, axis=0)
        weighted = values_f * step_blk[:, :, None]
        group_scores = jnp.einsum('ign,jgn->gij', output_blk, input_blk, preferred_element_type=jnp.float32)
        scores = jnp.repeat(group_scores, H // G, axis=0)
        cum_heads = cum_decay.T
        differ = cum_heads[:, :, None] - cum_heads[:, None, :]
        kernel = jnp.where(causal[None], jnp.exp(jnp.where(causal[None], differ, 0.0)), 0.0)
        diagonal = jnp.einsum('hij,jhp->ihp', kernel * scores, weighted, precision=highest)
        input_heads = jnp.repeat(input_f, H // G, axis=1)
        output_heads = jnp.repeat(output_f, H // G, axis=1)
        offdiag = jnp.einsum('ihn,hnp->ihp', output_heads, state, precision=highest) * jnp.exp(cum_decay)[:, :, None]
        tail_weight = jnp.exp(cum_decay[-1][None, :] - cum_decay)
        new_state = state * jnp.exp(cum_decay[-1])[:, None, None] + jnp.einsum('jhn,jhp->hnp', input_heads * tail_weight[:, :, None], weighted, precision=highest)
        mixed = diagonal + offdiag + skip_gain[None, :, None] * values_f
        return (new_state, mixed)
    final_state, mixed = lax.scan(advance, jnp.zeros((H, N, P_SIZE), jnp.float32), (value_blocks, input_blocks, output_blocks, step_blocks, decay_blocks))
    return gated_norm(mixed.reshape(STREAM_SLOTS, E), gate_in, norm_gain)
```

```python
import functools

import jax
import jax.numpy as jnp
from jax import lax
from jax.experimental import pallas as pl
from jax.experimental.pallas import tpu as pltpu
from jax.sharding import PartitionSpec as P

H = 64
P_SIZE = 64
N = 64
G = 8
SPAN = 128
KCONV = 4
E = 4096
TOK = 256
TILE = 64
DEVS = 64
GW = E // G
PW = 2 * G * N
EDGE = 16
LANES = 128
QUART = 4
V_AT, G_AT, P_AT, S_AT = 0, 1024, 2048, 2304
CHUNK = 2432
STATE_W = GW + LANES

f32 = jnp.float32
bf16 = jnp.bfloat16
MIB = 1024 * 1024
VMEM_MIB = 32


def cost(flops, size, trans=0):
    return pl.CostEstimate(flops=flops, bytes_accessed=size, transcendentals=trans)


def whole(shape):
    return pl.BlockSpec(shape, lambda *_: (0,) * len(shape))


def group_cols(g):
    return pl.ds(pl.multiple_of(g * GW, GW), GW)


def iota(shape, dim):
    return lax.broadcasted_iota(jnp.int32, shape, dim)


def dot(a, b):
    return jnp.dot(a, b, preferred_element_type=f32)


def dot_rows(a, b):
    return lax.dot_general(a, b, (((0,), (0,)), ((), ())), preferred_element_type=f32)


def dot_cols(a, b):
    return lax.dot_general(a, b, (((1,), (1,)), ((), ())), preferred_element_type=f32)


def dot_whole(a, b):
    high = b.astype(bf16)
    low = (b - high.astype(f32)).astype(bf16)
    return dot(jnp.concatenate([a, a], axis=1), jnp.concatenate([high, low], axis=0))


def silu(x):
    half = 0.5 * x
    return half + half * jnp.tanh(half)


def split2(x):
    high = x.astype(bf16)
    low = (x - high.astype(f32)).astype(bf16)
    return jnp.where(iota(x.shape, 1) < H, high.astype(f32), low.astype(f32)).astype(bf16)


def expander(group):
    head = iota((LANES, GW), 0) & (H - 1)
    col = group * (H // G) + (iota((LANES, GW), 1) >> 6)
    return jnp.where(head == col, 1.0, 0.0).astype(bf16)


def pack_kernel(
    dev_ref, pos_ref, step_ref, val_hbm, gate_hbm, proj_hbm, out_hbm,
    val_ref, gate_ref, proj_ref, out_ref, in_sem, out_sem,
):
    loads = [
        pltpu.make_async_copy(src, dst, in_sem.at[i])
        for i, (src, dst) in enumerate(((val_hbm, val_ref), (gate_hbm, gate_ref), (proj_hbm, proj_ref)))
    ]
    for load in loads:
        load.start()
    dev = dev_ref[0]
    row = pos_ref[pl.ds(dev // 2, 1), :]
    other = pltpu.roll(row, 64, 1)
    lane = iota((1, LANES), 1)
    own = jnp.where((lane >> 6) == lax.rem(dev, 2), row, other)
    key = (own >> 8) * 8 + (lane & 1) * QUART + (lane >> 6)
    keys = jnp.concatenate([key, key + 2], axis=1)
    pick = jnp.where(iota((DEVS * 8, 2 * LANES), 0) == keys, 1.0, 0.0).astype(bf16)
    step = step_ref[...]
    out_ref[:, S_AT:] = dot(pick[:, :TILE], jnp.concatenate([step, step], axis=1)).astype(bf16)
    stores = []
    for i, (ref, at, width, part) in enumerate(
        ((val_ref, V_AT, 1024, 512), (gate_ref, G_AT, 1024, 512), (proj_ref, P_AT, 256, 256))
    ):
        loads[i].wait()
        for low in range(0, width, part):
            rows = [ref[:, b * width + low : b * width + low + part] for b in range(QUART)]
            out_ref[:, at + low : at + low + part] = dot(pick, jnp.concatenate(rows, axis=0)).astype(bf16)
            end = at + low + part if i < 2 else CHUNK
            cols = slice(at + low, end)
            store = pltpu.make_async_copy(out_ref.at[:, cols], out_hbm.at[:, cols], out_sem.at[len(stores)])
            store.start()
            stores.append(store)
    for store in stores:
        store.wait()


def rim_kernel(slot_ref, recv_ref, val_ref, proj_ref, out_ref):
    count = KCONV - 1
    slots = [slot_ref[i] for i in range(count)]
    starts = [jnp.maximum(k, 0) * QUART for k in slots]
    rows = [recv_ref[pl.ds(pl.multiple_of((k >> 4) * 16, 16), 16), :] for k in starts]
    rows = jnp.concatenate(rows, axis=0)
    row, col = iota((EDGE, 16 * count), 0), iota((EDGE, 16 * count), 1)
    at = jnp.full((EDGE, 16 * count), -16, jnp.int32)
    taken = jnp.full((EDGE, 1), -1, jnp.int32)
    for i, k in enumerate(starts):
        at = jnp.where(row == EDGE - count + i, 16 * i + (k & 15), at)
        taken = jnp.where(iota((EDGE, 1), 0) == EDGE - count + i, slots[i], taken)
    for b in range(QUART):
        place = jnp.where(col == at + b, 1.0, 0.0).astype(bf16)
        tile = dot(place, rows[:, V_AT:G_AT])
        cols = slice(b * 1024, (b + 1) * 1024)
        out_ref[:, cols] = jnp.where(taken >= 0, tile, val_ref[:, cols].astype(f32)).astype(bf16)
        tile = dot(place, rows[:, P_AT:S_AT])
        cols = slice(b * 256, (b + 1) * 256)
        out_ref[:, E + b * 256 : E + (b + 1) * 256] = jnp.where(
            taken >= 0, tile, proj_ref[:, cols].astype(f32)
        ).astype(bf16)


def placement(at_ref):
    return jnp.where(iota((TOK, LANES), 0) == at_ref[...], 1.0, 0.0).astype(bf16)


def spread_out(recv, wide_ref):
    for k in range(recv.shape[1] // LANES):
        wide_ref[k] = recv[:, k * LANES : (k + 1) * LANES].astype(f32)


def quarter_rows(wide_ref, b, count):
    rows = [wide_ref[k, pl.ds(b, 2 * DEVS, stride=QUART), :] for k in range(count)]
    return jnp.concatenate(rows, axis=1).astype(bf16)


def conv_chunk(x, before, weights, bias):
    ext = jnp.concatenate([before, x], axis=0)
    total = bias + weights[KCONV - 1 : KCONV, :] * x
    for back in range(1, KCONV):
        total = total + weights[KCONV - 1 - back : KCONV - back, :] * pltpu.roll(ext, back, 0)[8:]
    return silu(total).astype(bf16)


CHUNK_ROWS = 64


def conv_columns(tile_ref, text_ref, taken_ref, cols, weights, bias, use):
    before = jnp.zeros((8, LANES), f32)
    for low in range(0, TOK, CHUNK_ROWS):
        rows = slice(low, low + CHUNK_ROWS)
        x = jnp.where(taken_ref[rows, :] > 0, tile_ref[rows, cols], text_ref[rows, cols].astype(f32))
        use(rows, x, conv_chunk(x, before, weights, bias))
        before = x[CHUNK_ROWS - 8 :]


def softplus(v):
    return jnp.maximum(v, 0.0) + jnp.log1p(jnp.exp(-jnp.abs(v)))


def three(x):
    a = x.astype(bf16)
    left = x - a.astype(f32)
    b = left.astype(bf16)
    return a, b, (left - b.astype(f32)).astype(bf16)


def order(i):
    return lax.rem(i, G // 2) * 2 + i // (G // 2)


def place_kernel(
    recv_hbm, val_hbm, proj_hbm, at_ref, step_ref, w_ref, b_ref, sbias_ref, dlog_ref,
    conv_hbm, in_hbm, out_hbm, state_ref, cum_ref, size_ref, total_ref, hv_ref, hp_ref, we_ref,
    recv_ref, val_ref, proj_ref, conv_ref, in_ref, out_ref, place_scr, taken_scr, wide_scr, tail_scr,
    tile_scr, weight_scr, part_scr, recv_sem, val_sem, proj_sem, conv_sem, bc_sem,
):
    def load(i):
        cols = group_cols(order(i))
        return pltpu.make_async_copy(val_hbm.at[:, cols], val_ref.at[:, cols], val_sem.at[i])

    def store(i):
        cols = group_cols(order(i))
        return pltpu.make_async_copy(conv_ref.at[:, cols], conv_hbm.at[:, cols], conv_sem.at[i])

    def arrived(i, low, high):
        return pltpu.make_async_copy(recv_hbm.at[:, low:high], recv_ref.at[:, low:high], recv_sem.at[i])

    load_proj = pltpu.make_async_copy(proj_hbm, proj_ref, proj_sem)
    pieces = [arrived(0, P_AT, CHUNK), arrived(1, 0, GW), arrived(2, GW, 2 * GW)]
    store_bc = [
        pltpu.make_async_copy(src, dst, bc_sem.at[i])
        for i, (src, dst) in enumerate(((in_ref, in_hbm), (out_ref, out_hbm)))
    ]
    pieces[0].start()
    load_proj.start()
    pieces[1].start()
    for i in range(G // 2):
        load(i).start()
    pieces[2].start()
    for i in range(G // 2, G):
        load(i).start()

    def first():
        place_scr[...] = placement(at_ref)
        taken_scr[...] = dot(place_scr[...], jnp.ones((LANES, LANES), bf16))
        pieces[0].wait()
        spread_out(recv_ref[:, P_AT:], wide_scr)
        load_proj.wait()
        for b in range(QUART):
            tile_scr[0, :, :256] = dot(place_scr[...], quarter_rows(wide_scr, b, 2))
            for half in range(2):
                pair = b * 2 + half
                cols = slice(pair * LANES, (pair + 1) * LANES)

                def use(rows, x, y, pair=pair, cols=cols):
                    if rows.start == 0:
                        hp_ref[:, cols] = x[:EDGE].astype(bf16)
                    if pair < G // 2:
                        in_ref[pair, rows, :] = y
                    else:
                        out_ref[pair - G // 2, rows, :] = y

                at = slice(E + pair * LANES, E + (pair + 1) * LANES)
                conv_columns(
                    tile_scr.at[0, :, half * LANES : (half + 1) * LANES], proj_ref.at[:, cols], taken_scr,
                    slice(None), w_ref[:, at], b_ref[:, at], use,
                )
        for copy in store_bc:
            copy.start()
        steps = wide_scr[2, pl.ds(0, 2 * DEVS, stride=QUART), :].astype(bf16)
        tile = dot(place_scr[...], steps)
        step = step_ref[...].astype(f32)
        step = jnp.where(taken_scr[...] > 0, tile, jnp.concatenate([step, step], axis=1))
        sbias, dlog = sbias_ref[...], dlog_ref[...]
        size = softplus(step + jnp.concatenate([sbias, sbias], axis=1))
        logs = -jnp.exp(jnp.concatenate([dlog, dlog], axis=1)) * size
        size_ref[...] = size
        lower = jnp.where(iota((SPAN, SPAN), 0) >= iota((SPAN, SPAN), 1), 1.0, 0.0).astype(bf16)
        cums = []
        for k in range(TOK // SPAN):
            parts = three(logs[k * SPAN : (k + 1) * SPAN])
            cums.append(dot(lower, parts[0]) + (dot(lower, parts[1]) + dot(lower, parts[2])))
        last = [c[SPAN - 1 : SPAN, :] for c in cums]
        for k, c in enumerate(cums):
            rows = slice(k * SPAN, (k + 1) * SPAN)
            cum_ref[rows, :] = c
            left = last[k] - c
            if k == 0:
                left = left + last[1]
            tail_scr[rows, :] = split2(jnp.exp(left) * size[rows])
        total_ref[...] = jnp.broadcast_to(jnp.exp(last[0] + last[1]), total_ref.shape)

    first()
    for odd in range(2):
        pieces[1 + odd].wait()
        spread_out(recv_ref[:, odd * GW : (odd + 1) * GW], wide_scr)

        @pl.loop(0, G // 4)
        def _(two, odd=odd):
            for slot in range(2):
                pair = 2 * two + slot
                g = 2 * pair + odd
                i = odd * (G // 2) + pair
                tile_scr[slot] = dot(place_scr[...], quarter_rows(wide_scr, pair, GW // LANES))
                weight_scr[slot] = dot(tail_scr[...], expander(g))
                we_ref[:, group_cols(g)] = weight_scr[slot, :EDGE, :]
                load(i).wait()
                for k in range(GW // LANES):
                    cols = pl.ds(pl.multiple_of(g * GW + k * LANES, LANES), LANES)
                    part = slice(k * LANES, (k + 1) * LANES)

                    def use(rows, x, y, cols=cols, part=part, slot=slot):
                        if rows.start == 0:
                            hv_ref[:, cols] = x[:EDGE].astype(bf16)
                        conv_ref[rows, cols] = y
                        weight = weight_scr[slot, rows, part]
                        part_scr[slot, rows, part] = (y.astype(f32) * weight).astype(bf16)

                    conv_columns(
                        tile_scr.at[slot, :, part], val_ref.at[:, cols], taken_scr, slice(None),
                        w_ref[:, cols], b_ref[:, cols], use,
                    )
                store(i).start()
            for slot in range(2):
                pair = 2 * two + slot
                rows = pl.ds(pl.multiple_of((2 * pair + odd) * N, N), N)
                b_g = in_ref[pair, EDGE:, odd * N : (odd + 1) * N]
                state_ref[rows, :] = dot_rows(b_g, part_scr[slot, EDGE:, :])

    for copy in store_bc:
        copy.wait()
    for i in range(G):
        store(i).wait()


def power8(s):
    s2 = s * s
    s4 = s2 * s2
    s8 = s4 * s4
    return jnp.where(s < 0, -s8, s8).astype(bf16)


def root8(code):
    code = code.astype(f32)
    size = jnp.exp(0.125 * jnp.log(jnp.abs(code)))
    return jnp.where(code < 0, -size, size)


FLOOR = 1e-30


def edge_kernel(
    rim_ref, hv_ref, hp_ref, w_ref, b_ref, we_ref, total_ref, state_ref,
    send_ref, conv_ref, proj_ref,
    full_scr,
):
    def conv(x_ref, at, columns):
        before = rim_ref[EDGE - 8 :, columns].astype(f32)
        return conv_chunk(x_ref[:, at].astype(f32), before, w_ref[:, columns], b_ref[:, columns])

    p = [conv(hp_ref, slice(k * LANES, (k + 1) * LANES), slice(E + k * LANES, E + (k + 1) * LANES)) for k in range(PW // LANES)]
    p = jnp.concatenate(p, axis=1)
    proj_ref[...] = p
    top = jnp.zeros((8, LANES), f32)
    for g in range(G):
        b_g = p[:, g * N : (g + 1) * N]
        cols = slice(g * GW, (g + 1) * GW)
        y = conv(hv_ref, cols, cols)
        conv_ref[:, cols] = y
        rows = slice(g * N, (g + 1) * N)
        state = state_ref[rows, :] + dot_rows(b_g, (y.astype(f32) * we_ref[:, cols]).astype(bf16))
        full_scr[rows, :] = state
        sums = jnp.abs(state[:8])
        for k in range(8, N, 8):
            sums = sums + jnp.abs(state[k : k + 8])
        top = top + dot_cols(sums.astype(bf16), expander(g))
    top = jnp.maximum(jnp.sum(top, axis=0, keepdims=True) * 2.0**-14, FLOOR).astype(bf16).astype(f32)
    top = jnp.where(iota((8, LANES), 1) < H, top, 0.0)
    for g in range(G):
        back = 1.0 / dot(top.astype(bf16), expander(g))[:1]
        for low in range(g * N, (g + 1) * N, 32):
            send_ref[low : low + 32, :GW] = power8(full_scr[low : low + 32, :] * back)
    decay = split2(total_ref[...]).astype(f32)
    odd = (iota((8, LANES), 0) & 1) == 1
    side = jnp.where(odd, top, decay).astype(bf16)
    side = jnp.concatenate([side, side], axis=0)
    for low in range(0, G * N, 16):
        send_ref[low : low + 16, GW:] = side


def scan_kernel(dev_ref, recv_ref, after_ref, out_ref, bound_ref, side_scr):
    dev = dev_ref[0]
    side_scr[...] = dot(recv_ref[:, GW:], expander(dev // 8))

    def code(state, bound):
        return state * (1.0 / jnp.maximum(bound, FLOOR))

    def two(i, carry):
        rows = pl.ds(pl.multiple_of(i * 16, 16), 16)
        first, bound, own = carry
        state = root8(recv_ref[rows, :GW])
        side = side_scr[rows, :]
        second = side[:1] * first + state[:8] * side[1:2]
        second_bound = side[:1] * bound + side[1:2]
        out_ref[rows, :] = power8(jnp.concatenate([code(first, bound), code(second, second_bound)], axis=0))
        part = recv_ref[rows, GW:].astype(f32)
        part = part + pltpu.roll(part, H, 1)
        own = jnp.where(2 * i < dev, part[:1] * own + part[1:2], own)
        own = jnp.where(2 * i + 1 < dev, part[8:9] * own + part[9:10], own)
        return (
            side[8:9] * second + state[8:] * side[9:10],
            side[8:9] * second_bound + side[9:10],
            own,
        )

    zeros = (jnp.zeros((8, GW), f32), jnp.zeros((1, GW), f32), jnp.zeros((1, LANES), f32))
    own = lax.fori_loop(0, DEVS // 2, two, zeros, unroll=8)[2]
    bound_ref[...] = jnp.broadcast_to(own, bound_ref.shape)


def local_kernel(
    odd, recv_ref, at_ref, gate_ref, conv_ref, edge_ref, in_ref, out_ref, ein_ref, eout_ref,
    cum_ref, cumt_ref, size_ref, skip_ref, *rest,
):
    mix_out, scale_out, query_ref, place_scr, taken_scr, wide_scr, gate_scr, weighted_scr, first_scr, mix_ref, scale_ref = rest[-11:]
    i = pl.program_id(0)
    g = 2 * i + odd

    @pl.when(i == 0)
    def _():
        place_scr[...] = placement(at_ref)
        taken_scr[...] = dot(place_scr[...], jnp.ones((LANES, LANES), bf16))
        spread_out(recv_ref[...], wide_scr)

    def patched(edge, rest):
        return jnp.concatenate([edge, rest[EDGE:]], axis=0)

    half = slice(odd * N, (odd + 1) * N)
    b_g = patched(ein_ref[:, half], in_ref[0, :, half])
    c_g = patched(eout_ref[:, half], out_ref[0, :, half])
    query_ref[0] = c_g
    cum = cum_ref[...]
    spread = expander(g)
    skip = skip_ref[...]
    skip = jnp.broadcast_to(jnp.concatenate([skip, skip], axis=1), (8, LANES))
    skip = dot(split2(skip), spread)[:1]
    last = cum[SPAN - 1 : SPAN, :]
    upto = jnp.concatenate([cum[:SPAN], cum[SPAN:] + last], axis=0)
    scale_ref[...] = dot(split2(jnp.exp(upto)), spread)
    weighted_scr[...] = dot(split2(size_ref[...]), spread)
    gate_scr[...] = dot(place_scr[...], quarter_rows(wide_scr, i, GW // LANES))
    own = pltpu.roll(cum, lax.rem(LANES - g * (H // G), LANES), 1)
    for low in range(0, TOK, 32):
        rows = slice(low, low + 32)
        taken = taken_scr[rows, :] > 0
        for k in range(GW // LANES):
            cols = slice(k * LANES, (k + 1) * LANES)
            gate = silu(jnp.where(taken, gate_scr[rows, cols], gate_ref[rows, cols].astype(f32)))
            gate_scr[rows, cols] = gate
            scale_out[rows, cols] = (scale_ref[rows, cols] * gate).astype(bf16)
            x = conv_ref[rows, cols]
            if low == 0:
                x = patched(edge_ref[:, cols], x)
            x = x.astype(f32)
            weighted_scr[rows, cols] = weighted_scr[rows, cols] * x
            mix_ref[rows, cols] = skip[:, cols] * x
    tail = dot(split2(jnp.exp(last - cum[:SPAN])), spread)
    inner = dot(split2(jnp.exp(cum[SPAN:])), spread)
    state = dot_rows(b_g[:SPAN], (weighted_scr[:SPAN] * tail).astype(bf16))
    first_scr[...] = dot_whole(c_g[SPAN:], state) * inner
    causal = iota((SPAN, SPAN), 0) >= iota((SPAN, SPAN), 1)
    lane = iota((SPAN, LANES), 1)
    for k in range(TOK // SPAN):
        rows = slice(k * SPAN, (k + 1) * SPAN)
        scores = jnp.where(causal, dot_cols(c_g[rows], b_g[rows]), 0.0)
        for pair in range(H // G // 2):
            kernels = []
            for head in (2 * pair, 2 * pair + 1):
                apart = own[rows, head : head + 1] - cumt_ref[0, head : head + 1, rows]
                kernels.append((jnp.exp(jnp.minimum(apart, 0.0)) * scores).astype(bf16))
            cols = slice(pair * LANES, (pair + 1) * LANES)
            w = weighted_scr[rows, cols]
            low = jnp.where(lane < P_SIZE, w, 0.0).astype(bf16)
            high = jnp.where(lane < P_SIZE, 0.0, w).astype(bf16)
            mixed = dot(jnp.concatenate(kernels, axis=1), jnp.concatenate([low, high], axis=0))
            mixed = mixed + mix_ref[rows, cols]
            if k == 1:
                mixed = mixed + first_scr[:, cols]
            mix_out[rows, cols] = (mixed * gate_scr[rows, cols]).astype(bf16)


def final_kernel(
    bound_ref, entry_ref, gain_ref, qe_hbm, qo_hbm, me_hbm, se_hbm, mo_hbm, so_hbm, out_hbm,
    query_ref, mix_ref, scale_ref, out_ref, entry_scr, part_scr, square_scr, query_sem, mix_sem, scale_sem, out_sem,
):
    queries = [
        pltpu.make_async_copy(src, query_ref.at[i * G // 2 : (i + 1) * G // 2], query_sem.at[i])
        for i, src in enumerate((qe_hbm, qo_hbm))
    ]
    mixes, scales, stores = [], [], []
    for i in range(G):
        cols = slice(i % (G // 2) * GW, (i % (G // 2) + 1) * GW)
        mix, scale = (me_hbm, se_hbm) if i < G // 2 else (mo_hbm, so_hbm)
        mixes.append(pltpu.make_async_copy(mix.at[:, cols], mix_ref.at[i], mix_sem.at[i]))
        scales.append(pltpu.make_async_copy(scale.at[:, cols], scale_ref.at[i], scale_sem.at[i]))
        g = i % (G // 2) * 2 + i // (G // 2)
        cols = slice(g * GW, (g + 1) * GW)
        stores.append(pltpu.make_async_copy(out_ref.at[:, cols], out_hbm.at[:, cols], out_sem.at[i]))
    for load in (*queries, *(c for pair in zip(mixes, scales) for c in pair)):
        load.start()
    bound = split2(jnp.maximum(bound_ref[...], FLOOR))
    for g in range(G):
        rows = slice(g * N, (g + 1) * N)
        entry_scr[rows, :] = root8(entry_ref[rows, :]) * dot(bound, expander(g))[:1]
    for query in queries:
        query.wait()
    for i in range(G):
        g = i % (G // 2) * 2 + i // (G // 2)
        own = dot_whole(query_ref[i], entry_scr[g * N : (g + 1) * N, :])
        mixes[i].wait()
        scales[i].wait()
        for k in range(GW // LANES):
            cols = slice(k * LANES, (k + 1) * LANES)
            part = mix_ref[i, :, cols].astype(f32) + scale_ref[i, :, cols].astype(f32) * own[:, cols]
            part_scr[:, cols] = part
            square_scr[:, cols] = (part * part).astype(bf16)
        mean = dot(square_scr[...], jnp.ones((GW, LANES), bf16)) * (1.0 / GW)
        mean = lax.rsqrt(mean + 1e-05)
        for k in range(GW // LANES):
            cols = slice(k * LANES, (k + 1) * LANES)
            at = slice(g * GW + k * LANES, g * GW + (k + 1) * LANES)
            out_ref[:, at] = (part_scr[:, cols] * mean * gain_ref[:, at]).astype(bf16)
        stores[i].start()
    for store in stores:
        store.wait()


def call(kernel, outs, grid, in_specs, out_specs, scratch=(), est=None, name=None, vmem=VMEM_MIB, alias=None):
    return pl.pallas_call(
        kernel,
        out_shape=outs,
        grid_spec=pltpu.PrefetchScalarGridSpec(
            num_scalar_prefetch=0,
            grid=grid,
            in_specs=in_specs,
            out_specs=out_specs,
            scratch_shapes=scratch,
        ),
        compiler_params=pltpu.CompilerParams(vmem_limit_bytes=vmem * MIB),
        input_output_aliases=alias or {},
        cost_estimate=est,
        name=name,
    )


def struct(*shape, dtype=bf16):
    return pltpu.HBM(shape, dtype)


def near(*shape, dtype=bf16):
    return pltpu.VMEM(shape, dtype)


def far(a):
    return pltpu.with_memory_space_constraint(a, pltpu.HBM)


def kept(a):
    return pltpu.with_memory_space_constraint(a, pltpu.VMEM)


def exchange(rows):
    return lax.all_to_all(rows, "ctx", split_axis=0, concat_axis=0, tiled=True)


def twice(a):
    return jnp.concatenate([a, a], axis=-1)


def shards(
    text_values, text_gate, text_proj, text_step, tile_values, tile_gate, tile_proj, tile_step,
    tile_position, tile_count, conv_weight, conv_bias, step_bias, decay_log, skip_gain, norm_gain,
):
    device = lax.axis_index("ctx")
    scalar = pl.BlockSpec(memory_space=pltpu.SMEM)
    dev = device.reshape(1).astype(jnp.int32)

    hbm = pl.BlockSpec(memory_space=pl.ANY)
    sems = pltpu.SemaphoreType.DMA
    packed = call(
        pack_kernel,
        struct(DEVS * 8, CHUNK),
        (1,),
        [scalar, whole((32, LANES)), whole((TILE, H)), hbm, hbm, hbm],
        hbm,
        scratch=[pltpu.VMEM((TILE, E), bf16), pltpu.VMEM((TILE, E), bf16), pltpu.VMEM((TILE, PW), bf16),
                 pltpu.VMEM((DEVS * 8, CHUNK), bf16), sems((3,)), sems((5,))],
        est=cost(2 * 512 * 256 * CHUNK, 4_000_000),
        name="pack",
    )(dev, far(tile_position.reshape(32, LANES)), far(tile_step), far(tile_values), far(tile_gate), far(tile_proj))
    recv = kept(exchange(packed))

    position = tile_position.reshape(DEVS, TILE)
    ids = jnp.arange(TILE, dtype=jnp.int32)
    landing = ((position >> 8) == device) & (ids[None, :] < tile_count[:, None])
    local = jnp.where(landing, position & (TOK - 1), -1)
    at = jnp.max(local.reshape(DEVS, TILE // 2, 2), axis=1).reshape(1, 2 * DEVS)
    ends = jnp.arange(TOK - KCONV + 1, TOK)[:, None]
    rim_slot = jnp.max(jnp.where(at == ends, jnp.arange(2 * DEVS)[None, :], -1), axis=1)
    at = far(at)
    bias = conv_bias[None, :]

    recv_spec = whole((DEVS * 8, CHUNK))
    at_spec = whole((1, 2 * DEVS))
    rim = call(
        rim_kernel,
        struct(EDGE, E + PW),
        (1,),
        [scalar, recv_spec,
         pl.BlockSpec((EDGE, E), lambda i: (TOK // EDGE - 1, 0)),
         pl.BlockSpec((EDGE, PW), lambda i: (TOK // EDGE - 1, 0))],
        whole((EDGE, E + PW)),
        est=cost(2 * 16 * 48 * 5120, 3_000_000),
        name="rim",
    )(rim_slot, recv, far(text_values), far(text_proj))
    rim = lax.ppermute(rim, "ctx", [(i, i + 1) for i in range(DEVS - 1)])

    conv, inputs, outputs, state, cum, size, total, head_v, head_p, tail = call(
        place_kernel,
        (
            struct(TOK, E), struct(G // 2, TOK, LANES), struct(G // 2, TOK, LANES), near(G * N, GW, dtype=f32),
            struct(TOK, LANES, dtype=f32), struct(TOK, LANES, dtype=f32),
            near(8, LANES, dtype=f32),
            near(EDGE, E), near(EDGE, PW), near(EDGE, E, dtype=f32),
        ),
        (1,),
        [hbm, hbm, hbm, at_spec, whole((TOK, H)), whole((KCONV, E + PW)), whole((1, E + PW)),
         whole((1, H)), whole((1, H))],
        [hbm, hbm, hbm, whole((G * N, GW)), whole((TOK, LANES)), whole((TOK, LANES)),
         whole((8, LANES)), whole((EDGE, E)), whole((EDGE, PW)), whole((EDGE, E))],
        scratch=[pltpu.VMEM((DEVS * 8, CHUNK), bf16), pltpu.VMEM((TOK, E), bf16), pltpu.VMEM((TOK, PW), bf16),
                 pltpu.VMEM((TOK, E), bf16), pltpu.VMEM((G // 2, TOK, LANES), bf16), pltpu.VMEM((G // 2, TOK, LANES), bf16),
                 pltpu.VMEM((TOK, LANES), bf16), pltpu.VMEM((TOK, LANES), f32),
                 pltpu.VMEM((GW // LANES, DEVS * 8, LANES), f32), pltpu.VMEM((TOK, LANES), bf16),
                 pltpu.VMEM((2, TOK, GW), f32), pltpu.VMEM((2, TOK, GW), f32), pltpu.VMEM((2, TOK, GW), bf16),
                 sems((3,)), sems((G,)), sems(()), sems((G,)), sems((2,))],
        est=cost(2 * 256 * 512 * 5120, 10_000_000, 1_300_000),
        name="place",
    )(recv, far(text_values), far(text_proj), at, far(text_step), far(conv_weight), far(bias),
      far(step_bias[None, :]), far(decay_log[None, :]))

    send, edge, edge_p = call(
        edge_kernel,
        (struct(G * N, STATE_W), struct(EDGE, E), struct(EDGE, PW)),
        (1,),
        [whole((EDGE, E + PW)), whole((EDGE, E)), whole((EDGE, PW)), whole((KCONV, E + PW)),
         whole((1, E + PW)), whole((EDGE, E)), whole((8, LANES)), whole((G * N, GW))],
        [whole((G * N, STATE_W)), whole((EDGE, E)), whole((EDGE, PW))],
        scratch=[pltpu.VMEM((G * N, GW), f32)],
        est=cost(2 * 64 * 16 * 4096, 2_000_000, 100_000),
        name="edge",
    )(kept(rim), kept(head_v), kept(head_p), far(conv_weight), far(bias), kept(tail), kept(total), kept(state))
    states = kept(exchange(send))

    by_head = cum[:, :H].T.reshape(G, H // G, TOK)

    def rows_own(odd, more):
        per_pair = pl.BlockSpec((1, TOK, LANES), lambda i: (i, 0, 0))
        cols = pl.BlockSpec((TOK, GW), lambda i: (0, 2 * i + odd))
        own_cols = pl.BlockSpec((TOK, GW), lambda i: (0, i))
        anywhere = pl.BlockSpec(memory_space=pl.ANY)
        return call(
            functools.partial(local_kernel, odd),
            (struct(TOK, E // 2), struct(TOK, E // 2), struct(G // 2, TOK, N)),
            (G // 2,),
            [pl.BlockSpec((DEVS * 8, GW), lambda i: (0, G_AT // GW + odd)), at_spec, cols, cols,
             pl.BlockSpec((EDGE, GW), lambda i: (0, 2 * i + odd)), per_pair, per_pair,
             pl.BlockSpec((EDGE, LANES), lambda i: (0, i)), pl.BlockSpec((EDGE, LANES), lambda i: (0, G // 2 + i)),
             whole((TOK, LANES)), pl.BlockSpec((1, H // G, TOK), lambda i: (2 * i + odd, 0, 0)),
             whole((TOK, LANES)), whole((1, H))] + [anywhere] * len(more),
            [own_cols, own_cols, pl.BlockSpec((1, TOK, N), lambda i: (i, 0, 0))],
            scratch=[pltpu.VMEM((TOK, LANES), bf16), pltpu.VMEM((TOK, LANES), f32),
                     pltpu.VMEM((GW // LANES, DEVS * 8, LANES), f32), pltpu.VMEM((TOK, GW), f32), pltpu.VMEM((TOK, GW), f32), pltpu.VMEM((SPAN, GW), f32),
                     pltpu.VMEM((TOK, GW), f32), pltpu.VMEM((TOK, GW), f32)],
            est=cost(6_000_000_000, 8_000_000, 2_000_000),
            name=f"local{odd}",
        )(recv, at, far(text_gate), *map(far, (conv, edge, inputs, outputs, edge_p, edge_p, cum, by_head, size, skip_gain[None, :])), *more)

    even = rows_own(0, ())
    entries, bound = call(
        scan_kernel,
        (struct(G * N, GW), near(8, LANES, dtype=f32)),
        (1,),
        [scalar, whole((DEVS * 8, STATE_W)), pl.BlockSpec(memory_space=pl.ANY)],
        [whole((G * N, GW)), whole((8, LANES))],
        scratch=[pltpu.VMEM((G * N, GW), f32)],
        est=cost(2 * 512 * 512 * 128, 1_200_000),
        name="scan",
    )(dev, states, even[2])
    entry = kept(exchange(entries))
    odds = rows_own(1, (bound,))

    return call(
        final_kernel,
        struct(TOK, E),
        (1,),
        [whole((8, LANES)), whole((G * N, GW)), whole((1, E))] + [hbm] * 6,
        hbm,
        scratch=[pltpu.VMEM((G, TOK, N), bf16), pltpu.VMEM((G, TOK, GW), bf16), pltpu.VMEM((G, TOK, GW), bf16),
                 pltpu.VMEM((TOK, E), bf16), pltpu.VMEM((G * N, GW), f32), pltpu.VMEM((TOK, GW), f32),
                 pltpu.VMEM((TOK, GW), bf16), sems((2,)), sems((G,)), sems((G,)), sems((G,))],
        est=cost(2 * 256 * 64 * 4096, 11_000_000),
        name="final",
    )(kept(bound), entry, far(norm_gain[None, :]), *map(far, (even[2], odds[2], even[0], even[1], odds[0], odds[1])))


def solution(mesh):
    rows = P(("dp", "ctx"), None)
    specs = (rows,) * 8 + (P("dp"),) * 2 + (P(),) * 6
    return jax.shard_map(shards, mesh=mesh, in_specs=specs, out_specs=rows, check_vma=False)
```

```python
import functools

import jax
import jax.numpy as jnp
from jax import lax
from jax.experimental import pallas as pl
from jax.experimental.pallas import tpu as pltpu
from jax.sharding import PartitionSpec as P

H = 64
P_SIZE = 64
N = 64
G = 8
SPAN = 128
KCONV = 4
E = 4096
TOK = 256
TILE = 64
DEVS = 64
GW = E // G
PW = 2 * G * N
EDGE = 16
LANES = 128
QUART = 4
V_AT, G_AT, P_AT, S_AT = 0, 1024, 2048, 2304
CHUNK = 2432
STATE_W = GW + LANES

f32 = jnp.float32
bf16 = jnp.bfloat16
MIB = 1024 * 1024
VMEM_MIB = 32


def cost(flops, size, trans=0):
    return pl.CostEstimate(flops=flops, bytes_accessed=size, transcendentals=trans)


def whole(shape):
    return pl.BlockSpec(shape, lambda *_: (0,) * len(shape))


def group_cols(g):
    return pl.ds(pl.multiple_of(g * GW, GW), GW)


def iota(shape, dim):
    return lax.broadcasted_iota(jnp.int32, shape, dim)


def dot(a, b):
    return jnp.dot(a, b, preferred_element_type=f32)


def dot_rows(a, b):
    return lax.dot_general(a, b, (((0,), (0,)), ((), ())), preferred_element_type=f32)


def dot_cols(a, b):
    return lax.dot_general(a, b, (((1,), (1,)), ((), ())), preferred_element_type=f32)


def dot_whole(a, b):
    high = b.astype(bf16)
    low = (b - high.astype(f32)).astype(bf16)
    return dot(jnp.concatenate([a, a], axis=1), jnp.concatenate([high, low], axis=0))


def silu(x):
    half = 0.5 * x
    return half + half * jnp.tanh(half)


def split2(x):
    high = x.astype(bf16)
    low = (x - high.astype(f32)).astype(bf16)
    return jnp.where(iota(x.shape, 1) < H, high.astype(f32), low.astype(f32)).astype(bf16)


def expander(group):
    head = iota((LANES, GW), 0) & (H - 1)
    col = group * (H // G) + (iota((LANES, GW), 1) >> 6)
    return jnp.where(head == col, 1.0, 0.0).astype(bf16)


def pack_kernel(
    pos_hbm, step_hbm, val_hbm, gate_hbm, proj_hbm, out_hbm,
    pos_ref, step_ref, val_ref, gate_ref, proj_ref, out_ref, in_sem, out_sem,
):
    pairs = ((val_hbm, val_ref), (gate_hbm, gate_ref), (proj_hbm, proj_ref), (pos_hbm, pos_ref), (step_hbm, step_ref))
    loads = [pltpu.make_async_copy(src, dst, in_sem.at[i]) for i, (src, dst) in enumerate(pairs)]
    for load in (loads[3], loads[4], loads[0], loads[1], loads[2]):
        load.start()
    dev = lax.axis_index("ctx")
    loads[3].wait()
    loads[4].wait()
    row = pos_ref[pl.ds(dev // 2, 1), :]
    other = pltpu.roll(row, 64, 1)
    lane = iota((1, LANES), 1)
    own = jnp.where((lane >> 6) == lax.rem(dev, 2), row, other)
    key = (own >> 8) * 8 + (lane & 1) * QUART + (lane >> 6)
    keys = jnp.concatenate([key, key + 2], axis=1)
    pick = jnp.where(iota((DEVS * 8, 2 * LANES), 0) == keys, 1.0, 0.0).astype(bf16)
    step = step_ref[...]
    out_ref[:, S_AT:] = dot(pick[:, :TILE], jnp.concatenate([step, step], axis=1)).astype(bf16)
    stores = []
    for i, (ref, at, width, part) in enumerate(
        ((val_ref, V_AT, 1024, 512), (gate_ref, G_AT, 1024, 512), (proj_ref, P_AT, 256, 256))
    ):
        loads[i].wait()
        for low in range(0, width, part):
            rows = [ref[:, b * width + low : b * width + low + part] for b in range(QUART)]
            out_ref[:, at + low : at + low + part] = dot(pick, jnp.concatenate(rows, axis=0)).astype(bf16)
            end = at + low + part if i < 2 else CHUNK
            cols = slice(at + low, end)
            store = pltpu.make_async_copy(out_ref.at[:, cols], out_hbm.at[:, cols], out_sem.at[len(stores)])
            store.start()
            stores.append(store)
    for store in stores:
        store.wait()


def rim_kernel(slot_ref, recv_ref, val_ref, proj_ref, at_ref, step_ref, out_ref):
    count = KCONV - 1
    slots = [slot_ref[i] for i in range(count)]
    starts = [jnp.maximum(k, 0) * QUART for k in slots]
    rows = [recv_ref[pl.ds(pl.multiple_of((k >> 4) * 16, 16), 16), :] for k in starts]
    rows = jnp.concatenate(rows, axis=0)
    row, col = iota((EDGE, 16 * count), 0), iota((EDGE, 16 * count), 1)
    at = jnp.full((EDGE, 16 * count), -16, jnp.int32)
    taken = jnp.full((EDGE, 1), -1, jnp.int32)
    for i, k in enumerate(starts):
        at = jnp.where(row == EDGE - count + i, 16 * i + (k & 15), at)
        taken = jnp.where(iota((EDGE, 1), 0) == EDGE - count + i, slots[i], taken)
    for b in range(QUART):
        place = jnp.where(col == at + b, 1.0, 0.0).astype(bf16)
        tile = dot(place, rows[:, V_AT:G_AT])
        cols = slice(b * 1024, (b + 1) * 1024)
        out_ref[:, cols] = jnp.where(taken >= 0, tile, val_ref[:, cols].astype(f32)).astype(bf16)
        tile = dot(place, rows[:, P_AT:S_AT])
        cols = slice(b * 256, (b + 1) * 256)
        out_ref[:, E + b * 256 : E + (b + 1) * 256] = jnp.where(
            taken >= 0, tile, proj_ref[:, cols].astype(f32)
        ).astype(bf16)


def placement(at_ref):
    return jnp.where(iota((TOK, LANES), 0) == at_ref[...], 1.0, 0.0).astype(bf16)


def spread_out(recv, wide_ref):
    for k in range(recv.shape[1] // LANES):
        wide_ref[k] = recv[:, k * LANES : (k + 1) * LANES].astype(f32)


def quarter_rows(wide_ref, b, count):
    rows = [wide_ref[k, pl.ds(b, 2 * DEVS, stride=QUART), :] for k in range(count)]
    return jnp.concatenate(rows, axis=1).astype(bf16)


def conv_chunk(x, before, weights, bias):
    ext = jnp.concatenate([before, x], axis=0)
    total = bias + weights[KCONV - 1 : KCONV, :] * x
    for back in range(1, KCONV):
        total = total + weights[KCONV - 1 - back : KCONV - back, :] * pltpu.roll(ext, back, 0)[8:]
    return silu(total).astype(bf16)


CHUNK_ROWS = 64


def conv_columns(tile_ref, text_ref, taken_ref, cols, weights, bias, use):
    before = jnp.zeros((8, LANES), f32)
    for low in range(0, TOK, CHUNK_ROWS):
        rows = slice(low, low + CHUNK_ROWS)
        x = jnp.where(taken_ref[rows, :] > 0, tile_ref[rows, cols], text_ref[rows, cols].astype(f32))
        use(rows, x, conv_chunk(x, before, weights, bias))
        before = x[CHUNK_ROWS - 8 :]


def softplus(v):
    return jnp.maximum(v, 0.0) + jnp.log1p(jnp.exp(-jnp.abs(v)))


def three(x):
    a = x.astype(bf16)
    left = x - a.astype(f32)
    b = left.astype(bf16)
    return a, b, (left - b.astype(f32)).astype(bf16)


def order(i):
    return lax.rem(i, G // 2) * 2 + i // (G // 2)


def place_kernel(
    recv_hbm, val_hbm, proj_hbm, at_hbm, step_hbm, w_hbm, b_hbm, sbias_hbm, dlog_hbm,
    conv_hbm, in_hbm, out_hbm, state_ref, cum_ref, size_ref, total_ref, hv_ref, hp_ref, we_ref,
    at_ref, step_ref, w_ref, b_ref, sbias_ref, dlog_ref,
    recv_ref, val_ref, proj_ref, conv_ref, in_ref, out_ref, place_scr, taken_scr, wide_scr, tail_scr,
    tile_scr, weight_scr, part_scr, small_sem, recv_sem, val_sem, proj_sem, conv_sem, bc_sem,
):
    def load(i):
        cols = group_cols(order(i))
        return pltpu.make_async_copy(val_hbm.at[:, cols], val_ref.at[:, cols], val_sem.at[i])

    def store(i):
        cols = group_cols(order(i))
        return pltpu.make_async_copy(conv_ref.at[:, cols], conv_hbm.at[:, cols], conv_sem.at[i])

    def arrived(i, low, high):
        return pltpu.make_async_copy(recv_hbm.at[:, low:high], recv_ref.at[:, low:high], recv_sem.at[i])

    load_proj = pltpu.make_async_copy(proj_hbm, proj_ref, proj_sem)
    pieces = [arrived(0, P_AT, CHUNK), arrived(1, 0, GW), arrived(2, GW, 2 * GW)]
    store_bc = [
        pltpu.make_async_copy(src, dst, bc_sem.at[i])
        for i, (src, dst) in enumerate(((in_ref, in_hbm), (out_ref, out_hbm)))
    ]
    pairs = (
        (at_hbm, at_ref), (w_hbm, w_ref), (b_hbm, b_ref), (step_hbm, step_ref), (sbias_hbm, sbias_ref), (dlog_hbm, dlog_ref),
    )
    small = [pltpu.make_async_copy(src, dst, small_sem.at[i]) for i, (src, dst) in enumerate(pairs)]
    small[0].start()
    pieces[0].start()
    load_proj.start()
    for load_small in small[1:]:
        load_small.start()
    pieces[1].start()
    for i in range(G // 2):
        load(i).start()
    pieces[2].start()
    for i in range(G // 2, G):
        load(i).start()

    def first():
        small[0].wait()
        place_scr[...] = placement(at_ref)
        taken_scr[...] = dot(place_scr[...], jnp.ones((LANES, LANES), bf16))
        for load_small in small[1:]:
            load_small.wait()
        pieces[0].wait()
        spread_out(recv_ref[:, P_AT:], wide_scr)
        load_proj.wait()
        for b in range(QUART):
            tile_scr[0, :, :256] = dot(place_scr[...], quarter_rows(wide_scr, b, 2))
            for half in range(2):
                pair = b * 2 + half
                cols = slice(pair * LANES, (pair + 1) * LANES)

                def use(rows, x, y, pair=pair, cols=cols):
                    if rows.start == 0:
                        hp_ref[:, cols] = x[:EDGE].astype(bf16)
                    if pair < G // 2:
                        in_ref[pair, rows, :] = y
                    else:
                        out_ref[pair - G // 2, rows, :] = y

                at = slice(E + pair * LANES, E + (pair + 1) * LANES)
                conv_columns(
                    tile_scr.at[0, :, half * LANES : (half + 1) * LANES], proj_ref.at[:, cols], taken_scr,
                    slice(None), w_ref[:, at], b_ref[:, at], use,
                )
        for copy in store_bc:
            copy.start()
        steps = wide_scr[2, pl.ds(0, 2 * DEVS, stride=QUART), :].astype(bf16)
        tile = dot(place_scr[...], steps)
        step = step_ref[...].astype(f32)
        step = jnp.where(taken_scr[...] > 0, tile, jnp.concatenate([step, step], axis=1))
        sbias, dlog = sbias_ref[...], dlog_ref[...]
        size = softplus(step + jnp.concatenate([sbias, sbias], axis=1))
        logs = -jnp.exp(jnp.concatenate([dlog, dlog], axis=1)) * size
        size_ref[...] = size
        lower = jnp.where(iota((SPAN, SPAN), 0) >= iota((SPAN, SPAN), 1), 1.0, 0.0).astype(bf16)
        cums = []
        for k in range(TOK // SPAN):
            parts = three(logs[k * SPAN : (k + 1) * SPAN])
            cums.append(dot(lower, parts[0]) + (dot(lower, parts[1]) + dot(lower, parts[2])))
        last = [c[SPAN - 1 : SPAN, :] for c in cums]
        for k, c in enumerate(cums):
            rows = slice(k * SPAN, (k + 1) * SPAN)
            cum_ref[rows, :] = c
            left = last[k] - c
            if k == 0:
                left = left + last[1]
            tail_scr[rows, :] = split2(jnp.exp(left) * size[rows])
        total_ref[...] = jnp.broadcast_to(jnp.exp(last[0] + last[1]), total_ref.shape)

    first()
    for odd in range(2):
        pieces[1 + odd].wait()
        spread_out(recv_ref[:, odd * GW : (odd + 1) * GW], wide_scr)

        @pl.loop(0, G // 4)
        def _(two, odd=odd):
            for slot in range(2):
                load(odd * (G // 2) + 2 * two + slot).wait()
            for slot in range(2):
                pair = 2 * two + slot
                g = 2 * pair + odd
                tile_scr[slot] = dot(place_scr[...], quarter_rows(wide_scr, pair, GW // LANES))
                weight_scr[slot] = dot(tail_scr[...], expander(g))
                we_ref[:, group_cols(g)] = weight_scr[slot, :EDGE, :]
                for k in range(GW // LANES):
                    cols = pl.ds(pl.multiple_of(g * GW + k * LANES, LANES), LANES)
                    part = slice(k * LANES, (k + 1) * LANES)

                    def use(rows, x, y, cols=cols, part=part, slot=slot):
                        if rows.start == 0:
                            hv_ref[:, cols] = x[:EDGE].astype(bf16)
                        conv_ref[rows, cols] = y
                        weight = weight_scr[slot, rows, part]
                        part_scr[slot, rows, part] = (y.astype(f32) * weight).astype(bf16)

                    conv_columns(
                        tile_scr.at[slot, :, part], val_ref.at[:, cols], taken_scr, slice(None),
                        w_ref[:, cols], b_ref[:, cols], use,
                    )
            for slot in range(2):
                pair = 2 * two + slot
                rows = pl.ds(pl.multiple_of((2 * pair + odd) * N, N), N)
                b_g = in_ref[pair, EDGE:, odd * N : (odd + 1) * N]
                state_ref[rows, :] = dot_rows(b_g, part_scr[slot, EDGE:, :])
            for slot in range(2):
                store(odd * (G // 2) + 2 * two + slot).start()

    for copy in store_bc:
        copy.wait()
    for i in range(G):
        store(i).wait()


def power8(s):
    s2 = s * s
    s4 = s2 * s2
    s8 = s4 * s4
    return jnp.where(s < 0, -s8, s8).astype(bf16)


def root8(code):
    code = code.astype(f32)
    size = jnp.exp(0.125 * jnp.log(jnp.abs(code)))
    return jnp.where(code < 0, -size, size)


FLOOR = 1e-30


def edge_kernel(
    rim_ref, hv_ref, hp_ref, w_ref, b_ref, we_ref, total_ref, state_ref,
    send_ref, conv_ref, proj_ref,
    full_scr,
):
    def conv(x_ref, at, columns):
        before = rim_ref[EDGE - 8 :, columns].astype(f32)
        return conv_chunk(x_ref[:, at].astype(f32), before, w_ref[:, columns], b_ref[:, columns])

    p = [conv(hp_ref, slice(k * LANES, (k + 1) * LANES), slice(E + k * LANES, E + (k + 1) * LANES)) for k in range(PW // LANES)]
    p = jnp.concatenate(p, axis=1)
    proj_ref[...] = p
    top = jnp.zeros((8, LANES), f32)
    for g in range(G):
        b_g = p[:, g * N : (g + 1) * N]
        cols = slice(g * GW, (g + 1) * GW)
        y = conv(hv_ref, cols, cols)
        conv_ref[:, cols] = y
        rows = slice(g * N, (g + 1) * N)
        state = state_ref[rows, :] + dot_rows(b_g, (y.astype(f32) * we_ref[:, cols]).astype(bf16))
        full_scr[rows, :] = state
        sums = jnp.abs(state[:8])
        for k in range(8, N, 8):
            sums = sums + jnp.abs(state[k : k + 8])
        top = top + dot_cols(sums.astype(bf16), expander(g))
    top = jnp.maximum(jnp.sum(top, axis=0, keepdims=True) * 2.0**-14, FLOOR).astype(bf16).astype(f32)
    top = jnp.where(iota((8, LANES), 1) < H, top, 0.0)
    for g in range(G):
        back = 1.0 / dot(top.astype(bf16), expander(g))[:1]
        for low in range(g * N, (g + 1) * N, 32):
            send_ref[low : low + 32, :GW] = power8(full_scr[low : low + 32, :] * back)
    decay = split2(total_ref[...]).astype(f32)
    odd = (iota((8, LANES), 0) & 1) == 1
    side = jnp.where(odd, top, decay).astype(bf16)
    side = jnp.concatenate([side, side], axis=0)
    for low in range(0, G * N, 16):
        send_ref[low : low + 16, GW:] = side


def scan_kernel(dev_ref, recv_ref, after_ref, out_ref, bound_ref, side_scr):
    dev = dev_ref[0]
    side_scr[...] = dot(recv_ref[:, GW:], expander(dev // 8))

    def code(state, bound):
        return state * (1.0 / jnp.maximum(bound, FLOOR))

    def two(i, carry):
        rows = pl.ds(pl.multiple_of(i * 16, 16), 16)
        first, bound, own = carry
        state = root8(recv_ref[rows, :GW])
        side = side_scr[rows, :]
        second = side[:1] * first + state[:8] * side[1:2]
        second_bound = side[:1] * bound + side[1:2]
        out_ref[rows, :] = power8(jnp.concatenate([code(first, bound), code(second, second_bound)], axis=0))
        part = recv_ref[rows, GW:].astype(f32)
        part = part + pltpu.roll(part, H, 1)
        own = jnp.where(2 * i < dev, part[:1] * own + part[1:2], own)
        own = jnp.where(2 * i + 1 < dev, part[8:9] * own + part[9:10], own)
        return (
            side[8:9] * second + state[8:] * side[9:10],
            side[8:9] * second_bound + side[9:10],
            own,
        )

    zeros = (jnp.zeros((8, GW), f32), jnp.zeros((1, GW), f32), jnp.zeros((1, LANES), f32))
    own = lax.fori_loop(0, DEVS // 2, two, zeros, unroll=8)[2]
    bound_ref[...] = jnp.broadcast_to(own, bound_ref.shape)


def local_kernel(
    odd, recv_ref, at_ref, gate_ref, conv_ref, edge_ref, in_ref, out_ref, ein_ref, eout_ref,
    cum_ref, cumt_ref, size_ref, skip_ref, *rest,
):
    mix_out, scale_out, query_ref, token_ref, place_scr, taken_scr, wide_scr, gate_scr, weighted_scr, first_scr, mix_ref, scale_ref = rest[-12:]
    token_ref[...] = jnp.zeros_like(token_ref)
    i = pl.program_id(0)
    g = 2 * i + odd

    @pl.when(i == 0)
    def _():
        place_scr[...] = placement(at_ref)
        taken_scr[...] = dot(place_scr[...], jnp.ones((LANES, LANES), bf16))
        spread_out(recv_ref[...], wide_scr)

    def patched(edge, rest):
        return jnp.concatenate([edge, rest[EDGE:]], axis=0)

    half = slice(odd * N, (odd + 1) * N)
    b_g = patched(ein_ref[:, half], in_ref[0, :, half])
    c_g = patched(eout_ref[:, half], out_ref[0, :, half])
    query_ref[0] = c_g
    cum = cum_ref[...]
    spread = expander(g)
    skip = skip_ref[...]
    skip = jnp.broadcast_to(jnp.concatenate([skip, skip], axis=1), (8, LANES))
    skip = dot(split2(skip), spread)[:1]
    last = cum[SPAN - 1 : SPAN, :]
    upto = jnp.concatenate([cum[:SPAN], cum[SPAN:] + last], axis=0)
    scale_ref[...] = dot(split2(jnp.exp(upto)), spread)
    weighted_scr[...] = dot(split2(size_ref[...]), spread)
    gate_scr[...] = dot(place_scr[...], quarter_rows(wide_scr, i, GW // LANES))
    own = pltpu.roll(cum, lax.rem(LANES - g * (H // G), LANES), 1)
    for low in range(0, TOK, 32):
        rows = slice(low, low + 32)
        taken = taken_scr[rows, :] > 0
        for k in range(GW // LANES):
            cols = slice(k * LANES, (k + 1) * LANES)
            gate = silu(jnp.where(taken, gate_scr[rows, cols], gate_ref[rows, cols].astype(f32)))
            gate_scr[rows, cols] = gate
            scale_out[rows, cols] = (scale_ref[rows, cols] * gate).astype(bf16)
            x = conv_ref[rows, cols]
            if low == 0:
                x = patched(edge_ref[:, cols], x)
            x = x.astype(f32)
            weighted_scr[rows, cols] = weighted_scr[rows, cols] * x
            mix_ref[rows, cols] = skip[:, cols] * x
    tail = dot(split2(jnp.exp(last - cum[:SPAN])), spread)
    inner = dot(split2(jnp.exp(cum[SPAN:])), spread)
    state = dot_rows(b_g[:SPAN], (weighted_scr[:SPAN] * tail).astype(bf16))
    first_scr[...] = dot_whole(c_g[SPAN:], state) * inner
    causal = iota((SPAN, SPAN), 0) >= iota((SPAN, SPAN), 1)
    lane = iota((SPAN, LANES), 1)
    for k in range(TOK // SPAN):
        rows = slice(k * SPAN, (k + 1) * SPAN)
        scores = jnp.where(causal, dot_cols(c_g[rows], b_g[rows]), 0.0)
        for pair in range(H // G // 2):
            kernels = []
            for head in (2 * pair, 2 * pair + 1):
                apart = own[rows, head : head + 1] - cumt_ref[0, head : head + 1, rows]
                kernels.append((jnp.exp(jnp.minimum(apart, 0.0)) * scores).astype(bf16))
            cols = slice(pair * LANES, (pair + 1) * LANES)
            w = weighted_scr[rows, cols]
            low = jnp.where(lane < P_SIZE, w, 0.0).astype(bf16)
            high = jnp.where(lane < P_SIZE, 0.0, w).astype(bf16)
            mixed = dot(jnp.concatenate(kernels, axis=1), jnp.concatenate([low, high], axis=0))
            mixed = mixed + mix_ref[rows, cols]
            if k == 1:
                mixed = mixed + first_scr[:, cols]
            mix_out[rows, cols] = (mixed * gate_scr[rows, cols]).astype(bf16)


def final_kernel(
    bound_ref, entry_ref, gain_hbm, qe_hbm, qo_hbm, me_hbm, se_hbm, mo_hbm, so_hbm, out_hbm,
    gain_ref, query_ref, mix_ref, scale_ref, out_ref, entry_scr, part_scr, gain_sem, query_sem, mix_sem, scale_sem, out_sem,
):
    gain = pltpu.make_async_copy(gain_hbm, gain_ref, gain_sem)
    queries = [
        pltpu.make_async_copy(src, query_ref.at[i * G // 2 : (i + 1) * G // 2], query_sem.at[i])
        for i, src in enumerate((qe_hbm, qo_hbm))
    ]
    mixes, scales, stores = [], [], []
    for i in range(G):
        cols = slice(i % (G // 2) * GW, (i % (G // 2) + 1) * GW)
        mix, scale = (me_hbm, se_hbm) if i < G // 2 else (mo_hbm, so_hbm)
        mixes.append(pltpu.make_async_copy(mix.at[:, cols], mix_ref.at[i], mix_sem.at[i]))
        scales.append(pltpu.make_async_copy(scale.at[:, cols], scale_ref.at[i], scale_sem.at[i]))
        g = i % (G // 2) * 2 + i // (G // 2)
        cols = slice(g * GW, (g + 1) * GW)
        stores.append(pltpu.make_async_copy(out_ref.at[:, cols], out_hbm.at[:, cols], out_sem.at[i]))
    for load in (*queries, gain, *(c for pair in zip(mixes, scales) for c in pair)):
        load.start()
    bound = split2(jnp.maximum(bound_ref[...], FLOOR))
    for g in range(G):
        rows = slice(g * N, (g + 1) * N)
        entry_scr[rows, :] = root8(entry_ref[rows, :]) * dot(bound, expander(g))[:1]
    for load in (*queries, gain):
        load.wait()
    for i in range(G):
        g = i % (G // 2) * 2 + i // (G // 2)
        if i % 2 == 0:
            for load in (*mixes[i : i + 2], *scales[i : i + 2]):
                load.wait()
        slot = i % 2
        own = dot_whole(query_ref[i], entry_scr[g * N : (g + 1) * N, :])
        squares = jnp.zeros((TOK, LANES), f32)
        for k in range(GW // LANES):
            cols = slice(k * LANES, (k + 1) * LANES)
            part = mix_ref[i, :, cols].astype(f32) + scale_ref[i, :, cols].astype(f32) * own[:, cols]
            part_scr[slot, :, cols] = part
            squares = squares + part * part
        high = squares.astype(bf16)
        low = (squares - high.astype(f32)).astype(bf16)
        mean = dot(jnp.concatenate([high, low], axis=1), jnp.ones((2 * LANES, LANES), bf16)) * (1.0 / GW)
        mean = lax.rsqrt(mean + 1e-05)
        for k in range(GW // LANES):
            cols = slice(k * LANES, (k + 1) * LANES)
            at = slice(g * GW + k * LANES, g * GW + (k + 1) * LANES)
            out_ref[:, at] = (part_scr[slot, :, cols] * mean * gain_ref[:, at]).astype(bf16)
        if i % 2 == 1:
            stores[i - 1].start()
            stores[i].start()
    for store in stores:
        store.wait()


def call(kernel, outs, grid, in_specs, out_specs, scratch=(), est=None, name=None, vmem=VMEM_MIB, alias=None):
    return pl.pallas_call(
        kernel,
        out_shape=outs,
        grid_spec=pltpu.PrefetchScalarGridSpec(
            num_scalar_prefetch=0,
            grid=grid,
            in_specs=in_specs,
            out_specs=out_specs,
            scratch_shapes=scratch,
        ),
        compiler_params=pltpu.CompilerParams(vmem_limit_bytes=vmem * MIB),
        input_output_aliases=alias or {},
        cost_estimate=est,
        name=name,
    )


def struct(*shape, dtype=bf16):
    return pltpu.HBM(shape, dtype)


def near(*shape, dtype=bf16):
    return pltpu.VMEM(shape, dtype)


def far(a):
    return pltpu.with_memory_space_constraint(a, pltpu.HBM)


def kept(a):
    return pltpu.with_memory_space_constraint(a, pltpu.VMEM)


def exchange(rows):
    return lax.all_to_all(rows, "ctx", split_axis=0, concat_axis=0, tiled=True)


def twice(a):
    return jnp.concatenate([a, a], axis=-1)


def shards(
    text_values, text_gate, text_proj, text_step, tile_values, tile_gate, tile_proj, tile_step,
    tile_position, tile_count, conv_weight, conv_bias, step_bias, decay_log, skip_gain, norm_gain,
):
    device = lax.axis_index("ctx")
    scalar = pl.BlockSpec(memory_space=pltpu.SMEM)
    dev = device.reshape(1).astype(jnp.int32)

    hbm = pl.BlockSpec(memory_space=pl.ANY)
    vmem = pl.BlockSpec(memory_space=pltpu.VMEM)
    sems = pltpu.SemaphoreType.DMA
    packed = call(
        pack_kernel,
        struct(DEVS * 8, CHUNK),
        (1,),
        [hbm] * 5,
        hbm,
        scratch=[pltpu.VMEM((32, LANES), jnp.int32), pltpu.VMEM((TILE, H), bf16), pltpu.VMEM((TILE, E), bf16), pltpu.VMEM((TILE, E), bf16), pltpu.VMEM((TILE, PW), bf16),
                 pltpu.VMEM((DEVS * 8, CHUNK), bf16), sems((5,)), sems((5,))],
        est=cost(2 * 512 * 256 * CHUNK, 4_000_000),
        name="pack",
    )(far(tile_position.reshape(32, LANES)), far(tile_step), far(tile_values), far(tile_gate), far(tile_proj))
    recv = kept(exchange(packed))

    position = tile_position.reshape(DEVS, TILE)
    ids = jnp.arange(TILE, dtype=jnp.int32)
    landing = ((position >> 8) == device) & (ids[None, :] < tile_count[:, None])
    local = jnp.where(landing, position & (TOK - 1), -1)
    at = jnp.max(local.reshape(DEVS, TILE // 2, 2), axis=1).reshape(1, 2 * DEVS)
    ends = jnp.arange(TOK - KCONV + 1, TOK)[:, None]
    rim_slot = jnp.max(jnp.where(at == ends, jnp.arange(2 * DEVS)[None, :], -1), axis=1)
    at = far(at)
    steps = far(text_step)
    bias = conv_bias[None, :]

    recv_spec = whole((DEVS * 8, CHUNK))
    at_spec = whole((1, 2 * DEVS))
    rim = call(
        rim_kernel,
        struct(EDGE, E + PW),
        (1,),
        [scalar, vmem,
         pl.BlockSpec((EDGE, E), lambda i: (TOK // EDGE - 1, 0)),
         pl.BlockSpec((EDGE, PW), lambda i: (TOK // EDGE - 1, 0)), hbm, hbm],
        whole((EDGE, E + PW)),
        est=cost(2 * 16 * 48 * 5120, 3_000_000),
        name="rim",
    )(rim_slot, recv, far(text_values), far(text_proj), at, steps)
    rim = lax.ppermute(rim, "ctx", [(i, i + 1) for i in range(DEVS - 1)])

    conv, inputs, outputs, state, cum, size, total, head_v, head_p, tail = call(
        place_kernel,
        (
            struct(TOK, E), struct(G // 2, TOK, LANES), struct(G // 2, TOK, LANES), near(G * N, GW, dtype=f32),
            struct(TOK, LANES, dtype=f32), struct(TOK, LANES, dtype=f32),
            near(8, LANES, dtype=f32),
            near(EDGE, E), near(EDGE, PW), near(EDGE, E, dtype=f32),
        ),
        (1,),
        [hbm] * 9,
        [hbm, hbm, hbm, vmem, whole((TOK, LANES)), whole((TOK, LANES)), vmem, vmem, vmem, vmem],
        scratch=[pltpu.VMEM((1, 2 * DEVS), jnp.int32), pltpu.VMEM((TOK, H), bf16), pltpu.VMEM((KCONV, E + PW), f32),
                 pltpu.VMEM((1, E + PW), f32), pltpu.VMEM((1, H), f32), pltpu.VMEM((1, H), f32),
                 pltpu.VMEM((DEVS * 8, CHUNK), bf16), pltpu.VMEM((TOK, E), bf16), pltpu.VMEM((TOK, PW), bf16),
                 pltpu.VMEM((TOK, E), bf16), pltpu.VMEM((G // 2, TOK, LANES), bf16), pltpu.VMEM((G // 2, TOK, LANES), bf16),
                 pltpu.VMEM((TOK, LANES), bf16), pltpu.VMEM((TOK, LANES), f32),
                 pltpu.VMEM((GW // LANES, DEVS * 8, LANES), f32), pltpu.VMEM((TOK, LANES), bf16),
                 pltpu.VMEM((2, TOK, GW), f32), pltpu.VMEM((2, TOK, GW), f32), pltpu.VMEM((2, TOK, GW), bf16),
                 sems((6,)), sems((3,)), sems((G,)), sems(()), sems((G,)), sems((2,))],
        est=cost(2 * 256 * 512 * 5120, 10_000_000, 1_300_000),
        name="place",
    )(recv, far(text_values), far(text_proj), at, steps, far(conv_weight), far(bias),
      far(step_bias[None, :]), far(decay_log[None, :]))

    send, edge, edge_p = call(
        edge_kernel,
        (struct(G * N, STATE_W), struct(EDGE, E), struct(EDGE, PW)),
        (1,),
        [vmem, vmem, vmem, whole((KCONV, E + PW)), whole((1, E + PW)), vmem, vmem, vmem],
        [whole((G * N, STATE_W)), whole((EDGE, E)), whole((EDGE, PW))],
        scratch=[pltpu.VMEM((G * N, GW), f32)],
        est=cost(2 * 64 * 16 * 4096, 2_000_000, 100_000),
        name="edge",
    )(kept(rim), kept(head_v), kept(head_p), far(conv_weight), far(bias), kept(tail), kept(total), kept(state))
    states = kept(exchange(send))

    by_head = cum[:, :H].T.reshape(G, H // G, TOK)

    def rows_own(odd, more):
        per_pair = pl.BlockSpec((1, TOK, LANES), lambda i: (i, 0, 0))
        cols = pl.BlockSpec((TOK, GW), lambda i: (0, 2 * i + odd))
        own_cols = pl.BlockSpec((TOK, GW), lambda i: (0, i))
        anywhere = pl.BlockSpec(memory_space=pl.ANY)
        return call(
            functools.partial(local_kernel, odd),
            (struct(TOK, E // 2), struct(TOK, E // 2), struct(G // 2, TOK, N), near(8, LANES, dtype=f32)),
            (G // 2,),
            [pl.BlockSpec((DEVS * 8, GW), lambda i: (0, G_AT // GW + odd)), at_spec, cols, cols,
             pl.BlockSpec((EDGE, GW), lambda i: (0, 2 * i + odd)), per_pair, per_pair,
             pl.BlockSpec((EDGE, LANES), lambda i: (0, i)), pl.BlockSpec((EDGE, LANES), lambda i: (0, G // 2 + i)),
             whole((TOK, LANES)), pl.BlockSpec((1, H // G, TOK), lambda i: (2 * i + odd, 0, 0)),
             whole((TOK, LANES)), whole((1, H))] + [anywhere] * len(more),
            [own_cols, own_cols, pl.BlockSpec((1, TOK, N), lambda i: (i, 0, 0)), whole((8, LANES))],
            scratch=[pltpu.VMEM((TOK, LANES), bf16), pltpu.VMEM((TOK, LANES), f32),
                     pltpu.VMEM((GW // LANES, DEVS * 8, LANES), f32), pltpu.VMEM((TOK, GW), f32), pltpu.VMEM((TOK, GW), f32), pltpu.VMEM((SPAN, GW), f32),
                     pltpu.VMEM((TOK, GW), f32), pltpu.VMEM((TOK, GW), f32)],
            est=cost(6_000_000_000, 8_000_000, 2_000_000),
            name=f"local{odd}",
        )(recv, at, far(text_gate), *map(far, (conv, edge, inputs, outputs, edge_p, edge_p, cum, by_head, size, skip_gain[None, :])), *more)

    even = rows_own(0, ())
    entries, bound = call(
        scan_kernel,
        (struct(G * N, GW), near(8, LANES, dtype=f32)),
        (1,),
        [scalar, vmem, vmem],
        [whole((G * N, GW)), vmem],
        scratch=[pltpu.VMEM((G * N, GW), f32)],
        est=cost(2 * 512 * 512 * 128, 1_200_000),
        name="scan",
    )(dev, states, kept(even[3]))
    entry = kept(exchange(entries))
    odds = rows_own(1, (bound,))

    return call(
        final_kernel,
        struct(TOK, E),
        (1,),
        [vmem, vmem] + [hbm] * 7,
        hbm,
        scratch=[pltpu.VMEM((1, E), f32), pltpu.VMEM((G, TOK, N), bf16), pltpu.VMEM((G, TOK, GW), bf16), pltpu.VMEM((G, TOK, GW), bf16),
                 pltpu.VMEM((TOK, E), bf16), pltpu.VMEM((G * N, GW), f32), pltpu.VMEM((2, TOK, GW), f32),
                 sems(()), sems((2,)), sems((G,)), sems((G,)), sems((G,))],
        est=cost(2 * 256 * 64 * 4096, 11_000_000),
        name="final",
    )(kept(bound), entry, far(norm_gain[None, :]), *map(far, (even[2], odds[2], even[0], even[1], odds[0], odds[1])))


def solution(mesh):
    rows = P(("dp", "ctx"), None)
    specs = (rows,) * 8 + (P("dp"),) * 2 + (P(),) * 6
    return jax.shard_map(shards, mesh=mesh, in_specs=specs, out_specs=rows, check_vma=False)
```

```python
import functools

import jax
import jax.numpy as jnp
from jax import lax
from jax.experimental import pallas as pl
from jax.experimental.pallas import tpu as pltpu
from jax.sharding import PartitionSpec as P

H = 64
P_SIZE = 64
N = 64
G = 8
SPAN = 128
KCONV = 4
E = 4096
TOK = 256
TILE = 64
DEVS = 64
GW = E // G
PW = 2 * G * N
EDGE = 16
LANES = 128
QUART = 4
V_AT, P_AT, S_AT = 0, 1024, 1280
CHUNK = 1408
G_CHUNK = 1024
STATE_W = GW + LANES

f32 = jnp.float32
bf16 = jnp.bfloat16
MIB = 1024 * 1024
VMEM_MIB = 32


def cost(flops, size, trans=0):
    return pl.CostEstimate(flops=flops, bytes_accessed=size, transcendentals=trans)


def whole(shape):
    return pl.BlockSpec(shape, lambda *_: (0,) * len(shape))


def group_cols(g):
    return pl.ds(pl.multiple_of(g * GW, GW), GW)


def iota(shape, dim):
    return lax.broadcasted_iota(jnp.int32, shape, dim)


def dot(a, b):
    return jnp.dot(a, b, preferred_element_type=f32)


def dot_rows(a, b):
    return lax.dot_general(a, b, (((0,), (0,)), ((), ())), preferred_element_type=f32)


def dot_cols(a, b):
    return lax.dot_general(a, b, (((1,), (1,)), ((), ())), preferred_element_type=f32)


def dot_whole(a, b):
    high = b.astype(bf16)
    low = (b - high.astype(f32)).astype(bf16)
    return dot(jnp.concatenate([a, a], axis=1), jnp.concatenate([high, low], axis=0))


def silu(x):
    half = 0.5 * x
    return half + half * jnp.tanh(half)


def split2(x):
    high = x.astype(bf16)
    low = (x - high.astype(f32)).astype(bf16)
    return jnp.where(iota(x.shape, 1) < H, high.astype(f32), low.astype(f32)).astype(bf16)


def expander(group):
    head = iota((LANES, GW), 0) & (H - 1)
    col = group * (H // G) + (iota((LANES, GW), 1) >> 6)
    return jnp.where(head == col, 1.0, 0.0).astype(bf16)


def slot_keys(pos_ref):
    dev = lax.axis_index("ctx")
    row = pos_ref[pl.ds(dev // 2, 1), :]
    other = pltpu.roll(row, 64, 1)
    lane = iota((1, LANES), 1)
    own = jnp.where((lane >> 6) == lax.rem(dev, 2), row, other)
    key = (own >> 8) * 8 + (lane & 1) * QUART + (lane >> 6)
    keys = jnp.concatenate([key, key + 2], axis=1)
    return jnp.where(iota((DEVS * 8, 2 * LANES), 0) == keys, 1.0, 0.0).astype(bf16)


def quarters(ref, width, low, count):
    return jnp.concatenate([ref[:, b * width + low : b * width + low + count] for b in range(QUART)], axis=0)


def pack_kernel(
    pos_hbm, step_hbm, val_hbm, proj_hbm, out_hbm,
    pos_ref, step_ref, val_ref, proj_ref, out_ref, in_sem, out_sem,
):
    pairs = ((pos_hbm, pos_ref), (step_hbm, step_ref), (proj_hbm, proj_ref), (val_hbm, val_ref))
    loads = [pltpu.make_async_copy(src, dst, in_sem.at[i]) for i, (src, dst) in enumerate(pairs)]
    for load in loads:
        load.start()
    loads[0].wait()
    pick = slot_keys(pos_ref)
    loads[1].wait()
    step = step_ref[...]
    out_ref[:, S_AT:] = dot(pick[:, :TILE], jnp.concatenate([step, step], axis=1)).astype(bf16)
    loads[2].wait()
    out_ref[:, P_AT:S_AT] = dot(pick, quarters(proj_ref, 256, 0, 256)).astype(bf16)
    loads[3].wait()
    stores = []
    for i, (low, high) in enumerate(((P_AT, CHUNK), (0, GW), (GW, 2 * GW))):
        if i:
            out_ref[:, low:high] = dot(pick, quarters(val_ref, 1024, low, GW)).astype(bf16)
        store = pltpu.make_async_copy(out_ref.at[:, low:high], out_hbm.at[:, low:high], out_sem.at[i])
        store.start()
        stores.append(store)
    for store in stores:
        store.wait()


def gate_kernel(pos_ref, gate_ref, at_ref, step_ref, slot_ref, out_ref):
    pick = slot_keys(pos_ref)
    for low in (0, GW):
        out_ref[:, low : low + GW] = dot(pick, quarters(gate_ref, 1024, low, GW)).astype(bf16)


def rim_kernel(slot_ref, recv_ref, val_ref, proj_ref, out_ref):
    count = KCONV - 1
    slots = [slot_ref[i] for i in range(count)]
    starts = [jnp.maximum(k, 0) * QUART for k in slots]
    rows = [recv_ref[pl.ds(pl.multiple_of((k >> 4) * 16, 16), 16), :] for k in starts]
    rows = jnp.concatenate(rows, axis=0)
    row, col = iota((EDGE, 16 * count), 0), iota((EDGE, 16 * count), 1)
    at = jnp.full((EDGE, 16 * count), -16, jnp.int32)
    taken = jnp.full((EDGE, 1), -1, jnp.int32)
    for i, k in enumerate(starts):
        at = jnp.where(row == EDGE - count + i, 16 * i + (k & 15), at)
        taken = jnp.where(iota((EDGE, 1), 0) == EDGE - count + i, slots[i], taken)
    for b in range(QUART):
        place = jnp.where(col == at + b, 1.0, 0.0).astype(bf16)
        tile = dot(place, rows[:, V_AT:P_AT])
        cols = slice(b * 1024, (b + 1) * 1024)
        out_ref[:, cols] = jnp.where(taken >= 0, tile, val_ref[:, cols].astype(f32)).astype(bf16)
        tile = dot(place, rows[:, P_AT:S_AT])
        cols = slice(b * 256, (b + 1) * 256)
        out_ref[:, E + b * 256 : E + (b + 1) * 256] = jnp.where(
            taken >= 0, tile, proj_ref[:, cols].astype(f32)
        ).astype(bf16)


def placement(at_ref):
    return jnp.where(iota((TOK, LANES), 0) == at_ref[...], 1.0, 0.0).astype(bf16)


def spread_out(recv, wide_ref):
    for k in range(recv.shape[1] // LANES):
        wide_ref[k] = recv[:, k * LANES : (k + 1) * LANES].astype(f32)


def quarter_rows(wide_ref, b, count):
    rows = [wide_ref[k, pl.ds(b, 2 * DEVS, stride=QUART), :] for k in range(count)]
    return jnp.concatenate(rows, axis=1).astype(bf16)


def conv_chunk(x, before, weights, bias):
    ext = jnp.concatenate([before, x], axis=0)
    total = bias + weights[KCONV - 1 : KCONV, :] * x
    for back in range(1, KCONV):
        total = total + weights[KCONV - 1 - back : KCONV - back, :] * pltpu.roll(ext, back, 0)[8:]
    return silu(total).astype(bf16)


CHUNK_ROWS = 64


def conv_columns(tile_ref, text_ref, taken_ref, cols, weights, bias, use):
    before = jnp.zeros((8, LANES), f32)
    for low in range(0, TOK, CHUNK_ROWS):
        rows = slice(low, low + CHUNK_ROWS)
        x = jnp.where(taken_ref[rows, :] > 0, tile_ref[rows, cols], text_ref[rows, cols].astype(f32))
        use(rows, x, conv_chunk(x, before, weights, bias))
        before = x[CHUNK_ROWS - 8 :]


def softplus(v):
    return jnp.maximum(v, 0.0) + jnp.log1p(jnp.exp(-jnp.abs(v)))


def three(x):
    a = x.astype(bf16)
    left = x - a.astype(f32)
    b = left.astype(bf16)
    return a, b, (left - b.astype(f32)).astype(bf16)


def order(i):
    return lax.rem(i, G // 2) * 2 + i // (G // 2)


def place_kernel(
    recv_hbm, val_hbm, proj_hbm, at_hbm, step_hbm, w_hbm, b_hbm, sbias_hbm, dlog_hbm,
    conv_hbm, in_hbm, out_hbm, state_ref, cum_ref, size_ref, total_ref, hv_ref, hp_ref, we_ref,
    at_ref, step_ref, w_ref, b_ref, sbias_ref, dlog_ref,
    recv_ref, val_ref, proj_ref, conv_ref, in_ref, out_ref, place_scr, taken_scr, wide_scr, tail_scr,
    tile_scr, weight_scr, part_scr, small_sem, recv_sem, val_sem, proj_sem, conv_sem, bc_sem,
):
    def load(i):
        cols = group_cols(order(i))
        return pltpu.make_async_copy(val_hbm.at[:, cols], val_ref.at[:, cols], val_sem.at[i])

    def store(i):
        cols = group_cols(order(i))
        return pltpu.make_async_copy(conv_ref.at[:, cols], conv_hbm.at[:, cols], conv_sem.at[i])

    def arrived(i, low, high):
        return pltpu.make_async_copy(recv_hbm.at[:, low:high], recv_ref.at[:, low:high], recv_sem.at[i])

    load_proj = pltpu.make_async_copy(proj_hbm, proj_ref, proj_sem)
    pieces = [arrived(0, P_AT, CHUNK), arrived(1, 0, GW), arrived(2, GW, 2 * GW)]
    store_bc = [
        pltpu.make_async_copy(src, dst, bc_sem.at[i])
        for i, (src, dst) in enumerate(((in_ref, in_hbm), (out_ref, out_hbm)))
    ]
    pairs = (
        (at_hbm, at_ref), (w_hbm, w_ref), (b_hbm, b_ref), (step_hbm, step_ref), (sbias_hbm, sbias_ref), (dlog_hbm, dlog_ref),
    )
    small = [pltpu.make_async_copy(src, dst, small_sem.at[i]) for i, (src, dst) in enumerate(pairs)]
    small[0].start()
    pieces[0].start()
    load_proj.start()
    for load_small in small[1:]:
        load_small.start()
    pieces[1].start()
    for i in range(G // 2):
        load(i).start()
    pieces[2].start()
    for i in range(G // 2, G):
        load(i).start()

    def first():
        small[0].wait()
        place_scr[...] = placement(at_ref)
        taken_scr[...] = dot(place_scr[...], jnp.ones((LANES, LANES), bf16))
        for load_small in small[1:]:
            load_small.wait()
        pieces[0].wait()
        spread_out(recv_ref[:, P_AT:], wide_scr)
        load_proj.wait()
        for b in range(QUART):
            tile_scr[0, :, :256] = dot(place_scr[...], quarter_rows(wide_scr, b, 2))
            for half in range(2):
                pair = b * 2 + half
                cols = slice(pair * LANES, (pair + 1) * LANES)

                def use(rows, x, y, pair=pair, cols=cols):
                    if rows.start == 0:
                        hp_ref[:, cols] = x[:EDGE].astype(bf16)
                    if pair < G // 2:
                        in_ref[pair, rows, :] = y
                    else:
                        out_ref[pair - G // 2, rows, :] = y

                at = slice(E + pair * LANES, E + (pair + 1) * LANES)
                conv_columns(
                    tile_scr.at[0, :, half * LANES : (half + 1) * LANES], proj_ref.at[:, cols], taken_scr,
                    slice(None), w_ref[:, at], b_ref[:, at], use,
                )
        for copy in store_bc:
            copy.start()
        steps = wide_scr[2, pl.ds(0, 2 * DEVS, stride=QUART), :].astype(bf16)
        tile = dot(place_scr[...], steps)
        step = step_ref[...].astype(f32)
        step = jnp.where(taken_scr[...] > 0, tile, jnp.concatenate([step, step], axis=1))
        sbias, dlog = sbias_ref[...], dlog_ref[...]
        size = softplus(step + jnp.concatenate([sbias, sbias], axis=1))
        logs = -jnp.exp(jnp.concatenate([dlog, dlog], axis=1)) * size
        size_ref[...] = size
        lower = jnp.where(iota((SPAN, SPAN), 0) >= iota((SPAN, SPAN), 1), 1.0, 0.0).astype(bf16)
        cums = []
        for k in range(TOK // SPAN):
            parts = three(logs[k * SPAN : (k + 1) * SPAN])
            cums.append(dot(lower, parts[0]) + (dot(lower, parts[1]) + dot(lower, parts[2])))
        last = [c[SPAN - 1 : SPAN, :] for c in cums]
        for k, c in enumerate(cums):
            rows = slice(k * SPAN, (k + 1) * SPAN)
            cum_ref[rows, :] = c
            left = last[k] - c
            if k == 0:
                left = left + last[1]
            tail_scr[rows, :] = split2(jnp.exp(left) * size[rows])
        total_ref[...] = jnp.broadcast_to(jnp.exp(last[0] + last[1]), total_ref.shape)

    first()
    for odd in range(2):
        pieces[1 + odd].wait()
        spread_out(recv_ref[:, odd * GW : (odd + 1) * GW], wide_scr)

        @pl.loop(0, G // 4)
        def _(two, odd=odd):
            for slot in range(2):
                load(odd * (G // 2) + 2 * two + slot).wait()
            for slot in range(2):
                pair = 2 * two + slot
                g = 2 * pair + odd
                tile_scr[slot] = dot(place_scr[...], quarter_rows(wide_scr, pair, GW // LANES))
                weight_scr[slot] = dot(tail_scr[...], expander(g))
                we_ref[:, group_cols(g)] = weight_scr[slot, :EDGE, :]
                for k in range(GW // LANES):
                    cols = pl.ds(pl.multiple_of(g * GW + k * LANES, LANES), LANES)
                    part = slice(k * LANES, (k + 1) * LANES)

                    def use(rows, x, y, cols=cols, part=part, slot=slot):
                        if rows.start == 0:
                            hv_ref[:, cols] = x[:EDGE].astype(bf16)
                        conv_ref[rows, cols] = y
                        weight = weight_scr[slot, rows, part]
                        part_scr[slot, rows, part] = (y.astype(f32) * weight).astype(bf16)

                    conv_columns(
                        tile_scr.at[slot, :, part], val_ref.at[:, cols], taken_scr, slice(None),
                        w_ref[:, cols], b_ref[:, cols], use,
                    )
            for slot in range(2):
                pair = 2 * two + slot
                rows = pl.ds(pl.multiple_of((2 * pair + odd) * N, N), N)
                b_g = in_ref[pair, EDGE:, odd * N : (odd + 1) * N]
                state_ref[rows, :] = dot_rows(b_g, part_scr[slot, EDGE:, :])
            for slot in range(2):
                store(odd * (G // 2) + 2 * two + slot).start()

    for copy in store_bc:
        copy.wait()
    for i in range(G):
        store(i).wait()


def power8(s):
    s2 = s * s
    s4 = s2 * s2
    s8 = s4 * s4
    return jnp.where(s < 0, -s8, s8).astype(bf16)


def root8(code):
    code = code.astype(f32)
    size = jnp.exp(0.125 * jnp.log(jnp.abs(code)))
    return jnp.where(code < 0, -size, size)


FLOOR = 1e-30


def edge_kernel(
    rim_ref, hv_ref, hp_ref, w_ref, b_ref, we_ref, total_ref, state_ref,
    send_ref, conv_ref, proj_ref,
    full_scr,
):
    def conv(x_ref, at, columns):
        before = rim_ref[EDGE - 8 :, columns].astype(f32)
        return conv_chunk(x_ref[:, at].astype(f32), before, w_ref[:, columns], b_ref[:, columns])

    p = [conv(hp_ref, slice(k * LANES, (k + 1) * LANES), slice(E + k * LANES, E + (k + 1) * LANES)) for k in range(PW // LANES)]
    p = jnp.concatenate(p, axis=1)
    proj_ref[...] = p
    top = jnp.zeros((8, LANES), f32)
    for g in range(G):
        b_g = p[:, g * N : (g + 1) * N]
        cols = slice(g * GW, (g + 1) * GW)
        y = conv(hv_ref, cols, cols)
        conv_ref[:, cols] = y
        rows = slice(g * N, (g + 1) * N)
        state = state_ref[rows, :] + dot_rows(b_g, (y.astype(f32) * we_ref[:, cols]).astype(bf16))
        full_scr[rows, :] = state
        sums = jnp.abs(state[:8])
        for k in range(8, N, 8):
            sums = sums + jnp.abs(state[k : k + 8])
        top = top + dot_cols(sums.astype(bf16), expander(g))
    top = jnp.maximum(jnp.sum(top, axis=0, keepdims=True) * 2.0**-14, FLOOR).astype(bf16).astype(f32)
    top = jnp.where(iota((8, LANES), 1) < H, top, 0.0)
    for g in range(G):
        back = 1.0 / dot(top.astype(bf16), expander(g))[:1]
        for low in range(g * N, (g + 1) * N, 32):
            send_ref[low : low + 32, :GW] = power8(full_scr[low : low + 32, :] * back)
    decay = split2(total_ref[...]).astype(f32)
    odd = (iota((8, LANES), 0) & 1) == 1
    side = jnp.where(odd, top, decay).astype(bf16)
    side = jnp.concatenate([side, side], axis=0)
    for low in range(0, G * N, 16):
        send_ref[low : low + 16, GW:] = side


def scan_kernel(dev_ref, recv_ref, after_ref, out_ref, bound_ref, side_scr):
    dev = dev_ref[0]
    side_scr[...] = dot(recv_ref[:, GW:], expander(dev // 8))

    def code(state, bound):
        return state * (1.0 / jnp.maximum(bound, FLOOR))

    def two(i, carry):
        rows = pl.ds(pl.multiple_of(i * 16, 16), 16)
        first, bound, own = carry
        state = root8(recv_ref[rows, :GW])
        side = side_scr[rows, :]
        second = side[:1] * first + state[:8] * side[1:2]
        second_bound = side[:1] * bound + side[1:2]
        out_ref[rows, :] = power8(jnp.concatenate([code(first, bound), code(second, second_bound)], axis=0))
        part = recv_ref[rows, GW:].astype(f32)
        part = part + pltpu.roll(part, H, 1)
        own = jnp.where(2 * i < dev, part[:1] * own + part[1:2], own)
        own = jnp.where(2 * i + 1 < dev, part[8:9] * own + part[9:10], own)
        return (
            side[8:9] * second + state[8:] * side[9:10],
            side[8:9] * second_bound + side[9:10],
            own,
        )

    zeros = (jnp.zeros((8, GW), f32), jnp.zeros((1, GW), f32), jnp.zeros((1, LANES), f32))
    own = lax.fori_loop(0, DEVS // 2, two, zeros, unroll=8)[2]
    bound_ref[...] = jnp.broadcast_to(own, bound_ref.shape)


def local_kernel(
    odd, recv_ref, at_ref, gate_ref, conv_ref, edge_ref, in_ref, out_ref, ein_ref, eout_ref,
    cum_ref, cumt_ref, size_ref, skip_ref, *rest,
):
    mix_out, scale_out, query_ref, token_ref, place_scr, taken_scr, wide_scr, gate_scr, weighted_scr, first_scr, mix_ref, scale_ref = rest[-12:]
    token_ref[...] = jnp.zeros_like(token_ref)
    i = pl.program_id(0)
    g = 2 * i + odd

    @pl.when(i == 0)
    def _():
        place_scr[...] = placement(at_ref)
        taken_scr[...] = dot(place_scr[...], jnp.ones((LANES, LANES), bf16))
        spread_out(recv_ref[...], wide_scr)

    def patched(edge, rest):
        return jnp.concatenate([edge, rest[EDGE:]], axis=0)

    half = slice(odd * N, (odd + 1) * N)
    b_g = patched(ein_ref[:, half], in_ref[0, :, half])
    c_g = patched(eout_ref[:, half], out_ref[0, :, half])
    query_ref[0] = c_g
    cum = cum_ref[...]
    spread = expander(g)
    skip = skip_ref[...]
    skip = jnp.broadcast_to(jnp.concatenate([skip, skip], axis=1), (8, LANES))
    skip = dot(split2(skip), spread)[:1]
    last = cum[SPAN - 1 : SPAN, :]
    upto = jnp.concatenate([cum[:SPAN], cum[SPAN:] + last], axis=0)
    scale_ref[...] = dot(split2(jnp.exp(upto)), spread)
    weighted_scr[...] = dot(split2(size_ref[...]), spread)
    gate_scr[...] = dot(place_scr[...], quarter_rows(wide_scr, i, GW // LANES))
    own = pltpu.roll(cum, lax.rem(LANES - g * (H // G), LANES), 1)
    for low in range(0, TOK, 32):
        rows = slice(low, low + 32)
        taken = taken_scr[rows, :] > 0
        for k in range(GW // LANES):
            cols = slice(k * LANES, (k + 1) * LANES)
            gate = silu(jnp.where(taken, gate_scr[rows, cols], gate_ref[rows, cols].astype(f32)))
            gate_scr[rows, cols] = gate
            scale_out[rows, cols] = (scale_ref[rows, cols] * gate).astype(bf16)
            x = conv_ref[rows, cols]
            if low == 0:
                x = patched(edge_ref[:, cols], x)
            x = x.astype(f32)
            weighted_scr[rows, cols] = weighted_scr[rows, cols] * x
            mix_ref[rows, cols] = skip[:, cols] * x
    tail = dot(split2(jnp.exp(last - cum[:SPAN])), spread)
    inner = dot(split2(jnp.exp(cum[SPAN:])), spread)
    state = dot_rows(b_g[:SPAN], (weighted_scr[:SPAN] * tail).astype(bf16))
    first_scr[...] = dot_whole(c_g[SPAN:], state) * inner
    causal = iota((SPAN, SPAN), 0) >= iota((SPAN, SPAN), 1)
    lane = iota((SPAN, LANES), 1)
    for k in range(TOK // SPAN):
        rows = slice(k * SPAN, (k + 1) * SPAN)
        scores = jnp.where(causal, dot_cols(c_g[rows], b_g[rows]), 0.0)
        for pair in range(H // G // 2):
            kernels = []
            for head in (2 * pair, 2 * pair + 1):
                apart = own[rows, head : head + 1] - cumt_ref[0, head : head + 1, rows]
                kernels.append((jnp.exp(jnp.minimum(apart, 0.0)) * scores).astype(bf16))
            cols = slice(pair * LANES, (pair + 1) * LANES)
            w = weighted_scr[rows, cols]
            low = jnp.where(lane < P_SIZE, w, 0.0).astype(bf16)
            high = jnp.where(lane < P_SIZE, 0.0, w).astype(bf16)
            mixed = dot(jnp.concatenate(kernels, axis=1), jnp.concatenate([low, high], axis=0))
            mixed = mixed + mix_ref[rows, cols]
            if k == 1:
                mixed = mixed + first_scr[:, cols]
            mix_out[rows, cols] = (mixed * gate_scr[rows, cols]).astype(bf16)


def final_kernel(
    bound_ref, entry_ref, gain_hbm, qe_hbm, qo_hbm, me_hbm, se_hbm, mo_hbm, so_hbm, out_hbm,
    gain_ref, query_ref, mix_ref, scale_ref, out_ref, entry_scr, part_scr, gain_sem, query_sem, mix_sem, scale_sem, out_sem,
):
    gain = pltpu.make_async_copy(gain_hbm, gain_ref, gain_sem)
    queries = [
        pltpu.make_async_copy(src, query_ref.at[i * G // 2 : (i + 1) * G // 2], query_sem.at[i])
        for i, src in enumerate((qe_hbm, qo_hbm))
    ]
    mixes, scales, stores = [], [], []
    for i in range(G):
        cols = slice(i % (G // 2) * GW, (i % (G // 2) + 1) * GW)
        mix, scale = (me_hbm, se_hbm) if i < G // 2 else (mo_hbm, so_hbm)
        mixes.append(pltpu.make_async_copy(mix.at[:, cols], mix_ref.at[i], mix_sem.at[i]))
        scales.append(pltpu.make_async_copy(scale.at[:, cols], scale_ref.at[i], scale_sem.at[i]))
        g = i % (G // 2) * 2 + i // (G // 2)
        cols = slice(g * GW, (g + 1) * GW)
        stores.append(pltpu.make_async_copy(out_ref.at[:, cols], out_hbm.at[:, cols], out_sem.at[i]))
    for load in (*queries, gain, *(c for pair in zip(mixes, scales) for c in pair)):
        load.start()
    bound = split2(jnp.maximum(bound_ref[...], FLOOR))
    for g in range(G):
        rows = slice(g * N, (g + 1) * N)
        entry_scr[rows, :] = root8(entry_ref[rows, :]) * dot(bound, expander(g))[:1]
    for load in (*queries, gain):
        load.wait()
    for i in range(G):
        g = i % (G // 2) * 2 + i // (G // 2)
        if i % 2 == 0:
            for load in (*mixes[i : i + 2], *scales[i : i + 2]):
                load.wait()
        slot = i % 2
        own = dot_whole(query_ref[i], entry_scr[g * N : (g + 1) * N, :])
        squares = jnp.zeros((TOK, LANES), f32)
        for k in range(GW // LANES):
            cols = slice(k * LANES, (k + 1) * LANES)
            part = mix_ref[i, :, cols].astype(f32) + scale_ref[i, :, cols].astype(f32) * own[:, cols]
            part_scr[slot, :, cols] = part
            squares = squares + part * part
        high = squares.astype(bf16)
        low = (squares - high.astype(f32)).astype(bf16)
        mean = dot(jnp.concatenate([high, low], axis=1), jnp.ones((2 * LANES, LANES), bf16)) * (1.0 / GW)
        mean = lax.rsqrt(mean + 1e-05)
        for k in range(GW // LANES):
            cols = slice(k * LANES, (k + 1) * LANES)
            at = slice(g * GW + k * LANES, g * GW + (k + 1) * LANES)
            out_ref[:, at] = (part_scr[slot, :, cols] * mean * gain_ref[:, at]).astype(bf16)
        if i % 2 == 1:
            stores[i - 1].start()
            stores[i].start()
    for store in stores:
        store.wait()


def call(kernel, outs, grid, in_specs, out_specs, scratch=(), est=None, name=None, vmem=VMEM_MIB, alias=None):
    return pl.pallas_call(
        kernel,
        out_shape=outs,
        grid_spec=pltpu.PrefetchScalarGridSpec(
            num_scalar_prefetch=0,
            grid=grid,
            in_specs=in_specs,
            out_specs=out_specs,
            scratch_shapes=scratch,
        ),
        compiler_params=pltpu.CompilerParams(vmem_limit_bytes=vmem * MIB),
        input_output_aliases=alias or {},
        cost_estimate=est,
        name=name,
    )


def struct(*shape, dtype=bf16):
    return pltpu.HBM(shape, dtype)


def near(*shape, dtype=bf16):
    return pltpu.VMEM(shape, dtype)


def far(a):
    return pltpu.with_memory_space_constraint(a, pltpu.HBM)


def kept(a):
    return pltpu.with_memory_space_constraint(a, pltpu.VMEM)


def exchange(rows):
    return lax.all_to_all(rows, "ctx", split_axis=0, concat_axis=0, tiled=True)


def twice(a):
    return jnp.concatenate([a, a], axis=-1)


def shards(
    text_values, text_gate, text_proj, text_step, tile_values, tile_gate, tile_proj, tile_step,
    tile_position, tile_count, conv_weight, conv_bias, step_bias, decay_log, skip_gain, norm_gain,
):
    device = lax.axis_index("ctx")
    scalar = pl.BlockSpec(memory_space=pltpu.SMEM)
    dev = device.reshape(1).astype(jnp.int32)

    hbm = pl.BlockSpec(memory_space=pl.ANY)
    vmem = pl.BlockSpec(memory_space=pltpu.VMEM)
    sems = pltpu.SemaphoreType.DMA
    positions = tile_position.reshape(32, LANES)
    packed = call(
        pack_kernel,
        struct(DEVS * 8, CHUNK),
        (1,),
        [hbm] * 4,
        hbm,
        scratch=[pltpu.VMEM((32, LANES), jnp.int32), pltpu.VMEM((TILE, H), bf16), pltpu.VMEM((TILE, E), bf16),
                 pltpu.VMEM((TILE, PW), bf16), pltpu.VMEM((DEVS * 8, CHUNK), bf16), sems((4,)), sems((3,))],
        est=cost(2 * 512 * 256 * CHUNK, 3_000_000),
        name="pack",
    )(far(positions), far(tile_step), far(tile_values), far(tile_proj))
    recv = exchange(packed)
    position = tile_position.reshape(DEVS, TILE)
    ids = jnp.arange(TILE, dtype=jnp.int32)
    landing = ((position >> 8) == device) & (ids[None, :] < tile_count[:, None])
    local = jnp.where(landing, position & (TOK - 1), -1)
    at = jnp.max(local.reshape(DEVS, TILE // 2, 2), axis=1).reshape(1, 2 * DEVS)
    ends = jnp.arange(TOK - KCONV + 1, TOK)[:, None]
    rim_slot = jnp.max(jnp.where(at == ends, jnp.arange(2 * DEVS)[None, :], -1), axis=1)
    at = far(at)
    steps = far(text_step)
    gates = call(
        gate_kernel,
        struct(DEVS * 8, G_CHUNK),
        (1,),
        [whole((32, LANES)), whole((TILE, E)), hbm, hbm, hbm],
        whole((DEVS * 8, G_CHUNK)),
        est=cost(2 * 512 * 256 * G_CHUNK, 2_000_000),
        name="gates",
    )(far(positions), far(tile_gate), at, steps, rim_slot)
    gates, recv = lax.optimization_barrier((gates, recv))
    recv = kept(recv)
    recv_gate = exchange(gates)

    bias = conv_bias[None, :]

    recv_spec = whole((DEVS * 8, CHUNK))
    at_spec = whole((1, 2 * DEVS))
    rim = call(
        rim_kernel,
        struct(EDGE, E + PW),
        (1,),
        [scalar, vmem,
         pl.BlockSpec((EDGE, E), lambda i: (TOK // EDGE - 1, 0)),
         pl.BlockSpec((EDGE, PW), lambda i: (TOK // EDGE - 1, 0))],
        whole((EDGE, E + PW)),
        est=cost(2 * 16 * 48 * 5120, 3_000_000),
        name="rim",
    )(rim_slot, recv, far(text_values), far(text_proj))
    rim = lax.ppermute(rim, "ctx", [(i, i + 1) for i in range(DEVS - 1)])

    conv, inputs, outputs, state, cum, size, total, head_v, head_p, tail = call(
        place_kernel,
        (
            struct(TOK, E), struct(G // 2, TOK, LANES), struct(G // 2, TOK, LANES), near(G * N, GW, dtype=f32),
            struct(TOK, LANES, dtype=f32), struct(TOK, LANES, dtype=f32),
            near(8, LANES, dtype=f32),
            near(EDGE, E), near(EDGE, PW), near(EDGE, E, dtype=f32),
        ),
        (1,),
        [hbm] * 9,
        [hbm, hbm, hbm, vmem, whole((TOK, LANES)), whole((TOK, LANES)), vmem, vmem, vmem, vmem],
        scratch=[pltpu.VMEM((1, 2 * DEVS), jnp.int32), pltpu.VMEM((TOK, H), bf16), pltpu.VMEM((KCONV, E + PW), f32),
                 pltpu.VMEM((1, E + PW), f32), pltpu.VMEM((1, H), f32), pltpu.VMEM((1, H), f32),
                 pltpu.VMEM((DEVS * 8, CHUNK), bf16), pltpu.VMEM((TOK, E), bf16), pltpu.VMEM((TOK, PW), bf16),
                 pltpu.VMEM((TOK, E), bf16), pltpu.VMEM((G // 2, TOK, LANES), bf16), pltpu.VMEM((G // 2, TOK, LANES), bf16),
                 pltpu.VMEM((TOK, LANES), bf16), pltpu.VMEM((TOK, LANES), f32),
                 pltpu.VMEM((GW // LANES, DEVS * 8, LANES), f32), pltpu.VMEM((TOK, LANES), bf16),
                 pltpu.VMEM((2, TOK, GW), f32), pltpu.VMEM((2, TOK, GW), f32), pltpu.VMEM((2, TOK, GW), bf16),
                 sems((6,)), sems((3,)), sems((G,)), sems(()), sems((G,)), sems((2,))],
        est=cost(2 * 256 * 512 * 5120, 10_000_000, 1_300_000),
        name="place",
    )(recv, far(text_values), far(text_proj), at, steps, far(conv_weight), far(bias),
      far(step_bias[None, :]), far(decay_log[None, :]))

    send, edge, edge_p = call(
        edge_kernel,
        (struct(G * N, STATE_W), struct(EDGE, E), struct(EDGE, PW)),
        (1,),
        [vmem, vmem, vmem, whole((KCONV, E + PW)), whole((1, E + PW)), vmem, vmem, vmem],
        [whole((G * N, STATE_W)), whole((EDGE, E)), whole((EDGE, PW))],
        scratch=[pltpu.VMEM((G * N, GW), f32)],
        est=cost(2 * 64 * 16 * 4096, 2_000_000, 100_000),
        name="edge",
    )(kept(rim), kept(head_v), kept(head_p), far(conv_weight), far(bias), kept(tail), kept(total), kept(state))
    send, recv_gate = lax.optimization_barrier((send, recv_gate))
    states = kept(exchange(send))

    by_head = cum[:, :H].T.reshape(G, H // G, TOK)

    def rows_own(odd, more):
        per_pair = pl.BlockSpec((1, TOK, LANES), lambda i: (i, 0, 0))
        cols = pl.BlockSpec((TOK, GW), lambda i: (0, 2 * i + odd))
        own_cols = pl.BlockSpec((TOK, GW), lambda i: (0, i))
        anywhere = pl.BlockSpec(memory_space=pl.ANY)
        return call(
            functools.partial(local_kernel, odd),
            (struct(TOK, E // 2), struct(TOK, E // 2), struct(G // 2, TOK, N), near(8, LANES, dtype=f32)),
            (G // 2,),
            [pl.BlockSpec((DEVS * 8, GW), lambda i: (0, odd)), at_spec, cols, cols,
             pl.BlockSpec((EDGE, GW), lambda i: (0, 2 * i + odd)), per_pair, per_pair,
             pl.BlockSpec((EDGE, LANES), lambda i: (0, i)), pl.BlockSpec((EDGE, LANES), lambda i: (0, G // 2 + i)),
             whole((TOK, LANES)), pl.BlockSpec((1, H // G, TOK), lambda i: (2 * i + odd, 0, 0)),
             whole((TOK, LANES)), whole((1, H))] + [anywhere] * len(more),
            [own_cols, own_cols, pl.BlockSpec((1, TOK, N), lambda i: (i, 0, 0)), whole((8, LANES))],
            scratch=[pltpu.VMEM((TOK, LANES), bf16), pltpu.VMEM((TOK, LANES), f32),
                     pltpu.VMEM((GW // LANES, DEVS * 8, LANES), f32), pltpu.VMEM((TOK, GW), f32), pltpu.VMEM((TOK, GW), f32), pltpu.VMEM((SPAN, GW), f32),
                     pltpu.VMEM((TOK, GW), f32), pltpu.VMEM((TOK, GW), f32)],
            est=cost(6_000_000_000, 8_000_000, 2_000_000),
            name=f"local{odd}",
        )(recv_gate, at, far(text_gate), *map(far, (conv, edge, inputs, outputs, edge_p, edge_p, cum, by_head, size, skip_gain[None, :])), *more)

    even = rows_own(0, ())
    entries, bound = call(
        scan_kernel,
        (struct(G * N, GW), near(8, LANES, dtype=f32)),
        (1,),
        [scalar, vmem, vmem],
        [whole((G * N, GW)), vmem],
        scratch=[pltpu.VMEM((G * N, GW), f32)],
        est=cost(2 * 512 * 512 * 128, 1_200_000),
        name="scan",
    )(dev, states, kept(even[3]))
    entry = kept(exchange(entries))
    odds = rows_own(1, (bound,))

    return call(
        final_kernel,
        struct(TOK, E),
        (1,),
        [vmem, vmem] + [hbm] * 7,
        hbm,
        scratch=[pltpu.VMEM((1, E), f32), pltpu.VMEM((G, TOK, N), bf16), pltpu.VMEM((G, TOK, GW), bf16), pltpu.VMEM((G, TOK, GW), bf16),
                 pltpu.VMEM((TOK, E), bf16), pltpu.VMEM((G * N, GW), f32), pltpu.VMEM((2, TOK, GW), f32),
                 sems(()), sems((2,)), sems((G,)), sems((G,)), sems((G,))],
        est=cost(2 * 256 * 64 * 4096, 11_000_000),
        name="final",
    )(kept(bound), entry, far(norm_gain[None, :]), *map(far, (even[2], odds[2], even[0], even[1], odds[0], odds[1])))


def solution(mesh):
    rows = P(("dp", "ctx"), None)
    specs = (rows,) * 8 + (P("dp"),) * 2 + (P(),) * 6
    return jax.shard_map(shards, mesh=mesh, in_specs=specs, out_specs=rows, check_vma=False)
```

```python
import functools

import jax
import jax.numpy as jnp
from jax import lax
from jax.experimental import pallas as pl
from jax.experimental.pallas import tpu as pltpu
from jax.sharding import PartitionSpec as P

H = 64
P_SIZE = 64
N = 64
G = 8
SPAN = 128
KCONV = 4
E = 4096
TOK = 256
TILE = 64
DEVS = 64
GW = E // G
PW = 2 * G * N
EDGE = 16
LANES = 128
QUART = 4
V_AT, P_AT, S_AT = 0, 1024, 1280
CHUNK = 1408
G_CHUNK = 1024
RIM_W = 1024
STATE_W = GW + LANES

f32 = jnp.float32
bf16 = jnp.bfloat16
MIB = 1024 * 1024
VMEM_MIB = 32


def cost(flops, size, trans=0):
    return pl.CostEstimate(flops=flops, bytes_accessed=size, transcendentals=trans)


def whole(shape):
    return pl.BlockSpec(shape, lambda *_: (0,) * len(shape))


def group_cols(g):
    return pl.ds(pl.multiple_of(g * GW, GW), GW)


def iota(shape, dim):
    return lax.broadcasted_iota(jnp.int32, shape, dim)


def dot(a, b):
    return jnp.dot(a, b, preferred_element_type=f32)


def dot_rows(a, b):
    return lax.dot_general(a, b, (((0,), (0,)), ((), ())), preferred_element_type=f32)


def dot_cols(a, b):
    return lax.dot_general(a, b, (((1,), (1,)), ((), ())), preferred_element_type=f32)


def dot_whole(a, b):
    high = b.astype(bf16)
    low = (b - high.astype(f32)).astype(bf16)
    return dot(jnp.concatenate([a, a], axis=1), jnp.concatenate([high, low], axis=0))


def silu(x):
    half = 0.5 * x
    return half + half * jnp.tanh(half)


def split2(x):
    high = x.astype(bf16)
    low = (x - high.astype(f32)).astype(bf16)
    return jnp.where(iota(x.shape, 1) < H, high.astype(f32), low.astype(f32)).astype(bf16)


def expander(group):
    head = iota((LANES, GW), 0) & (H - 1)
    col = group * (H // G) + (iota((LANES, GW), 1) >> 6)
    return jnp.where(head == col, 1.0, 0.0).astype(bf16)


def slot_keys(pos_ref):
    dev = lax.axis_index("ctx")
    row = pos_ref[pl.ds(dev // 2, 1), :]
    other = pltpu.roll(row, 64, 1)
    lane = iota((1, LANES), 1)
    own = jnp.where((lane >> 6) == lax.rem(dev, 2), row, other)
    key = (own >> 8) * 8 + (lane & 1) * QUART + (lane >> 6)
    keys = jnp.concatenate([key, key + 2], axis=1)
    return jnp.where(iota((DEVS * 8, 2 * LANES), 0) == keys, 1.0, 0.0).astype(bf16)


def quarters(ref, width, low, count):
    return jnp.concatenate([ref[:, b * width + low : b * width + low + count] for b in range(QUART)], axis=0)


def pack_kernel(
    pos_hbm, step_hbm, val_hbm, proj_hbm, out_hbm,
    pos_ref, step_ref, val_ref, proj_ref, out_ref, in_sem, out_sem,
):
    pairs = ((pos_hbm, pos_ref), (step_hbm, step_ref), (proj_hbm, proj_ref), (val_hbm, val_ref))
    loads = [pltpu.make_async_copy(src, dst, in_sem.at[i]) for i, (src, dst) in enumerate(pairs)]
    for load in loads:
        load.start()
    loads[0].wait()
    pick = slot_keys(pos_ref)
    loads[1].wait()
    step = step_ref[...]
    out_ref[:, S_AT:] = dot(pick[:, :TILE], jnp.concatenate([step, step], axis=1)).astype(bf16)
    loads[2].wait()
    out_ref[:, P_AT:S_AT] = dot(pick, quarters(proj_ref, 256, 0, 256)).astype(bf16)
    loads[3].wait()
    stores = []
    for i, (low, high) in enumerate(((P_AT, CHUNK), (0, GW), (GW, 2 * GW))):
        if i:
            out_ref[:, low:high] = dot(pick, quarters(val_ref, 1024, low, GW)).astype(bf16)
        store = pltpu.make_async_copy(out_ref.at[:, low:high], out_hbm.at[:, low:high], out_sem.at[i])
        store.start()
        stores.append(store)
    for store in stores:
        store.wait()


def gate_kernel(pos_ref, gate_ref, at_ref, step_ref, slot_ref, out_ref):
    pick = slot_keys(pos_ref)
    for low in (0, GW):
        out_ref[:, low : low + GW] = dot(pick, quarters(gate_ref, 1024, low, GW)).astype(bf16)


def rim_kernel(slot_ref, recv_ref, val_ref, proj_ref, out_ref):
    count = KCONV - 1
    slots = [slot_ref[i] for i in range(count)]
    starts = [jnp.maximum(k, 0) * QUART for k in slots]
    rows = [recv_ref[pl.ds(pl.multiple_of((k >> 4) * 16, 16), 16), :] for k in starts]
    rows = jnp.concatenate(rows, axis=0)
    row, col = iota((EDGE, 16 * count), 0), iota((EDGE, 16 * count), 1)
    at = jnp.full((EDGE, 16 * count), -16, jnp.int32)
    taken = jnp.full((EDGE, 1), -1, jnp.int32)
    for i, k in enumerate(starts):
        at = jnp.where(row == EDGE - count + i, 16 * i + (k & 15), at)
        taken = jnp.where(iota((EDGE, 1), 0) == EDGE - count + i, slots[i], taken)
    blocks, proj = [], []
    for b in range(QUART):
        place = jnp.where(col == at + b, 1.0, 0.0).astype(bf16)
        tile = dot(place, rows[:, V_AT:P_AT])
        text = val_ref[:, b * RIM_W : (b + 1) * RIM_W].astype(f32)
        blocks.append(jnp.where(taken >= 0, tile, text))
        tile = dot(place, rows[:, P_AT:S_AT])
        text = proj_ref[:, b * 256 : (b + 1) * 256].astype(f32)
        proj.append(jnp.where(taken >= 0, tile, text))
    blocks.append(jnp.concatenate(proj, axis=1))
    out = blocks[0]
    row = iota((EDGE, RIM_W), 0)
    for i, block in enumerate(blocks):
        out = jnp.where((row >= i * count) & (row < (i + 1) * count), pltpu.roll(block, (i + 1) * count, 0), out)
    out_ref[...] = out.astype(bf16)


def rim_rows(rim, block):
    return pltpu.roll(rim, EDGE - (block + 1) * (KCONV - 1), 0)[EDGE - 8 :]


def placement(at_ref):
    return jnp.where(iota((TOK, LANES), 0) == at_ref[...], 1.0, 0.0).astype(bf16)


def spread_out(recv, wide_ref):
    for k in range(recv.shape[1] // LANES):
        wide_ref[k] = recv[:, k * LANES : (k + 1) * LANES].astype(f32)


def quarter_rows(wide_ref, b, count):
    rows = [wide_ref[k, pl.ds(b, 2 * DEVS, stride=QUART), :] for k in range(count)]
    return jnp.concatenate(rows, axis=1).astype(bf16)


def conv_chunk(x, before, weights, bias):
    ext = jnp.concatenate([before, x], axis=0)
    total = bias + weights[KCONV - 1 : KCONV, :] * x
    for back in range(1, KCONV):
        total = total + weights[KCONV - 1 - back : KCONV - back, :] * pltpu.roll(ext, back, 0)[8:]
    return silu(total).astype(bf16)


CHUNK_ROWS = 64


def conv_columns(tile_ref, text_ref, taken_ref, cols, weights, bias, use):
    before = jnp.zeros((8, LANES), f32)
    for low in range(0, TOK, CHUNK_ROWS):
        rows = slice(low, low + CHUNK_ROWS)
        x = jnp.where(taken_ref[rows, :] > 0, tile_ref[rows, cols], text_ref[rows, cols].astype(f32))
        use(rows, x, conv_chunk(x, before, weights, bias))
        before = x[CHUNK_ROWS - 8 :]


def softplus(v):
    return jnp.maximum(v, 0.0) + jnp.log1p(jnp.exp(-jnp.abs(v)))


def three(x):
    a = x.astype(bf16)
    left = x - a.astype(f32)
    b = left.astype(bf16)
    return a, b, (left - b.astype(f32)).astype(bf16)


def order(i):
    return lax.rem(i, G // 2) * 2 + i // (G // 2)


def place_kernel(
    recv_hbm, val_hbm, proj_hbm, at_hbm, step_hbm, w_hbm, b_hbm, sbias_hbm, dlog_hbm,
    conv_hbm, in_hbm, out_hbm, state_ref, cum_ref, size_ref, total_ref, hv_ref, hp_ref, we_ref,
    at_ref, step_ref, w_ref, b_ref, sbias_ref, dlog_ref,
    recv_ref, val_ref, proj_ref, conv_ref, in_ref, out_ref, place_scr, taken_scr, wide_scr, tail_scr,
    tile_scr, weight_scr, part_scr, small_sem, recv_sem, val_sem, proj_sem, conv_sem, bc_sem,
):
    def load(i):
        cols = group_cols(order(i))
        return pltpu.make_async_copy(val_hbm.at[:, cols], val_ref.at[:, cols], val_sem.at[i])

    def store(i):
        cols = group_cols(order(i))
        return pltpu.make_async_copy(conv_ref.at[:, cols], conv_hbm.at[:, cols], conv_sem.at[i])

    def arrived(i, low, high):
        return pltpu.make_async_copy(recv_hbm.at[:, low:high], recv_ref.at[:, low:high], recv_sem.at[i])

    load_proj = pltpu.make_async_copy(proj_hbm, proj_ref, proj_sem)
    pieces = [arrived(0, P_AT, CHUNK), arrived(1, 0, GW), arrived(2, GW, 2 * GW)]
    store_bc = [
        pltpu.make_async_copy(src, dst, bc_sem.at[i])
        for i, (src, dst) in enumerate(((in_ref, in_hbm), (out_ref, out_hbm)))
    ]
    pairs = (
        (at_hbm, at_ref), (w_hbm, w_ref), (b_hbm, b_ref), (step_hbm, step_ref), (sbias_hbm, sbias_ref), (dlog_hbm, dlog_ref),
    )
    small = [pltpu.make_async_copy(src, dst, small_sem.at[i]) for i, (src, dst) in enumerate(pairs)]
    small[0].start()
    pieces[0].start()
    load_proj.start()
    for load_small in small[1:]:
        load_small.start()
    pieces[1].start()
    for i in range(G // 2):
        load(i).start()
    pieces[2].start()
    for i in range(G // 2, G):
        load(i).start()

    def first():
        small[0].wait()
        place_scr[...] = placement(at_ref)
        taken_scr[...] = dot(place_scr[...], jnp.ones((LANES, LANES), bf16))
        for load_small in small[1:]:
            load_small.wait()
        pieces[0].wait()
        spread_out(recv_ref[:, P_AT:], wide_scr)
        load_proj.wait()
        for b in range(QUART):
            tile_scr[0, :, :256] = dot(place_scr[...], quarter_rows(wide_scr, b, 2))
            for half in range(2):
                pair = b * 2 + half
                cols = slice(pair * LANES, (pair + 1) * LANES)

                def use(rows, x, y, pair=pair, cols=cols):
                    if rows.start == 0:
                        hp_ref[:, cols] = x[:EDGE].astype(bf16)
                    if pair < G // 2:
                        in_ref[pair, rows, :] = y
                    else:
                        out_ref[pair - G // 2, rows, :] = y

                at = slice(E + pair * LANES, E + (pair + 1) * LANES)
                conv_columns(
                    tile_scr.at[0, :, half * LANES : (half + 1) * LANES], proj_ref.at[:, cols], taken_scr,
                    slice(None), w_ref[:, at], b_ref[:, at], use,
                )
        for copy in store_bc:
            copy.start()
        steps = wide_scr[2, pl.ds(0, 2 * DEVS, stride=QUART), :].astype(bf16)
        tile = dot(place_scr[...], steps)
        step = step_ref[...].astype(f32)
        step = jnp.where(taken_scr[...] > 0, tile, jnp.concatenate([step, step], axis=1))
        sbias, dlog = sbias_ref[...], dlog_ref[...]
        size = softplus(step + jnp.concatenate([sbias, sbias], axis=1))
        logs = -jnp.exp(jnp.concatenate([dlog, dlog], axis=1)) * size
        size_ref[...] = size
        lower = jnp.where(iota((SPAN, SPAN), 0) >= iota((SPAN, SPAN), 1), 1.0, 0.0).astype(bf16)
        cums = []
        for k in range(TOK // SPAN):
            parts = three(logs[k * SPAN : (k + 1) * SPAN])
            cums.append(dot(lower, parts[0]) + (dot(lower, parts[1]) + dot(lower, parts[2])))
        last = [c[SPAN - 1 : SPAN, :] for c in cums]
        for k, c in enumerate(cums):
            rows = slice(k * SPAN, (k + 1) * SPAN)
            cum_ref[rows, :] = c
            left = last[k] - c
            if k == 0:
                left = left + last[1]
            tail_scr[rows, :] = split2(jnp.exp(left) * size[rows])
        total_ref[...] = jnp.broadcast_to(jnp.exp(last[0] + last[1]), total_ref.shape)

    first()
    for odd in range(2):
        pieces[1 + odd].wait()
        spread_out(recv_ref[:, odd * GW : (odd + 1) * GW], wide_scr)

        @pl.loop(0, G // 4)
        def _(two, odd=odd):
            for slot in range(2):
                load(odd * (G // 2) + 2 * two + slot).wait()
            for slot in range(2):
                pair = 2 * two + slot
                g = 2 * pair + odd
                tile_scr[slot] = dot(place_scr[...], quarter_rows(wide_scr, pair, GW // LANES))
                weight_scr[slot] = dot(tail_scr[...], expander(g))
                we_ref[:, group_cols(g)] = weight_scr[slot, :EDGE, :]
                for k in range(GW // LANES):
                    cols = pl.ds(pl.multiple_of(g * GW + k * LANES, LANES), LANES)
                    part = slice(k * LANES, (k + 1) * LANES)

                    def use(rows, x, y, cols=cols, part=part, slot=slot):
                        if rows.start == 0:
                            hv_ref[:, cols] = x[:EDGE].astype(bf16)
                        conv_ref[rows, cols] = y
                        weight = weight_scr[slot, rows, part]
                        part_scr[slot, rows, part] = (y.astype(f32) * weight).astype(bf16)

                    conv_columns(
                        tile_scr.at[slot, :, part], val_ref.at[:, cols], taken_scr, slice(None),
                        w_ref[:, cols], b_ref[:, cols], use,
                    )
            for slot in range(2):
                pair = 2 * two + slot
                rows = pl.ds(pl.multiple_of((2 * pair + odd) * N, N), N)
                b_g = in_ref[pair, EDGE:, odd * N : (odd + 1) * N]
                state_ref[rows, :] = dot_rows(b_g, part_scr[slot, EDGE:, :])
            for slot in range(2):
                store(odd * (G // 2) + 2 * two + slot).start()

    for copy in store_bc:
        copy.wait()
    for i in range(G):
        store(i).wait()


def power8(s):
    s2 = s * s
    s4 = s2 * s2
    s8 = s4 * s4
    return jnp.where(s < 0, -s8, s8).astype(bf16)


def root8(code):
    code = code.astype(f32)
    size = jnp.exp(0.125 * jnp.log(jnp.abs(code)))
    return jnp.where(code < 0, -size, size)


FLOOR = 1e-30


def edge_kernel(
    rim_ref, hv_ref, hp_ref, w_ref, b_ref, we_ref, total_ref, state_ref,
    send_ref, conv_ref, proj_ref,
    full_scr,
):
    rim = rim_ref[...].astype(f32)
    befores = [rim_rows(rim, i) for i in range((E + PW) // RIM_W)]

    def conv(x_ref, at, columns):
        i, low = columns.start // RIM_W, columns.start % RIM_W
        before = befores[i][:, low : low + columns.stop - columns.start]
        return conv_chunk(x_ref[:, at].astype(f32), before, w_ref[:, columns], b_ref[:, columns])

    p = [conv(hp_ref, slice(k * LANES, (k + 1) * LANES), slice(E + k * LANES, E + (k + 1) * LANES)) for k in range(PW // LANES)]
    p = jnp.concatenate(p, axis=1)
    proj_ref[...] = p
    top = jnp.zeros((8, LANES), f32)
    for g in range(G):
        b_g = p[:, g * N : (g + 1) * N]
        cols = slice(g * GW, (g + 1) * GW)
        y = conv(hv_ref, cols, cols)
        conv_ref[:, cols] = y
        rows = slice(g * N, (g + 1) * N)
        state = state_ref[rows, :] + dot_rows(b_g, (y.astype(f32) * we_ref[:, cols]).astype(bf16))
        full_scr[rows, :] = state
        sums = jnp.abs(state[:8])
        for k in range(8, N, 8):
            sums = sums + jnp.abs(state[k : k + 8])
        top = top + dot_cols(sums.astype(bf16), expander(g))
    top = jnp.maximum(jnp.sum(top, axis=0, keepdims=True) * 2.0**-14, FLOOR).astype(bf16).astype(f32)
    top = jnp.where(iota((8, LANES), 1) < H, top, 0.0)
    for g in range(G):
        back = 1.0 / dot(top.astype(bf16), expander(g))[:1]
        for low in range(g * N, (g + 1) * N, 32):
            send_ref[low : low + 32, :GW] = power8(full_scr[low : low + 32, :] * back)
    decay = split2(total_ref[...]).astype(f32)
    odd = (iota((8, LANES), 0) & 1) == 1
    side = jnp.where(odd, top, decay).astype(bf16)
    side = jnp.concatenate([side, side], axis=0)
    for low in range(0, G * N, 16):
        send_ref[low : low + 16, GW:] = side


def scan_kernel(recv_ref, after_ref, out_hbm, bound_ref, side_scr, out_ref, out_sem):
    dev = lax.axis_index("ctx")
    side_scr[...] = dot(recv_ref[:, GW:], expander(dev // 8))

    def code(state, bound):
        return state * (1.0 / jnp.maximum(bound, FLOOR))

    def two(i, carry):
        rows = pl.ds(pl.multiple_of(i * 16, 16), 16)
        first, bound, own = carry
        state = root8(recv_ref[rows, :GW])
        side = side_scr[rows, :]
        second = side[:1] * first + state[:8] * side[1:2]
        second_bound = side[:1] * bound + side[1:2]
        out_ref[rows, :] = power8(jnp.concatenate([code(first, bound), code(second, second_bound)], axis=0))
        part = recv_ref[rows, GW:].astype(f32)
        part = part + pltpu.roll(part, H, 1)
        own = jnp.where(2 * i < dev, part[:1] * own + part[1:2], own)
        own = jnp.where(2 * i + 1 < dev, part[8:9] * own + part[9:10], own)
        return (
            side[8:9] * second + state[8:] * side[9:10],
            side[8:9] * second_bound + side[9:10],
            own,
        )

    zeros = (jnp.zeros((8, GW), f32), jnp.zeros((1, GW), f32), jnp.zeros((1, LANES), f32))
    carry, stores = zeros, []
    for part in range(4):
        carry = lax.fori_loop(part * DEVS // 8, (part + 1) * DEVS // 8, two, carry, unroll=8)
        rows = slice(part * DEVS * 2, (part + 1) * DEVS * 2)
        store = pltpu.make_async_copy(out_ref.at[rows, :], out_hbm.at[rows, :], out_sem.at[part])
        store.start()
        stores.append(store)
    bound_ref[...] = jnp.broadcast_to(carry[2], bound_ref.shape)
    for store in stores:
        store.wait()


def local_kernel(
    odd, recv_ref, at_ref, gate_ref, conv_ref, edge_ref, in_ref, out_ref, ein_ref, eout_ref,
    cum_ref, cumt_ref, size_ref, skip_ref, *rest,
):
    mix_out, scale_out, query_ref, token_ref, place_scr, taken_scr, wide_scr, gate_scr, weighted_scr, first_scr, mix_ref, scale_ref = rest[-12:]
    token_ref[...] = jnp.zeros_like(token_ref)
    i = pl.program_id(0)
    g = 2 * i + odd

    @pl.when(i == 0)
    def _():
        place_scr[...] = placement(at_ref)
        taken_scr[...] = dot(place_scr[...], jnp.ones((LANES, LANES), bf16))
        spread_out(recv_ref[...], wide_scr)

    def patched(edge, rest):
        return jnp.concatenate([edge, rest[EDGE:]], axis=0)

    half = slice(odd * N, (odd + 1) * N)
    b_g = patched(ein_ref[:, half], in_ref[0, :, half])
    c_g = patched(eout_ref[:, half], out_ref[0, :, half])
    query_ref[0] = c_g
    cum = cum_ref[...]
    spread = expander(g)
    skip = skip_ref[...]
    skip = jnp.broadcast_to(jnp.concatenate([skip, skip], axis=1), (8, LANES))
    skip = dot(split2(skip), spread)[:1]
    last = cum[SPAN - 1 : SPAN, :]
    upto = jnp.concatenate([cum[:SPAN], cum[SPAN:] + last], axis=0)
    scale_ref[...] = dot(split2(jnp.exp(upto)), spread)
    weighted_scr[...] = dot(split2(size_ref[...]), spread)
    gate_scr[...] = dot(place_scr[...], quarter_rows(wide_scr, i, GW // LANES))
    own = pltpu.roll(cum, lax.rem(LANES - g * (H // G), LANES), 1)
    for low in range(0, TOK, 32):
        rows = slice(low, low + 32)
        taken = taken_scr[rows, :] > 0
        for k in range(GW // LANES):
            cols = slice(k * LANES, (k + 1) * LANES)
            gate = silu(jnp.where(taken, gate_scr[rows, cols], gate_ref[rows, cols].astype(f32)))
            gate_scr[rows, cols] = gate
            scale_out[rows, cols] = (scale_ref[rows, cols] * gate).astype(bf16)
            x = conv_ref[rows, cols]
            if low == 0:
                x = patched(edge_ref[:, cols], x)
            x = x.astype(f32)
            weighted_scr[rows, cols] = weighted_scr[rows, cols] * x
            mix_ref[rows, cols] = skip[:, cols] * x
    tail = dot(split2(jnp.exp(last - cum[:SPAN])), spread)
    inner = dot(split2(jnp.exp(cum[SPAN:])), spread)
    state = dot_rows(b_g[:SPAN], (weighted_scr[:SPAN] * tail).astype(bf16))
    first_scr[...] = dot_whole(c_g[SPAN:], state) * inner
    causal = iota((SPAN, SPAN), 0) >= iota((SPAN, SPAN), 1)
    lane = iota((SPAN, LANES), 1)
    for k in range(TOK // SPAN):
        rows = slice(k * SPAN, (k + 1) * SPAN)
        scores = jnp.where(causal, dot_cols(c_g[rows], b_g[rows]), 0.0)
        for pair in range(H // G // 2):
            kernels = []
            for head in (2 * pair, 2 * pair + 1):
                apart = own[rows, head : head + 1] - cumt_ref[0, head : head + 1, rows]
                kernels.append((jnp.exp(jnp.minimum(apart, 0.0)) * scores).astype(bf16))
            cols = slice(pair * LANES, (pair + 1) * LANES)
            w = weighted_scr[rows, cols]
            low = jnp.where(lane < P_SIZE, w, 0.0).astype(bf16)
            high = jnp.where(lane < P_SIZE, 0.0, w).astype(bf16)
            mixed = dot(jnp.concatenate(kernels, axis=1), jnp.concatenate([low, high], axis=0))
            mixed = mixed + mix_ref[rows, cols]
            if k == 1:
                mixed = mixed + first_scr[:, cols]
            mix_out[rows, cols] = (mixed * gate_scr[rows, cols]).astype(bf16)


def final_kernel(
    bound_ref, entry_ref, gain_hbm, qe_hbm, qo_hbm, me_hbm, se_hbm, mo_hbm, so_hbm, out_hbm,
    gain_ref, query_ref, mix_ref, scale_ref, out_ref, entry_scr, part_scr, gain_sem, query_sem, mix_sem, scale_sem, out_sem,
):
    gain = pltpu.make_async_copy(gain_hbm, gain_ref, gain_sem)
    queries = [
        pltpu.make_async_copy(src, query_ref.at[i * G // 2 : (i + 1) * G // 2], query_sem.at[i])
        for i, src in enumerate((qe_hbm, qo_hbm))
    ]
    mixes, scales, stores = [], [], []
    for i in range(G):
        cols = slice(i % (G // 2) * GW, (i % (G // 2) + 1) * GW)
        mix, scale = (me_hbm, se_hbm) if i < G // 2 else (mo_hbm, so_hbm)
        mixes.append(pltpu.make_async_copy(mix.at[:, cols], mix_ref.at[i], mix_sem.at[i]))
        scales.append(pltpu.make_async_copy(scale.at[:, cols], scale_ref.at[i], scale_sem.at[i]))
        g = i % (G // 2) * 2 + i // (G // 2)
        cols = slice(g * GW, (g + 1) * GW)
        stores.append(pltpu.make_async_copy(out_ref.at[:, cols], out_hbm.at[:, cols], out_sem.at[i]))
    for load in (*queries, gain, *(c for pair in zip(mixes, scales) for c in pair)):
        load.start()
    bound = split2(jnp.maximum(bound_ref[...], FLOOR))
    for g in range(G):
        rows = slice(g * N, (g + 1) * N)
        entry_scr[rows, :] = root8(entry_ref[rows, :]) * dot(bound, expander(g))[:1]
    for load in (*queries, gain):
        load.wait()
    for i in range(G):
        g = i % (G // 2) * 2 + i // (G // 2)
        if i % 2 == 0:
            for load in (*mixes[i : i + 2], *scales[i : i + 2]):
                load.wait()
        slot = i % 2
        own = dot_whole(query_ref[i], entry_scr[g * N : (g + 1) * N, :])
        squares = jnp.zeros((TOK, LANES), f32)
        for k in range(GW // LANES):
            cols = slice(k * LANES, (k + 1) * LANES)
            part = mix_ref[i, :, cols].astype(f32) + scale_ref[i, :, cols].astype(f32) * own[:, cols]
            part_scr[slot, :, cols] = part
            squares = squares + part * part
        high = squares.astype(bf16)
        low = (squares - high.astype(f32)).astype(bf16)
        mean = dot(jnp.concatenate([high, low], axis=1), jnp.ones((2 * LANES, LANES), bf16)) * (1.0 / GW)
        mean = lax.rsqrt(mean + 1e-05)
        for k in range(GW // LANES):
            cols = slice(k * LANES, (k + 1) * LANES)
            at = slice(g * GW + k * LANES, g * GW + (k + 1) * LANES)
            out_ref[:, at] = (part_scr[slot, :, cols] * mean * gain_ref[:, at]).astype(bf16)
        if i % 2 == 1:
            stores[i - 1].start()
            stores[i].start()
    for store in stores:
        store.wait()


def call(kernel, outs, grid, in_specs, out_specs, scratch=(), est=None, name=None, vmem=VMEM_MIB, alias=None):
    return pl.pallas_call(
        kernel,
        out_shape=outs,
        grid_spec=pltpu.PrefetchScalarGridSpec(
            num_scalar_prefetch=0,
            grid=grid,
            in_specs=in_specs,
            out_specs=out_specs,
            scratch_shapes=scratch,
        ),
        compiler_params=pltpu.CompilerParams(vmem_limit_bytes=vmem * MIB),
        input_output_aliases=alias or {},
        cost_estimate=est,
        name=name,
    )


def struct(*shape, dtype=bf16):
    return pltpu.HBM(shape, dtype)


def near(*shape, dtype=bf16):
    return pltpu.VMEM(shape, dtype)


def far(a):
    return pltpu.with_memory_space_constraint(a, pltpu.HBM)


def kept(a):
    return pltpu.with_memory_space_constraint(a, pltpu.VMEM)


def exchange(rows):
    return lax.all_to_all(rows, "ctx", split_axis=0, concat_axis=0, tiled=True)


def twice(a):
    return jnp.concatenate([a, a], axis=-1)


def shards(
    text_values, text_gate, text_proj, text_step, tile_values, tile_gate, tile_proj, tile_step,
    tile_position, tile_count, conv_weight, conv_bias, step_bias, decay_log, skip_gain, norm_gain,
):
    device = lax.axis_index("ctx")
    scalar = pl.BlockSpec(memory_space=pltpu.SMEM)

    hbm = pl.BlockSpec(memory_space=pl.ANY)
    vmem = pl.BlockSpec(memory_space=pltpu.VMEM)
    sems = pltpu.SemaphoreType.DMA
    positions = tile_position.reshape(32, LANES)
    packed = call(
        pack_kernel,
        struct(DEVS * 8, CHUNK),
        (1,),
        [hbm] * 4,
        hbm,
        scratch=[pltpu.VMEM((32, LANES), jnp.int32), pltpu.VMEM((TILE, H), bf16), pltpu.VMEM((TILE, E), bf16),
                 pltpu.VMEM((TILE, PW), bf16), pltpu.VMEM((DEVS * 8, CHUNK), bf16), sems((4,)), sems((3,))],
        est=cost(2 * 512 * 256 * CHUNK, 3_000_000),
        name="pack",
    )(far(positions), far(tile_step), far(tile_values), far(tile_proj))
    recv = exchange(packed)
    position = tile_position.reshape(DEVS, TILE)
    ids = jnp.arange(TILE, dtype=jnp.int32)
    landing = ((position >> 8) == device) & (ids[None, :] < tile_count[:, None])
    local = jnp.where(landing, position & (TOK - 1), -1)
    at = jnp.max(local.reshape(DEVS, TILE // 2, 2), axis=1).reshape(1, 2 * DEVS)
    ends = jnp.arange(TOK - KCONV + 1, TOK)[:, None]
    rim_slot = jnp.max(jnp.where(at == ends, jnp.arange(2 * DEVS)[None, :], -1), axis=1)
    at = far(at)
    steps = far(text_step)
    gates = call(
        gate_kernel,
        struct(DEVS * 8, G_CHUNK),
        (1,),
        [whole((32, LANES)), whole((TILE, E)), hbm, hbm, hbm],
        whole((DEVS * 8, G_CHUNK)),
        est=cost(2 * 512 * 256 * G_CHUNK, 2_000_000),
        name="gates",
    )(far(positions), far(tile_gate), at, steps, rim_slot)
    gates, recv = lax.optimization_barrier((gates, recv))
    recv = kept(recv)
    recv_gate = exchange(gates)

    bias = conv_bias[None, :]

    recv_spec = whole((DEVS * 8, CHUNK))
    at_spec = whole((1, 2 * DEVS))
    rim = call(
        rim_kernel,
        struct(EDGE, RIM_W),
        (1,),
        [scalar, vmem,
         pl.BlockSpec((EDGE, E), lambda i: (TOK // EDGE - 1, 0)),
         pl.BlockSpec((EDGE, PW), lambda i: (TOK // EDGE - 1, 0))],
        whole((EDGE, RIM_W)),
        est=cost(2 * 16 * 48 * 5120, 3_000_000),
        name="rim",
    )(rim_slot, recv, far(text_values), far(text_proj))
    rim = lax.ppermute(rim, "ctx", [(i, i + 1) for i in range(DEVS - 1)])

    conv, inputs, outputs, state, cum, size, total, head_v, head_p, tail = call(
        place_kernel,
        (
            struct(TOK, E), struct(G // 2, TOK, LANES), struct(G // 2, TOK, LANES), near(G * N, GW, dtype=f32),
            struct(TOK, LANES, dtype=f32), struct(TOK, LANES, dtype=f32),
            near(8, LANES, dtype=f32),
            near(EDGE, E), near(EDGE, PW), near(EDGE, E, dtype=f32),
        ),
        (1,),
        [hbm] * 9,
        [hbm, hbm, hbm, vmem, whole((TOK, LANES)), whole((TOK, LANES)), vmem, vmem, vmem, vmem],
        scratch=[pltpu.VMEM((1, 2 * DEVS), jnp.int32), pltpu.VMEM((TOK, H), bf16), pltpu.VMEM((KCONV, E + PW), f32),
                 pltpu.VMEM((1, E + PW), f32), pltpu.VMEM((1, H), f32), pltpu.VMEM((1, H), f32),
                 pltpu.VMEM((DEVS * 8, CHUNK), bf16), pltpu.VMEM((TOK, E), bf16), pltpu.VMEM((TOK, PW), bf16),
                 pltpu.VMEM((TOK, E), bf16), pltpu.VMEM((G // 2, TOK, LANES), bf16), pltpu.VMEM((G // 2, TOK, LANES), bf16),
                 pltpu.VMEM((TOK, LANES), bf16), pltpu.VMEM((TOK, LANES), f32),
                 pltpu.VMEM((GW // LANES, DEVS * 8, LANES), f32), pltpu.VMEM((TOK, LANES), bf16),
                 pltpu.VMEM((2, TOK, GW), f32), pltpu.VMEM((2, TOK, GW), f32), pltpu.VMEM((2, TOK, GW), bf16),
                 sems((6,)), sems((3,)), sems((G,)), sems(()), sems((G,)), sems((2,))],
        est=cost(2 * 256 * 512 * 5120, 10_000_000, 1_300_000),
        name="place",
    )(recv, far(text_values), far(text_proj), at, steps, far(conv_weight), far(bias),
      far(step_bias[None, :]), far(decay_log[None, :]))

    send, edge, edge_p = call(
        edge_kernel,
        (struct(G * N, STATE_W), struct(EDGE, E), struct(EDGE, PW)),
        (1,),
        [vmem, vmem, vmem, whole((KCONV, E + PW)), whole((1, E + PW)), vmem, vmem, vmem],
        [whole((G * N, STATE_W)), whole((EDGE, E)), whole((EDGE, PW))],
        scratch=[pltpu.VMEM((G * N, GW), f32)],
        est=cost(2 * 64 * 16 * 4096, 2_000_000, 100_000),
        name="edge",
    )(kept(rim), kept(head_v), kept(head_p), far(conv_weight), far(bias), kept(tail), kept(total), kept(state))
    send, recv_gate = lax.optimization_barrier((send, recv_gate))
    states = kept(exchange(send))

    by_head = cum[:, :H].T.reshape(G, H // G, TOK)

    def rows_own(odd, more):
        per_pair = pl.BlockSpec((1, TOK, LANES), lambda i: (i, 0, 0))
        cols = pl.BlockSpec((TOK, GW), lambda i: (0, 2 * i + odd))
        own_cols = pl.BlockSpec((TOK, GW), lambda i: (0, i))
        anywhere = pl.BlockSpec(memory_space=pl.ANY)
        return call(
            functools.partial(local_kernel, odd),
            (struct(TOK, E // 2), struct(TOK, E // 2), struct(G // 2, TOK, N), near(8, LANES, dtype=f32)),
            (G // 2,),
            [pl.BlockSpec((DEVS * 8, GW), lambda i: (0, odd)), at_spec, cols, cols,
             pl.BlockSpec((EDGE, GW), lambda i: (0, 2 * i + odd)), per_pair, per_pair,
             pl.BlockSpec((EDGE, LANES), lambda i: (0, i)), pl.BlockSpec((EDGE, LANES), lambda i: (0, G // 2 + i)),
             whole((TOK, LANES)), pl.BlockSpec((1, H // G, TOK), lambda i: (2 * i + odd, 0, 0)),
             whole((TOK, LANES)), whole((1, H))] + [anywhere] * len(more),
            [own_cols, own_cols, pl.BlockSpec((1, TOK, N), lambda i: (i, 0, 0)), whole((8, LANES))],
            scratch=[pltpu.VMEM((TOK, LANES), bf16), pltpu.VMEM((TOK, LANES), f32),
                     pltpu.VMEM((GW // LANES, DEVS * 8, LANES), f32), pltpu.VMEM((TOK, GW), f32), pltpu.VMEM((TOK, GW), f32), pltpu.VMEM((SPAN, GW), f32),
                     pltpu.VMEM((TOK, GW), f32), pltpu.VMEM((TOK, GW), f32)],
            est=cost(6_000_000_000, 8_000_000, 2_000_000),
            name=f"local{odd}",
        )(recv_gate, at, far(text_gate), *map(far, (conv, edge, inputs, outputs, edge_p, edge_p, cum, by_head, size, skip_gain[None, :])), *more)

    even = rows_own(0, ())
    entries, bound = call(
        scan_kernel,
        (struct(G * N, GW), near(8, LANES, dtype=f32)),
        (1,),
        [vmem, vmem],
        [hbm, vmem],
        scratch=[pltpu.VMEM((G * N, GW), f32), pltpu.VMEM((G * N, GW), bf16), sems((4,))],
        est=cost(2 * 512 * 512 * 128, 1_200_000),
        name="scan",
    )(states, kept(even[3]))
    entry = kept(exchange(entries))
    odds = rows_own(1, (bound,))

    return call(
        final_kernel,
        struct(TOK, E),
        (1,),
        [vmem, vmem] + [hbm] * 7,
        hbm,
        scratch=[pltpu.VMEM((1, E), f32), pltpu.VMEM((G, TOK, N), bf16), pltpu.VMEM((G, TOK, GW), bf16), pltpu.VMEM((G, TOK, GW), bf16),
                 pltpu.VMEM((TOK, E), bf16), pltpu.VMEM((G * N, GW), f32), pltpu.VMEM((2, TOK, GW), f32),
                 sems(()), sems((2,)), sems((G,)), sems((G,)), sems((G,))],
        est=cost(2 * 256 * 64 * 4096, 11_000_000),
        name="final",
    )(kept(bound), entry, far(norm_gain[None, :]), *map(far, (even[2], odds[2], even[0], even[1], odds[0], odds[1])))


def solution(mesh):
    rows = P(("dp", "ctx"), None)
    specs = (rows,) * 8 + (P("dp"),) * 2 + (P(),) * 6
    return jax.shard_map(shards, mesh=mesh, in_specs=specs, out_specs=rows, check_vma=False)
```

```python
import functools

import jax
import jax.numpy as jnp
from jax import lax
from jax.experimental import pallas as pl
from jax.experimental.pallas import tpu as pltpu
from jax.sharding import PartitionSpec as P

H = 64
P_SIZE = 64
N = 64
G = 8
SPAN = 128
KCONV = 4
E = 4096
TOK = 256
TILE = 64
DEVS = 64
GW = E // G
PW = 2 * G * N
EDGE = 16
LANES = 128
QUART = 4
V_AT, P_AT, S_AT = 0, 1024, 1280
CHUNK = 1408
G_CHUNK = 1024
RIM_W = 1024
STATE_W = GW + LANES

f32 = jnp.float32
bf16 = jnp.bfloat16
MIB = 1024 * 1024
VMEM_MIB = 32


def cost(flops, size, trans=0):
    return pl.CostEstimate(flops=flops, bytes_accessed=size, transcendentals=trans)


def whole(shape):
    return pl.BlockSpec(shape, lambda *_: (0,) * len(shape))


def group_cols(g):
    return pl.ds(pl.multiple_of(g * GW, GW), GW)


def iota(shape, dim):
    return lax.broadcasted_iota(jnp.int32, shape, dim)


def dot(a, b):
    return jnp.dot(a, b, preferred_element_type=f32)


def dot_rows(a, b):
    return lax.dot_general(a, b, (((0,), (0,)), ((), ())), preferred_element_type=f32)


def dot_cols(a, b):
    return lax.dot_general(a, b, (((1,), (1,)), ((), ())), preferred_element_type=f32)


def dot_whole(a, b):
    high = b.astype(bf16)
    low = (b - high.astype(f32)).astype(bf16)
    return dot(jnp.concatenate([a, a], axis=1), jnp.concatenate([high, low], axis=0))


def silu(x):
    half = 0.5 * x
    return half + half * jnp.tanh(half)


def split2(x):
    high = x.astype(bf16)
    low = (x - high.astype(f32)).astype(bf16)
    return jnp.where(iota(x.shape, 1) < H, high.astype(f32), low.astype(f32)).astype(bf16)


def expander(group):
    head = iota((LANES, GW), 0) & (H - 1)
    col = group * (H // G) + (iota((LANES, GW), 1) >> 6)
    return jnp.where(head == col, 1.0, 0.0).astype(bf16)


def slot_keys(pos_ref):
    dev = lax.axis_index("ctx")
    row = pos_ref[pl.ds(dev // 2, 1), :]
    other = pltpu.roll(row, 64, 1)
    lane = iota((1, LANES), 1)
    own = jnp.where((lane >> 6) == lax.rem(dev, 2), row, other)
    key = (own >> 8) * 8 + (lane & 1) * QUART + (lane >> 6)
    keys = jnp.concatenate([key, key + 2], axis=1)
    return jnp.where(iota((DEVS * 8, 2 * LANES), 0) == keys, 1.0, 0.0).astype(bf16)


def quarters(ref, width, low, count):
    return jnp.concatenate([ref[:, b * width + low : b * width + low + count] for b in range(QUART)], axis=0)


def pack_kernel(
    pos_hbm, step_hbm, val_hbm, proj_hbm, out_hbm,
    pos_ref, step_ref, val_ref, proj_ref, out_ref, in_sem, out_sem,
):
    pairs = ((pos_hbm, pos_ref), (step_hbm, step_ref), (proj_hbm, proj_ref), (val_hbm, val_ref))
    loads = [pltpu.make_async_copy(src, dst, in_sem.at[i]) for i, (src, dst) in enumerate(pairs)]
    for load in loads:
        load.start()
    loads[0].wait()
    pick = slot_keys(pos_ref)
    loads[1].wait()
    step = step_ref[...]
    out_ref[:, S_AT:] = dot(pick[:, :TILE], jnp.concatenate([step, step], axis=1)).astype(bf16)
    loads[2].wait()
    out_ref[:, P_AT:S_AT] = dot(pick, quarters(proj_ref, 256, 0, 256)).astype(bf16)
    loads[3].wait()
    stores = []
    for i, (low, high) in enumerate(((P_AT, CHUNK), (0, GW), (GW, 2 * GW))):
        if i:
            out_ref[:, low:high] = dot(pick, quarters(val_ref, 1024, low, GW)).astype(bf16)
        store = pltpu.make_async_copy(out_ref.at[:, low:high], out_hbm.at[:, low:high], out_sem.at[i])
        store.start()
        stores.append(store)
    for store in stores:
        store.wait()


def gate_kernel(pos_ref, gate_ref, at_ref, step_ref, slot_ref, out_ref):
    pick = slot_keys(pos_ref)
    for low in (0, GW):
        out_ref[:, low : low + GW] = dot(pick, quarters(gate_ref, 1024, low, GW)).astype(bf16)


def rim_kernel(slot_ref, recv_ref, val_ref, proj_ref, out_ref):
    count = KCONV - 1
    slots = [slot_ref[i] for i in range(count)]
    starts = [jnp.maximum(k, 0) * QUART for k in slots]
    rows = [recv_ref[pl.ds(pl.multiple_of((k >> 4) * 16, 16), 16), :] for k in starts]
    rows = jnp.concatenate(rows, axis=0)
    row, col = iota((EDGE, 16 * count), 0), iota((EDGE, 16 * count), 1)
    at = jnp.full((EDGE, 16 * count), -16, jnp.int32)
    taken = jnp.full((EDGE, 1), -1, jnp.int32)
    for i, k in enumerate(starts):
        at = jnp.where(row == EDGE - count + i, 16 * i + (k & 15), at)
        taken = jnp.where(iota((EDGE, 1), 0) == EDGE - count + i, slots[i], taken)
    blocks, proj = [], []
    for b in range(QUART):
        place = jnp.where(col == at + b, 1.0, 0.0).astype(bf16)
        tile = dot(place, rows[:, V_AT:P_AT])
        text = val_ref[:, b * RIM_W : (b + 1) * RIM_W].astype(f32)
        blocks.append(jnp.where(taken >= 0, tile, text))
        tile = dot(place, rows[:, P_AT:S_AT])
        text = proj_ref[:, b * 256 : (b + 1) * 256].astype(f32)
        proj.append(jnp.where(taken >= 0, tile, text))
    blocks.append(jnp.concatenate(proj, axis=1))
    out = blocks[0]
    row = iota((EDGE, RIM_W), 0)
    for i, block in enumerate(blocks):
        out = jnp.where((row >= i * count) & (row < (i + 1) * count), pltpu.roll(block, (i + 1) * count, 0), out)
    out_ref[...] = out.astype(bf16)


def rim_rows(rim, block):
    return pltpu.roll(rim, EDGE - (block + 1) * (KCONV - 1), 0)[EDGE - 8 :]


def placement(at_ref):
    return jnp.where(iota((TOK, LANES), 0) == at_ref[...], 1.0, 0.0).astype(bf16)


def spread_out(recv, wide_ref):
    for k in range(recv.shape[1] // LANES):
        wide_ref[k] = recv[:, k * LANES : (k + 1) * LANES].astype(f32)


def quarter_rows(wide_ref, b, count):
    rows = [wide_ref[k, pl.ds(b, 2 * DEVS, stride=QUART), :] for k in range(count)]
    return jnp.concatenate(rows, axis=1).astype(bf16)


def conv_chunk(x, before, weights, bias):
    ext = jnp.concatenate([before, x], axis=0)
    total = bias + weights[KCONV - 1 : KCONV, :] * x
    for back in range(1, KCONV):
        total = total + weights[KCONV - 1 - back : KCONV - back, :] * pltpu.roll(ext, back, 0)[8:]
    return silu(total).astype(bf16)


CHUNK_ROWS = 64


def conv_columns(tile_ref, text_ref, taken_ref, cols, weights, bias, use):
    before = jnp.zeros((8, LANES), f32)
    for low in range(0, TOK, CHUNK_ROWS):
        rows = slice(low, low + CHUNK_ROWS)
        x = jnp.where(taken_ref[rows, :] > 0, tile_ref[rows, cols], text_ref[rows, cols].astype(f32))
        use(rows, x, conv_chunk(x, before, weights, bias))
        before = x[CHUNK_ROWS - 8 :]


def softplus(v):
    return jnp.maximum(v, 0.0) + jnp.log1p(jnp.exp(-jnp.abs(v)))


def three(x):
    a = x.astype(bf16)
    left = x - a.astype(f32)
    b = left.astype(bf16)
    return a, b, (left - b.astype(f32)).astype(bf16)


def order(i):
    return lax.rem(i, G // 2) * 2 + i // (G // 2)


def place_kernel(
    recv_hbm, val_hbm, proj_hbm, at_hbm, step_hbm, w_hbm, b_hbm, sbias_hbm, dlog_hbm,
    conv_hbm, in_hbm, out_hbm, state_ref, cum_ref, size_ref, total_ref, hv_ref, hp_ref, we_ref, wk_ref, bk_ref,
    at_ref, step_ref, w_ref, b_ref, sbias_ref, dlog_ref,
    recv_ref, val_ref, proj_ref, conv_ref, in_ref, out_ref, place_scr, taken_scr, wide_scr, tail_scr,
    tile_scr, weight_scr, part_scr, small_sem, recv_sem, val_sem, proj_sem, conv_sem, bc_sem,
):
    def load(i):
        cols = group_cols(order(i))
        return pltpu.make_async_copy(val_hbm.at[:, cols], val_ref.at[:, cols], val_sem.at[i])

    def store(i):
        cols = group_cols(order(i))
        return pltpu.make_async_copy(conv_ref.at[:, cols], conv_hbm.at[:, cols], conv_sem.at[i])

    def arrived(i, low, high):
        return pltpu.make_async_copy(recv_hbm.at[:, low:high], recv_ref.at[:, low:high], recv_sem.at[i])

    load_proj = pltpu.make_async_copy(proj_hbm, proj_ref, proj_sem)
    pieces = [arrived(0, P_AT, CHUNK), arrived(1, 0, GW), arrived(2, GW, 2 * GW)]
    store_bc = [
        pltpu.make_async_copy(src, dst, bc_sem.at[i])
        for i, (src, dst) in enumerate(((in_ref, in_hbm), (out_ref, out_hbm)))
    ]
    pairs = (
        (at_hbm, at_ref), (w_hbm, w_ref), (b_hbm, b_ref), (step_hbm, step_ref), (sbias_hbm, sbias_ref), (dlog_hbm, dlog_ref),
    )
    small = [pltpu.make_async_copy(src, dst, small_sem.at[i]) for i, (src, dst) in enumerate(pairs)]
    small[0].start()
    pieces[0].start()
    load_proj.start()
    for load_small in small[1:]:
        load_small.start()
    pieces[1].start()
    for i in range(G // 2):
        load(i).start()
    pieces[2].start()
    for i in range(G // 2, G):
        load(i).start()

    def first():
        small[0].wait()
        place_scr[...] = placement(at_ref)
        taken_scr[...] = dot(place_scr[...], jnp.ones((LANES, LANES), bf16))
        for load_small in small[1:]:
            load_small.wait()
        wk_ref[...] = w_ref[...]
        bk_ref[...] = b_ref[...]
        pieces[0].wait()
        spread_out(recv_ref[:, P_AT:], wide_scr)
        load_proj.wait()
        for b in range(QUART):
            tile_scr[0, :, :256] = dot(place_scr[...], quarter_rows(wide_scr, b, 2))
            for half in range(2):
                pair = b * 2 + half
                cols = slice(pair * LANES, (pair + 1) * LANES)

                def use(rows, x, y, pair=pair, cols=cols):
                    if rows.start == 0:
                        hp_ref[:, cols] = x[:EDGE].astype(bf16)
                    if pair < G // 2:
                        in_ref[pair, rows, :] = y
                    else:
                        out_ref[pair - G // 2, rows, :] = y

                at = slice(E + pair * LANES, E + (pair + 1) * LANES)
                conv_columns(
                    tile_scr.at[0, :, half * LANES : (half + 1) * LANES], proj_ref.at[:, cols], taken_scr,
                    slice(None), w_ref[:, at], b_ref[:, at], use,
                )
        for copy in store_bc:
            copy.start()
        steps = wide_scr[2, pl.ds(0, 2 * DEVS, stride=QUART), :].astype(bf16)
        tile = dot(place_scr[...], steps)
        step = step_ref[...].astype(f32)
        step = jnp.where(taken_scr[...] > 0, tile, jnp.concatenate([step, step], axis=1))
        sbias, dlog = sbias_ref[...], dlog_ref[...]
        size = softplus(step + jnp.concatenate([sbias, sbias], axis=1))
        logs = -jnp.exp(jnp.concatenate([dlog, dlog], axis=1)) * size
        size_ref[...] = size
        lower = jnp.where(iota((SPAN, SPAN), 0) >= iota((SPAN, SPAN), 1), 1.0, 0.0).astype(bf16)
        cums = []
        for k in range(TOK // SPAN):
            parts = three(logs[k * SPAN : (k + 1) * SPAN])
            cums.append(dot(lower, parts[0]) + (dot(lower, parts[1]) + dot(lower, parts[2])))
        last = [c[SPAN - 1 : SPAN, :] for c in cums]
        for k, c in enumerate(cums):
            rows = slice(k * SPAN, (k + 1) * SPAN)
            cum_ref[rows, :] = c
            left = last[k] - c
            if k == 0:
                left = left + last[1]
            tail_scr[rows, :] = split2(jnp.exp(left) * size[rows])
        total_ref[...] = jnp.broadcast_to(jnp.exp(last[0] + last[1]), total_ref.shape)

    first()
    for odd in range(2):
        pieces[1 + odd].wait()
        spread_out(recv_ref[:, odd * GW : (odd + 1) * GW], wide_scr)

        @pl.loop(0, G // 4)
        def _(two, odd=odd):
            for slot in range(2):
                load(odd * (G // 2) + 2 * two + slot).wait()
            for slot in range(2):
                pair = 2 * two + slot
                g = 2 * pair + odd
                tile_scr[slot] = dot(place_scr[...], quarter_rows(wide_scr, pair, GW // LANES))
                weight_scr[slot] = dot(tail_scr[...], expander(g))
                we_ref[:, group_cols(g)] = weight_scr[slot, :EDGE, :]
                for k in range(GW // LANES):
                    cols = pl.ds(pl.multiple_of(g * GW + k * LANES, LANES), LANES)
                    part = slice(k * LANES, (k + 1) * LANES)

                    def use(rows, x, y, cols=cols, part=part, slot=slot):
                        if rows.start == 0:
                            hv_ref[:, cols] = x[:EDGE].astype(bf16)
                        conv_ref[rows, cols] = y
                        weight = weight_scr[slot, rows, part]
                        part_scr[slot, rows, part] = (y.astype(f32) * weight).astype(bf16)

                    conv_columns(
                        tile_scr.at[slot, :, part], val_ref.at[:, cols], taken_scr, slice(None),
                        w_ref[:, cols], b_ref[:, cols], use,
                    )
            for slot in range(2):
                pair = 2 * two + slot
                rows = pl.ds(pl.multiple_of((2 * pair + odd) * N, N), N)
                b_g = in_ref[pair, EDGE:, odd * N : (odd + 1) * N]
                state_ref[rows, :] = dot_rows(b_g, part_scr[slot, EDGE:, :])
            for slot in range(2):
                store(odd * (G // 2) + 2 * two + slot).start()

    for copy in store_bc:
        copy.wait()
    for i in range(G):
        store(i).wait()


def power8(s):
    s2 = s * s
    s4 = s2 * s2
    s8 = s4 * s4
    return jnp.where(s < 0, -s8, s8).astype(bf16)


def root8(code):
    code = code.astype(f32)
    size = jnp.exp(0.125 * jnp.log(jnp.abs(code)))
    return jnp.where(code < 0, -size, size)


FLOOR = 1e-30


def edge_kernel(
    rim_ref, hv_ref, hp_ref, w_ref, b_ref, we_ref, total_ref, state_ref,
    send_ref, conv_ref, proj_ref,
    full_scr,
):
    rim = rim_ref[...].astype(f32)
    befores = [rim_rows(rim, i) for i in range((E + PW) // RIM_W)]

    def conv(x_ref, at, columns):
        i, low = columns.start // RIM_W, columns.start % RIM_W
        before = befores[i][:, low : low + columns.stop - columns.start]
        return conv_chunk(x_ref[:, at].astype(f32), before, w_ref[:, columns], b_ref[:, columns])

    p = [conv(hp_ref, slice(k * LANES, (k + 1) * LANES), slice(E + k * LANES, E + (k + 1) * LANES)) for k in range(PW // LANES)]
    p = jnp.concatenate(p, axis=1)
    proj_ref[...] = p
    top = jnp.zeros((8, LANES), f32)
    for g in range(G):
        b_g = p[:, g * N : (g + 1) * N]
        cols = slice(g * GW, (g + 1) * GW)
        y = conv(hv_ref, cols, cols)
        conv_ref[:, cols] = y
        rows = slice(g * N, (g + 1) * N)
        state = state_ref[rows, :] + dot_rows(b_g, (y.astype(f32) * we_ref[:, cols]).astype(bf16))
        full_scr[rows, :] = state
        sums = jnp.abs(state[:8])
        for k in range(8, N, 8):
            sums = sums + jnp.abs(state[k : k + 8])
        top = top + dot_cols(sums.astype(bf16), expander(g))
    top = jnp.maximum(jnp.sum(top, axis=0, keepdims=True) * 2.0**-14, FLOOR).astype(bf16).astype(f32)
    top = jnp.where(iota((8, LANES), 1) < H, top, 0.0)
    for g in range(G):
        back = 1.0 / dot(top.astype(bf16), expander(g))[:1]
        for low in range(g * N, (g + 1) * N, 32):
            send_ref[low : low + 32, :GW] = power8(full_scr[low : low + 32, :] * back)
    decay = split2(total_ref[...]).astype(f32)
    odd = (iota((8, LANES), 0) & 1) == 1
    side = jnp.where(odd, top, decay).astype(bf16)
    side = jnp.concatenate([side, side], axis=0)
    for low in range(0, G * N, 16):
        send_ref[low : low + 16, GW:] = side


def scan_kernel(recv_ref, after_ref, out_hbm, bound_ref, side_scr, out_ref, out_sem):
    dev = lax.axis_index("ctx")
    side_scr[...] = dot(recv_ref[:, GW:], expander(dev // 8))

    def code(state, bound):
        return state * (1.0 / jnp.maximum(bound, FLOOR))

    def two(i, carry):
        rows = pl.ds(pl.multiple_of(i * 16, 16), 16)
        first, bound, own = carry
        state = root8(recv_ref[rows, :GW])
        side = side_scr[rows, :]
        second = side[:1] * first + state[:8] * side[1:2]
        second_bound = side[:1] * bound + side[1:2]
        out_ref[rows, :] = power8(jnp.concatenate([code(first, bound), code(second, second_bound)], axis=0))
        part = recv_ref[rows, GW:].astype(f32)
        part = part + pltpu.roll(part, H, 1)
        own = jnp.where(2 * i < dev, part[:1] * own + part[1:2], own)
        own = jnp.where(2 * i + 1 < dev, part[8:9] * own + part[9:10], own)
        return (
            side[8:9] * second + state[8:] * side[9:10],
            side[8:9] * second_bound + side[9:10],
            own,
        )

    zeros = (jnp.zeros((8, GW), f32), jnp.zeros((1, GW), f32), jnp.zeros((1, LANES), f32))
    carry, stores = zeros, []
    for part in range(4):
        carry = lax.fori_loop(part * DEVS // 8, (part + 1) * DEVS // 8, two, carry, unroll=8)
        rows = slice(part * DEVS * 2, (part + 1) * DEVS * 2)
        store = pltpu.make_async_copy(out_ref.at[rows, :], out_hbm.at[rows, :], out_sem.at[part])
        store.start()
        stores.append(store)
    bound_ref[...] = jnp.broadcast_to(carry[2], bound_ref.shape)
    for store in stores:
        store.wait()


def local_kernel(
    odd, recv_ref, at_ref, gate_ref, conv_ref, edge_ref, in_ref, out_ref, ein_ref, eout_ref,
    cum_ref, cumt_ref, size_ref, skip_ref, *rest,
):
    mix_out, scale_out, query_ref, token_ref, place_scr, taken_scr, wide_scr, gate_scr, weighted_scr, first_scr, mix_ref, scale_ref = rest[-12:]
    token_ref[...] = jnp.zeros_like(token_ref)
    i = pl.program_id(0)
    g = 2 * i + odd

    @pl.when(i == 0)
    def _():
        place_scr[...] = placement(at_ref)
        taken_scr[...] = dot(place_scr[...], jnp.ones((LANES, LANES), bf16))
        spread_out(recv_ref[...], wide_scr)

    def patched(edge, rest):
        return jnp.concatenate([edge, rest[EDGE:]], axis=0)

    half = slice(odd * N, (odd + 1) * N)
    b_g = patched(ein_ref[:, half], in_ref[0, :, half])
    c_g = patched(eout_ref[:, half], out_ref[0, :, half])
    query_ref[0] = c_g
    cum = cum_ref[...]
    spread = expander(g)
    skip = skip_ref[...]
    skip = jnp.broadcast_to(jnp.concatenate([skip, skip], axis=1), (8, LANES))
    skip = dot(split2(skip), spread)[:1]
    last = cum[SPAN - 1 : SPAN, :]
    upto = jnp.concatenate([cum[:SPAN], cum[SPAN:] + last], axis=0)
    scale_ref[...] = dot(split2(jnp.exp(upto)), spread)
    weighted_scr[...] = dot(split2(size_ref[...]), spread)
    gate_scr[...] = dot(place_scr[...], quarter_rows(wide_scr, i, GW // LANES))
    own = pltpu.roll(cum, lax.rem(LANES - g * (H // G), LANES), 1)
    for low in range(0, TOK, 32):
        rows = slice(low, low + 32)
        taken = taken_scr[rows, :] > 0
        for k in range(GW // LANES):
            cols = slice(k * LANES, (k + 1) * LANES)
            gate = silu(jnp.where(taken, gate_scr[rows, cols], gate_ref[rows, cols].astype(f32)))
            gate_scr[rows, cols] = gate
            scale_out[rows, cols] = (scale_ref[rows, cols] * gate).astype(bf16)
            x = conv_ref[rows, cols]
            if low == 0:
                x = patched(edge_ref[:, cols], x)
            x = x.astype(f32)
            weighted_scr[rows, cols] = weighted_scr[rows, cols] * x
            mix_ref[rows, cols] = skip[:, cols] * x
    tail = dot(split2(jnp.exp(last - cum[:SPAN])), spread)
    inner = dot(split2(jnp.exp(cum[SPAN:])), spread)
    state = dot_rows(b_g[:SPAN], (weighted_scr[:SPAN] * tail).astype(bf16))
    first_scr[...] = dot_whole(c_g[SPAN:], state) * inner
    causal = iota((SPAN, SPAN), 0) >= iota((SPAN, SPAN), 1)
    lane = iota((SPAN, LANES), 1)
    for k in range(TOK // SPAN):
        rows = slice(k * SPAN, (k + 1) * SPAN)
        scores = jnp.where(causal, dot_cols(c_g[rows], b_g[rows]), 0.0)
        for pair in range(H // G // 2):
            kernels = []
            for head in (2 * pair, 2 * pair + 1):
                apart = own[rows, head : head + 1] - cumt_ref[0, head : head + 1, rows]
                kernels.append((jnp.exp(jnp.minimum(apart, 0.0)) * scores).astype(bf16))
            cols = slice(pair * LANES, (pair + 1) * LANES)
            w = weighted_scr[rows, cols]
            low = jnp.where(lane < P_SIZE, w, 0.0).astype(bf16)
            high = jnp.where(lane < P_SIZE, 0.0, w).astype(bf16)
            mixed = dot(jnp.concatenate(kernels, axis=1), jnp.concatenate([low, high], axis=0))
            mixed = mixed + mix_ref[rows, cols]
            if k == 1:
                mixed = mixed + first_scr[:, cols]
            mix_out[rows, cols] = (mixed * gate_scr[rows, cols]).astype(bf16)


def final_kernel(
    bound_ref, entry_ref, gain_hbm, qe_hbm, qo_hbm, me_hbm, se_hbm, mo_hbm, so_hbm, out_hbm,
    gain_ref, query_ref, mix_ref, scale_ref, out_ref, entry_scr, part_scr, gain_sem, query_sem, mix_sem, scale_sem, out_sem,
):
    gain = pltpu.make_async_copy(gain_hbm, gain_ref, gain_sem)
    queries = [
        pltpu.make_async_copy(src, query_ref.at[i * G // 2 : (i + 1) * G // 2], query_sem.at[i])
        for i, src in enumerate((qe_hbm, qo_hbm))
    ]
    mixes, scales, stores = [], [], []
    for i in range(G):
        cols = slice(i % (G // 2) * GW, (i % (G // 2) + 1) * GW)
        mix, scale = (me_hbm, se_hbm) if i < G // 2 else (mo_hbm, so_hbm)
        mixes.append(pltpu.make_async_copy(mix.at[:, cols], mix_ref.at[i], mix_sem.at[i]))
        scales.append(pltpu.make_async_copy(scale.at[:, cols], scale_ref.at[i], scale_sem.at[i]))
        g = i % (G // 2) * 2 + i // (G // 2)
        cols = slice(g * GW, (g + 1) * GW)
        stores.append(pltpu.make_async_copy(out_ref.at[:, cols], out_hbm.at[:, cols], out_sem.at[i]))
    for load in (*queries, gain, *(c for pair in zip(mixes, scales) for c in pair)):
        load.start()
    bound = split2(jnp.maximum(bound_ref[...], FLOOR))
    for g in range(G):
        rows = slice(g * N, (g + 1) * N)
        entry_scr[rows, :] = root8(entry_ref[rows, :]) * dot(bound, expander(g))[:1]
    for load in (*queries, gain):
        load.wait()
    for i in range(G):
        g = i % (G // 2) * 2 + i // (G // 2)
        if i % 2 == 0:
            for load in (*mixes[i : i + 2], *scales[i : i + 2]):
                load.wait()
        slot = i % 2
        own = dot_whole(query_ref[i], entry_scr[g * N : (g + 1) * N, :])
        squares = jnp.zeros((TOK, LANES), f32)
        for k in range(GW // LANES):
            cols = slice(k * LANES, (k + 1) * LANES)
            part = mix_ref[i, :, cols].astype(f32) + scale_ref[i, :, cols].astype(f32) * own[:, cols]
            part_scr[slot, :, cols] = part
            squares = squares + part * part
        high = squares.astype(bf16)
        low = (squares - high.astype(f32)).astype(bf16)
        mean = dot(jnp.concatenate([high, low], axis=1), jnp.ones((2 * LANES, LANES), bf16)) * (1.0 / GW)
        mean = lax.rsqrt(mean + 1e-05)
        for k in range(GW // LANES):
            cols = slice(k * LANES, (k + 1) * LANES)
            at = slice(g * GW + k * LANES, g * GW + (k + 1) * LANES)
            out_ref[:, at] = (part_scr[slot, :, cols] * mean * gain_ref[:, at]).astype(bf16)
        if i % 2 == 1:
            stores[i - 1].start()
            stores[i].start()
    for store in stores:
        store.wait()


def call(kernel, outs, grid, in_specs, out_specs, scratch=(), est=None, name=None, vmem=VMEM_MIB, alias=None):
    return pl.pallas_call(
        kernel,
        out_shape=outs,
        grid_spec=pltpu.PrefetchScalarGridSpec(
            num_scalar_prefetch=0,
            grid=grid,
            in_specs=in_specs,
            out_specs=out_specs,
            scratch_shapes=scratch,
        ),
        compiler_params=pltpu.CompilerParams(vmem_limit_bytes=vmem * MIB),
        input_output_aliases=alias or {},
        cost_estimate=est,
        name=name,
    )


def struct(*shape, dtype=bf16):
    return pltpu.HBM(shape, dtype)


def near(*shape, dtype=bf16):
    return pltpu.VMEM(shape, dtype)


def far(a):
    return pltpu.with_memory_space_constraint(a, pltpu.HBM)


def kept(a):
    return pltpu.with_memory_space_constraint(a, pltpu.VMEM)


def exchange(rows):
    return lax.all_to_all(rows, "ctx", split_axis=0, concat_axis=0, tiled=True)


def twice(a):
    return jnp.concatenate([a, a], axis=-1)


def shards(
    text_values, text_gate, text_proj, text_step, tile_values, tile_gate, tile_proj, tile_step,
    tile_position, tile_count, conv_weight, conv_bias, step_bias, decay_log, skip_gain, norm_gain,
):
    device = lax.axis_index("ctx")
    scalar = pl.BlockSpec(memory_space=pltpu.SMEM)

    hbm = pl.BlockSpec(memory_space=pl.ANY)
    vmem = pl.BlockSpec(memory_space=pltpu.VMEM)
    sems = pltpu.SemaphoreType.DMA
    positions = tile_position.reshape(32, LANES)
    packed = call(
        pack_kernel,
        struct(DEVS * 8, CHUNK),
        (1,),
        [hbm] * 4,
        hbm,
        scratch=[pltpu.VMEM((32, LANES), jnp.int32), pltpu.VMEM((TILE, H), bf16), pltpu.VMEM((TILE, E), bf16),
                 pltpu.VMEM((TILE, PW), bf16), pltpu.VMEM((DEVS * 8, CHUNK), bf16), sems((4,)), sems((3,))],
        est=cost(2 * 512 * 256 * CHUNK, 3_000_000),
        name="pack",
    )(far(positions), far(tile_step), far(tile_values), far(tile_proj))
    recv = exchange(packed)
    position = tile_position.reshape(DEVS, TILE)
    ids = jnp.arange(TILE, dtype=jnp.int32)
    landing = ((position >> 8) == device) & (ids[None, :] < tile_count[:, None])
    local = jnp.where(landing, position & (TOK - 1), -1)
    at = jnp.max(local.reshape(DEVS, TILE // 2, 2), axis=1).reshape(1, 2 * DEVS)
    ends = jnp.arange(TOK - KCONV + 1, TOK)[:, None]
    rim_slot = jnp.max(jnp.where(at == ends, jnp.arange(2 * DEVS)[None, :], -1), axis=1)
    at = far(at)
    steps = far(text_step)
    gates = call(
        gate_kernel,
        struct(DEVS * 8, G_CHUNK),
        (1,),
        [whole((32, LANES)), whole((TILE, E)), hbm, hbm, hbm],
        whole((DEVS * 8, G_CHUNK)),
        est=cost(2 * 512 * 256 * G_CHUNK, 2_000_000),
        name="gates",
    )(far(positions), far(tile_gate), at, steps, rim_slot)
    gates, recv = lax.optimization_barrier((gates, recv))
    recv = kept(recv)
    recv_gate = exchange(gates)

    bias = conv_bias[None, :]

    recv_spec = whole((DEVS * 8, CHUNK))
    at_spec = whole((1, 2 * DEVS))
    rim = call(
        rim_kernel,
        struct(EDGE, RIM_W),
        (1,),
        [scalar, vmem,
         pl.BlockSpec((EDGE, E), lambda i: (TOK // EDGE - 1, 0)),
         pl.BlockSpec((EDGE, PW), lambda i: (TOK // EDGE - 1, 0))],
        whole((EDGE, RIM_W)),
        est=cost(2 * 16 * 48 * 5120, 3_000_000),
        name="rim",
    )(rim_slot, recv, far(text_values), far(text_proj))
    rim = lax.ppermute(rim, "ctx", [(i, i + 1) for i in range(DEVS - 1)])

    conv, inputs, outputs, state, cum, size, total, head_v, head_p, tail, taps, shift = call(
        place_kernel,
        (
            struct(TOK, E), struct(G // 2, TOK, LANES), struct(G // 2, TOK, LANES), near(G * N, GW, dtype=f32),
            struct(TOK, LANES, dtype=f32), struct(TOK, LANES, dtype=f32),
            near(8, LANES, dtype=f32),
            near(EDGE, E), near(EDGE, PW), near(EDGE, E, dtype=f32),
            near(KCONV, E + PW, dtype=f32), near(1, E + PW, dtype=f32),
        ),
        (1,),
        [hbm] * 9,
        [hbm, hbm, hbm, vmem, whole((TOK, LANES)), whole((TOK, LANES)), vmem, vmem, vmem, vmem, vmem, vmem],
        scratch=[pltpu.VMEM((1, 2 * DEVS), jnp.int32), pltpu.VMEM((TOK, H), bf16), pltpu.VMEM((KCONV, E + PW), f32),
                 pltpu.VMEM((1, E + PW), f32), pltpu.VMEM((1, H), f32), pltpu.VMEM((1, H), f32),
                 pltpu.VMEM((DEVS * 8, CHUNK), bf16), pltpu.VMEM((TOK, E), bf16), pltpu.VMEM((TOK, PW), bf16),
                 pltpu.VMEM((TOK, E), bf16), pltpu.VMEM((G // 2, TOK, LANES), bf16), pltpu.VMEM((G // 2, TOK, LANES), bf16),
                 pltpu.VMEM((TOK, LANES), bf16), pltpu.VMEM((TOK, LANES), f32),
                 pltpu.VMEM((GW // LANES, DEVS * 8, LANES), f32), pltpu.VMEM((TOK, LANES), bf16),
                 pltpu.VMEM((2, TOK, GW), f32), pltpu.VMEM((2, TOK, GW), f32), pltpu.VMEM((2, TOK, GW), bf16),
                 sems((6,)), sems((3,)), sems((G,)), sems(()), sems((G,)), sems((2,))],
        est=cost(2 * 256 * 512 * 5120, 10_000_000, 1_300_000),
        name="place",
    )(recv, far(text_values), far(text_proj), at, steps, far(conv_weight), far(bias),
      far(step_bias[None, :]), far(decay_log[None, :]))

    send, edge, edge_p = call(
        edge_kernel,
        (struct(G * N, STATE_W), struct(EDGE, E), struct(EDGE, PW)),
        (1,),
        [vmem] * 8,
        [whole((G * N, STATE_W)), whole((EDGE, E)), whole((EDGE, PW))],
        scratch=[pltpu.VMEM((G * N, GW), f32)],
        est=cost(2 * 64 * 16 * 4096, 2_000_000, 100_000),
        name="edge",
    )(kept(rim), kept(head_v), kept(head_p), kept(taps), kept(shift), kept(tail), kept(total), kept(state))
    send, recv_gate = lax.optimization_barrier((send, recv_gate))
    states = kept(exchange(send))

    by_head = cum[:, :H].T.reshape(G, H // G, TOK)

    def rows_own(odd, more):
        per_pair = pl.BlockSpec((1, TOK, LANES), lambda i: (i, 0, 0))
        cols = pl.BlockSpec((TOK, GW), lambda i: (0, 2 * i + odd))
        own_cols = pl.BlockSpec((TOK, GW), lambda i: (0, i))
        anywhere = pl.BlockSpec(memory_space=pl.ANY)
        return call(
            functools.partial(local_kernel, odd),
            (struct(TOK, E // 2), struct(TOK, E // 2), struct(G // 2, TOK, N), near(8, LANES, dtype=f32)),
            (G // 2,),
            [pl.BlockSpec((DEVS * 8, GW), lambda i: (0, odd)), at_spec, cols, cols,
             pl.BlockSpec((EDGE, GW), lambda i: (0, 2 * i + odd)), per_pair, per_pair,
             pl.BlockSpec((EDGE, LANES), lambda i: (0, i)), pl.BlockSpec((EDGE, LANES), lambda i: (0, G // 2 + i)),
             whole((TOK, LANES)), pl.BlockSpec((1, H // G, TOK), lambda i: (2 * i + odd, 0, 0)),
             whole((TOK, LANES)), whole((1, H))] + [anywhere] * len(more),
            [own_cols, own_cols, pl.BlockSpec((1, TOK, N), lambda i: (i, 0, 0)), whole((8, LANES))],
            scratch=[pltpu.VMEM((TOK, LANES), bf16), pltpu.VMEM((TOK, LANES), f32),
                     pltpu.VMEM((GW // LANES, DEVS * 8, LANES), f32), pltpu.VMEM((TOK, GW), f32), pltpu.VMEM((TOK, GW), f32), pltpu.VMEM((SPAN, GW), f32),
                     pltpu.VMEM((TOK, GW), f32), pltpu.VMEM((TOK, GW), f32)],
            est=cost(6_000_000_000, 8_000_000, 2_000_000),
            name=f"local{odd}",
        )(recv_gate, at, far(text_gate), *map(far, (conv, edge, inputs, outputs, edge_p, edge_p, cum, by_head, size, skip_gain[None, :])), *more)

    even = rows_own(0, ())
    entries, bound = call(
        scan_kernel,
        (struct(G * N, GW), near(8, LANES, dtype=f32)),
        (1,),
        [vmem, vmem],
        [hbm, vmem],
        scratch=[pltpu.VMEM((G * N, GW), f32), pltpu.VMEM((G * N, GW), bf16), sems((4,))],
        est=cost(2 * 512 * 512 * 128, 1_200_000),
        name="scan",
    )(states, kept(even[3]))
    entry = kept(exchange(entries))
    odds = rows_own(1, (bound,))

    return call(
        final_kernel,
        struct(TOK, E),
        (1,),
        [vmem, vmem] + [hbm] * 7,
        hbm,
        scratch=[pltpu.VMEM((1, E), f32), pltpu.VMEM((G, TOK, N), bf16), pltpu.VMEM((G, TOK, GW), bf16), pltpu.VMEM((G, TOK, GW), bf16),
                 pltpu.VMEM((TOK, E), bf16), pltpu.VMEM((G * N, GW), f32), pltpu.VMEM((2, TOK, GW), f32),
                 sems(()), sems((2,)), sems((G,)), sems((G,)), sems((G,))],
        est=cost(2 * 256 * 64 * 4096, 11_000_000),
        name="final",
    )(kept(bound), entry, far(norm_gain[None, :]), *map(far, (even[2], odds[2], even[0], even[1], odds[0], odds[1])))


def solution(mesh):
    rows = P(("dp", "ctx"), None)
    specs = (rows,) * 8 + (P("dp"),) * 2 + (P(),) * 6
    return jax.shard_map(shards, mesh=mesh, in_specs=specs, out_specs=rows, check_vma=False)
```

```python
import functools

import jax
import jax.numpy as jnp
from jax import lax
from jax.experimental import pallas as pl
from jax.experimental.pallas import tpu as pltpu
from jax.sharding import PartitionSpec as P

H = 64
P_SIZE = 64
N = 64
G = 8
SPAN = 128
KCONV = 4
E = 4096
TOK = 256
TILE = 64
DEVS = 64
GW = E // G
PW = 2 * G * N
EDGE = 16
LANES = 128
QUART = 4
V_AT, P_AT, S_AT = 0, 1024, 1280
CHUNK = 1408
G_CHUNK = 1024
RIM_W = 1024
STATE_W = GW + LANES

f32 = jnp.float32
bf16 = jnp.bfloat16
MIB = 1024 * 1024
VMEM_MIB = 32


def cost(flops, size, trans=0):
    return pl.CostEstimate(flops=flops, bytes_accessed=size, transcendentals=trans)


def whole(shape):
    return pl.BlockSpec(shape, lambda *_: (0,) * len(shape))


def group_cols(g):
    return pl.ds(pl.multiple_of(g * GW, GW), GW)


def iota(shape, dim):
    return lax.broadcasted_iota(jnp.int32, shape, dim)


def dot(a, b):
    return jnp.dot(a, b, preferred_element_type=f32)


def dot_rows(a, b):
    return lax.dot_general(a, b, (((0,), (0,)), ((), ())), preferred_element_type=f32)


def dot_cols(a, b):
    return lax.dot_general(a, b, (((1,), (1,)), ((), ())), preferred_element_type=f32)


def dot_whole(a, b):
    high = b.astype(bf16)
    low = (b - high.astype(f32)).astype(bf16)
    return dot(jnp.concatenate([a, a], axis=1), jnp.concatenate([high, low], axis=0))


def silu(x):
    half = 0.5 * x
    return half + half * jnp.tanh(half)


def split2(x):
    high = x.astype(bf16)
    low = (x - high.astype(f32)).astype(bf16)
    return jnp.where(iota(x.shape, 1) < H, high.astype(f32), low.astype(f32)).astype(bf16)


def expander(group):
    head = iota((LANES, GW), 0) & (H - 1)
    col = group * (H // G) + (iota((LANES, GW), 1) >> 6)
    return jnp.where(head == col, 1.0, 0.0).astype(bf16)


def slot_keys(pos_ref):
    dev = lax.axis_index("ctx")
    row = pos_ref[pl.ds(dev // 2, 1), :]
    other = pltpu.roll(row, 64, 1)
    lane = iota((1, LANES), 1)
    own = jnp.where((lane >> 6) == lax.rem(dev, 2), row, other)
    key = (own >> 8) * 8 + (lane & 1) * QUART + (lane >> 6)
    keys = jnp.concatenate([key, key + 2], axis=1)
    return jnp.where(iota((DEVS * 8, 2 * LANES), 0) == keys, 1.0, 0.0).astype(bf16)


def quarters(ref, width, low, count):
    return jnp.concatenate([ref[:, b * width + low : b * width + low + count] for b in range(QUART)], axis=0)


def pack_kernel(
    pos_hbm, step_hbm, val_hbm, proj_hbm, out_hbm,
    pos_ref, step_ref, val_ref, proj_ref, out_ref, in_sem, out_sem,
):
    pairs = ((pos_hbm, pos_ref), (step_hbm, step_ref), (proj_hbm, proj_ref), (val_hbm, val_ref))
    loads = [pltpu.make_async_copy(src, dst, in_sem.at[i]) for i, (src, dst) in enumerate(pairs)]
    for load in loads:
        load.start()
    loads[0].wait()
    pick = slot_keys(pos_ref)
    loads[1].wait()
    step = step_ref[...]
    out_ref[:, S_AT:] = dot(pick[:, :TILE], jnp.concatenate([step, step], axis=1)).astype(bf16)
    loads[2].wait()
    out_ref[:, P_AT:S_AT] = dot(pick, quarters(proj_ref, 256, 0, 256)).astype(bf16)
    loads[3].wait()
    stores = []
    for i, (low, high) in enumerate(((P_AT, CHUNK), (0, GW), (GW, 2 * GW))):
        if i:
            out_ref[:, low:high] = dot(pick, quarters(val_ref, 1024, low, GW)).astype(bf16)
        store = pltpu.make_async_copy(out_ref.at[:, low:high], out_hbm.at[:, low:high], out_sem.at[i])
        store.start()
        stores.append(store)
    for store in stores:
        store.wait()


def gate_kernel(pos_ref, gate_ref, at_ref, step_ref, slot_ref, out_ref):
    pick = slot_keys(pos_ref)
    for low in (0, GW):
        out_ref[:, low : low + GW] = dot(pick, quarters(gate_ref, 1024, low, GW)).astype(bf16)


def rim_kernel(slot_ref, recv_ref, val_ref, proj_ref, out_ref):
    count = KCONV - 1
    slots = [slot_ref[i] for i in range(count)]
    starts = [jnp.maximum(k, 0) * QUART for k in slots]
    rows = [recv_ref[pl.ds(pl.multiple_of((k >> 4) * 16, 16), 16), :] for k in starts]
    rows = jnp.concatenate(rows, axis=0)
    row, col = iota((EDGE, 16 * count), 0), iota((EDGE, 16 * count), 1)
    at = jnp.full((EDGE, 16 * count), -16, jnp.int32)
    taken = jnp.full((EDGE, 1), -1, jnp.int32)
    for i, k in enumerate(starts):
        at = jnp.where(row == EDGE - count + i, 16 * i + (k & 15), at)
        taken = jnp.where(iota((EDGE, 1), 0) == EDGE - count + i, slots[i], taken)
    blocks, proj = [], []
    for b in range(QUART):
        place = jnp.where(col == at + b, 1.0, 0.0).astype(bf16)
        tile = dot(place, rows[:, V_AT:P_AT])
        text = val_ref[:, b * RIM_W : (b + 1) * RIM_W].astype(f32)
        blocks.append(jnp.where(taken >= 0, tile, text))
        tile = dot(place, rows[:, P_AT:S_AT])
        text = proj_ref[:, b * 256 : (b + 1) * 256].astype(f32)
        proj.append(jnp.where(taken >= 0, tile, text))
    blocks.append(jnp.concatenate(proj, axis=1))
    out = blocks[0]
    row = iota((EDGE, RIM_W), 0)
    for i, block in enumerate(blocks):
        out = jnp.where((row >= i * count) & (row < (i + 1) * count), pltpu.roll(block, (i + 1) * count, 0), out)
    out_ref[...] = out.astype(bf16)


def rim_rows(rim, block):
    return pltpu.roll(rim, EDGE - (block + 1) * (KCONV - 1), 0)[EDGE - 8 :]


def placement(at_ref):
    return jnp.where(iota((TOK, LANES), 0) == at_ref[...], 1.0, 0.0).astype(bf16)


def spread_out(recv, wide_ref):
    for k in range(recv.shape[1] // LANES):
        wide_ref[k] = recv[:, k * LANES : (k + 1) * LANES].astype(f32)


def quarter_rows(wide_ref, b, count):
    rows = [wide_ref[k, pl.ds(b, 2 * DEVS, stride=QUART), :] for k in range(count)]
    return jnp.concatenate(rows, axis=1).astype(bf16)


def conv_chunk(x, before, weights, bias):
    ext = jnp.concatenate([before, x], axis=0)
    total = bias + weights[KCONV - 1 : KCONV, :] * x
    for back in range(1, KCONV):
        total = total + weights[KCONV - 1 - back : KCONV - back, :] * pltpu.roll(ext, back, 0)[8:]
    return silu(total).astype(bf16)


CHUNK_ROWS = 64


def conv_columns(tile_ref, text_ref, taken_ref, cols, weights, bias, use):
    before = jnp.zeros((8, LANES), f32)
    for low in range(0, TOK, CHUNK_ROWS):
        rows = slice(low, low + CHUNK_ROWS)
        x = jnp.where(taken_ref[rows, :] > 0, tile_ref[rows, cols], text_ref[rows, cols].astype(f32))
        use(rows, x, conv_chunk(x, before, weights, bias))
        before = x[CHUNK_ROWS - 8 :]


def softplus(v):
    return jnp.maximum(v, 0.0) + jnp.log1p(jnp.exp(-jnp.abs(v)))


def three(x):
    a = x.astype(bf16)
    left = x - a.astype(f32)
    b = left.astype(bf16)
    return a, b, (left - b.astype(f32)).astype(bf16)


def order(i):
    return lax.rem(i, G // 2) * 2 + i // (G // 2)


def place_kernel(
    recv_hbm, val_hbm, proj_hbm, at_hbm, step_hbm, w_hbm, b_hbm, sbias_hbm, dlog_hbm,
    conv_hbm, in_hbm, out_hbm, state_ref, cum_ref, size_ref, total_ref, hv_ref, hp_ref, we_ref, wk_ref, bk_ref,
    at_ref, step_ref, w_ref, b_ref, sbias_ref, dlog_ref,
    recv_ref, val_ref, proj_ref, conv_ref, in_ref, out_ref, place_scr, taken_scr, wide_scr, tail_scr,
    tile_scr, weight_scr, part_scr, turned_scr, small_sem, recv_sem, val_sem, proj_sem, conv_sem, bc_sem,
):
    def load(i):
        cols = group_cols(order(i))
        return pltpu.make_async_copy(val_hbm.at[:, cols], val_ref.at[:, cols], val_sem.at[i])

    def store(i):
        cols = group_cols(order(i))
        return pltpu.make_async_copy(conv_ref.at[:, cols], conv_hbm.at[:, cols], conv_sem.at[i])

    def arrived(i, low, high):
        return pltpu.make_async_copy(recv_hbm.at[:, low:high], recv_ref.at[:, low:high], recv_sem.at[i])

    load_proj = pltpu.make_async_copy(proj_hbm, proj_ref, proj_sem)
    pieces = [arrived(0, P_AT, CHUNK), arrived(1, 0, GW), arrived(2, GW, 2 * GW)]
    store_bc = [
        pltpu.make_async_copy(src, dst, bc_sem.at[i])
        for i, (src, dst) in enumerate(((in_ref, in_hbm), (out_ref, out_hbm)))
    ]
    pairs = (
        (at_hbm, at_ref), (w_hbm, w_ref), (b_hbm, b_ref), (step_hbm, step_ref), (sbias_hbm, sbias_ref), (dlog_hbm, dlog_ref),
    )
    small = [pltpu.make_async_copy(src, dst, small_sem.at[i]) for i, (src, dst) in enumerate(pairs)]
    small[0].start()
    pieces[0].start()
    load_proj.start()
    for load_small in small[1:]:
        load_small.start()
    pieces[1].start()
    for i in range(G // 2):
        load(i).start()
    pieces[2].start()
    for i in range(G // 2, G):
        load(i).start()

    def first():
        small[0].wait()
        place_scr[...] = placement(at_ref)
        taken_scr[...] = dot(place_scr[...], jnp.ones((LANES, LANES), bf16))
        for load_small in small[1:]:
            load_small.wait()
        wk_ref[...] = w_ref[...]
        bk_ref[...] = b_ref[...]
        pieces[0].wait()
        spread_out(recv_ref[:, P_AT:], wide_scr)
        load_proj.wait()
        for b in range(QUART):
            tile_scr[0, :, :256] = dot(place_scr[...], quarter_rows(wide_scr, b, 2))
            for half in range(2):
                pair = b * 2 + half
                cols = slice(pair * LANES, (pair + 1) * LANES)

                def use(rows, x, y, pair=pair, cols=cols):
                    if rows.start == 0:
                        hp_ref[:, cols] = x[:EDGE].astype(bf16)
                    if pair < G // 2:
                        in_ref[pair, rows, :] = y
                    else:
                        out_ref[pair - G // 2, rows, :] = y

                at = slice(E + pair * LANES, E + (pair + 1) * LANES)
                conv_columns(
                    tile_scr.at[0, :, half * LANES : (half + 1) * LANES], proj_ref.at[:, cols], taken_scr,
                    slice(None), w_ref[:, at], b_ref[:, at], use,
                )
        for copy in store_bc:
            copy.start()
        for pair in range(G // 2):
            turned = jnp.transpose(in_ref[pair].astype(f32))
            turned_scr[pair] = jnp.where(iota((LANES, TOK), 1) >= EDGE, turned, 0.0).astype(bf16)
        steps = wide_scr[2, pl.ds(0, 2 * DEVS, stride=QUART), :].astype(bf16)
        tile = dot(place_scr[...], steps)
        step = step_ref[...].astype(f32)
        step = jnp.where(taken_scr[...] > 0, tile, jnp.concatenate([step, step], axis=1))
        sbias, dlog = sbias_ref[...], dlog_ref[...]
        size = softplus(step + jnp.concatenate([sbias, sbias], axis=1))
        logs = -jnp.exp(jnp.concatenate([dlog, dlog], axis=1)) * size
        size_ref[...] = size
        lower = jnp.where(iota((SPAN, SPAN), 0) >= iota((SPAN, SPAN), 1), 1.0, 0.0).astype(bf16)
        cums = []
        for k in range(TOK // SPAN):
            parts = three(logs[k * SPAN : (k + 1) * SPAN])
            cums.append(dot(lower, parts[0]) + (dot(lower, parts[1]) + dot(lower, parts[2])))
        last = [c[SPAN - 1 : SPAN, :] for c in cums]
        for k, c in enumerate(cums):
            rows = slice(k * SPAN, (k + 1) * SPAN)
            cum_ref[rows, :] = c
            left = last[k] - c
            if k == 0:
                left = left + last[1]
            tail_scr[rows, :] = split2(jnp.exp(left) * size[rows])
        total_ref[...] = jnp.broadcast_to(jnp.exp(last[0] + last[1]), total_ref.shape)

    first()
    for odd in range(2):
        pieces[1 + odd].wait()
        spread_out(recv_ref[:, odd * GW : (odd + 1) * GW], wide_scr)

        @pl.loop(0, G // 4)
        def _(two, odd=odd):
            for slot in range(2):
                load(odd * (G // 2) + 2 * two + slot).wait()
            for slot in range(2):
                pair = 2 * two + slot
                g = 2 * pair + odd
                tile_scr[slot] = dot(place_scr[...], quarter_rows(wide_scr, pair, GW // LANES))
                weight_scr[slot] = dot(tail_scr[...], expander(g))
                we_ref[:, group_cols(g)] = weight_scr[slot, :EDGE, :]
                for k in range(GW // LANES):
                    cols = pl.ds(pl.multiple_of(g * GW + k * LANES, LANES), LANES)
                    part = slice(k * LANES, (k + 1) * LANES)

                    def use(rows, x, y, cols=cols, part=part, slot=slot):
                        if rows.start == 0:
                            hv_ref[:, cols] = x[:EDGE].astype(bf16)
                        conv_ref[rows, cols] = y
                        weight = weight_scr[slot, rows, part]
                        part_scr[slot, rows, part] = (y.astype(f32) * weight).astype(bf16)

                    conv_columns(
                        tile_scr.at[slot, :, part], val_ref.at[:, cols], taken_scr, slice(None),
                        w_ref[:, cols], b_ref[:, cols], use,
                    )
            for slot in range(2):
                pair = 2 * two + slot
                rows = pl.ds(pl.multiple_of((2 * pair + odd) * N, N), N)
                b_g = turned_scr[pair, odd * N : (odd + 1) * N, :]
                state_ref[rows, :] = dot(b_g, part_scr[slot])
            for slot in range(2):
                store(odd * (G // 2) + 2 * two + slot).start()

    for copy in store_bc:
        copy.wait()
    for i in range(G):
        store(i).wait()


def power8(s):
    s2 = s * s
    s4 = s2 * s2
    s8 = s4 * s4
    return jnp.where(s < 0, -s8, s8).astype(bf16)


def root8(code):
    code = code.astype(f32)
    size = jnp.exp(0.125 * jnp.log(jnp.abs(code)))
    return jnp.where(code < 0, -size, size)


FLOOR = 1e-30


def edge_kernel(
    rim_ref, hv_ref, hp_ref, w_ref, b_ref, we_ref, total_ref, state_ref,
    send_ref, conv_ref, proj_ref,
    full_scr,
):
    rim = rim_ref[...].astype(f32)
    befores = [rim_rows(rim, i) for i in range((E + PW) // RIM_W)]

    def conv(x_ref, at, columns):
        i, low = columns.start // RIM_W, columns.start % RIM_W
        before = befores[i][:, low : low + columns.stop - columns.start]
        return conv_chunk(x_ref[:, at].astype(f32), before, w_ref[:, columns], b_ref[:, columns])

    p = [conv(hp_ref, slice(k * LANES, (k + 1) * LANES), slice(E + k * LANES, E + (k + 1) * LANES)) for k in range(PW // LANES)]
    p = jnp.concatenate(p, axis=1)
    proj_ref[...] = p
    top = jnp.zeros((8, LANES), f32)
    for g in range(G):
        b_g = p[:, g * N : (g + 1) * N]
        cols = slice(g * GW, (g + 1) * GW)
        y = conv(hv_ref, cols, cols)
        conv_ref[:, cols] = y
        rows = slice(g * N, (g + 1) * N)
        state = state_ref[rows, :] + dot_rows(b_g, (y.astype(f32) * we_ref[:, cols]).astype(bf16))
        full_scr[rows, :] = state
        sums = jnp.abs(state[:8])
        for k in range(8, N, 8):
            sums = sums + jnp.abs(state[k : k + 8])
        top = top + dot_cols(sums.astype(bf16), expander(g))
    top = jnp.maximum(jnp.sum(top, axis=0, keepdims=True) * 2.0**-14, FLOOR).astype(bf16).astype(f32)
    top = jnp.where(iota((8, LANES), 1) < H, top, 0.0)
    for g in range(G):
        back = 1.0 / dot(top.astype(bf16), expander(g))[:1]
        for low in range(g * N, (g + 1) * N, 32):
            send_ref[low : low + 32, :GW] = power8(full_scr[low : low + 32, :] * back)
    decay = split2(total_ref[...]).astype(f32)
    odd = (iota((8, LANES), 0) & 1) == 1
    side = jnp.where(odd, top, decay).astype(bf16)
    side = jnp.concatenate([side, side], axis=0)
    for low in range(0, G * N, 16):
        send_ref[low : low + 16, GW:] = side


def scan_kernel(recv_ref, after_ref, out_hbm, bound_ref, side_scr, out_ref, out_sem):
    dev = lax.axis_index("ctx")
    side_scr[...] = dot(recv_ref[:, GW:], expander(dev // 8))

    def code(state, bound):
        return state * (1.0 / jnp.maximum(bound, FLOOR))

    def two(i, carry):
        rows = pl.ds(pl.multiple_of(i * 16, 16), 16)
        first, bound, own = carry
        state = root8(recv_ref[rows, :GW])
        side = side_scr[rows, :]
        second = side[:1] * first + state[:8] * side[1:2]
        second_bound = side[:1] * bound + side[1:2]
        out_ref[rows, :] = power8(jnp.concatenate([code(first, bound), code(second, second_bound)], axis=0))
        part = recv_ref[rows, GW:].astype(f32)
        part = part + pltpu.roll(part, H, 1)
        own = jnp.where(2 * i < dev, part[:1] * own + part[1:2], own)
        own = jnp.where(2 * i + 1 < dev, part[8:9] * own + part[9:10], own)
        return (
            side[8:9] * second + state[8:] * side[9:10],
            side[8:9] * second_bound + side[9:10],
            own,
        )

    zeros = (jnp.zeros((8, GW), f32), jnp.zeros((1, GW), f32), jnp.zeros((1, LANES), f32))
    carry, stores = zeros, []
    for part in range(4):
        carry = lax.fori_loop(part * DEVS // 8, (part + 1) * DEVS // 8, two, carry, unroll=8)
        rows = slice(part * DEVS * 2, (part + 1) * DEVS * 2)
        store = pltpu.make_async_copy(out_ref.at[rows, :], out_hbm.at[rows, :], out_sem.at[part])
        store.start()
        stores.append(store)
    bound_ref[...] = jnp.broadcast_to(carry[2], bound_ref.shape)
    for store in stores:
        store.wait()


def local_kernel(
    odd, recv_ref, at_ref, gate_ref, conv_ref, edge_ref, in_ref, out_ref, ein_ref, eout_ref,
    cum_ref, cumt_ref, size_ref, skip_ref, *rest,
):
    mix_out, scale_out, query_ref, token_ref, place_scr, taken_scr, wide_scr, gate_scr, weighted_scr, first_scr, mix_ref, scale_ref = rest[-12:]
    token_ref[...] = jnp.zeros_like(token_ref)
    i = pl.program_id(0)
    g = 2 * i + odd

    @pl.when(i == 0)
    def _():
        place_scr[...] = placement(at_ref)
        taken_scr[...] = dot(place_scr[...], jnp.ones((LANES, LANES), bf16))
        spread_out(recv_ref[...], wide_scr)

    def patched(edge, rest):
        return jnp.concatenate([edge, rest[EDGE:]], axis=0)

    half = slice(odd * N, (odd + 1) * N)
    b_g = patched(ein_ref[:, half], in_ref[0, :, half])
    c_g = patched(eout_ref[:, half], out_ref[0, :, half])
    query_ref[0] = c_g
    cum = cum_ref[...]
    spread = expander(g)
    skip = skip_ref[...]
    skip = jnp.broadcast_to(jnp.concatenate([skip, skip], axis=1), (8, LANES))
    skip = dot(split2(skip), spread)[:1]
    last = cum[SPAN - 1 : SPAN, :]
    upto = jnp.concatenate([cum[:SPAN], cum[SPAN:] + last], axis=0)
    scale_ref[...] = dot(split2(jnp.exp(upto)), spread)
    weighted_scr[...] = dot(split2(size_ref[...]), spread)
    gate_scr[...] = dot(place_scr[...], quarter_rows(wide_scr, i, GW // LANES))
    own = pltpu.roll(cum, lax.rem(LANES - g * (H // G), LANES), 1)
    for low in range(0, TOK, 32):
        rows = slice(low, low + 32)
        taken = taken_scr[rows, :] > 0
        for k in range(GW // LANES):
            cols = slice(k * LANES, (k + 1) * LANES)
            gate = silu(jnp.where(taken, gate_scr[rows, cols], gate_ref[rows, cols].astype(f32)))
            gate_scr[rows, cols] = gate
            scale_out[rows, cols] = (scale_ref[rows, cols] * gate).astype(bf16)
            x = conv_ref[rows, cols]
            if low == 0:
                x = patched(edge_ref[:, cols], x)
            x = x.astype(f32)
            weighted_scr[rows, cols] = weighted_scr[rows, cols] * x
            mix_ref[rows, cols] = skip[:, cols] * x
    tail = dot(split2(jnp.exp(last - cum[:SPAN])), spread)
    inner = dot(split2(jnp.exp(cum[SPAN:])), spread)
    state = dot_rows(b_g[:SPAN], (weighted_scr[:SPAN] * tail).astype(bf16))
    first_scr[...] = dot_whole(c_g[SPAN:], state) * inner
    causal = iota((SPAN, SPAN), 0) >= iota((SPAN, SPAN), 1)
    lane = iota((SPAN, LANES), 1)
    for k in range(TOK // SPAN):
        rows = slice(k * SPAN, (k + 1) * SPAN)
        scores = jnp.where(causal, dot_cols(c_g[rows], b_g[rows]), 0.0)
        for pair in range(H // G // 2):
            kernels = []
            for head in (2 * pair, 2 * pair + 1):
                apart = own[rows, head : head + 1] - cumt_ref[0, head : head + 1, rows]
                kernels.append((jnp.exp(jnp.minimum(apart, 0.0)) * scores).astype(bf16))
            cols = slice(pair * LANES, (pair + 1) * LANES)
            w = weighted_scr[rows, cols]
            low = jnp.where(lane < P_SIZE, w, 0.0).astype(bf16)
            high = jnp.where(lane < P_SIZE, 0.0, w).astype(bf16)
            mixed = dot(jnp.concatenate(kernels, axis=1), jnp.concatenate([low, high], axis=0))
            mixed = mixed + mix_ref[rows, cols]
            if k == 1:
                mixed = mixed + first_scr[:, cols]
            mix_out[rows, cols] = (mixed * gate_scr[rows, cols]).astype(bf16)


def final_kernel(
    bound_ref, entry_ref, gain_hbm, qe_hbm, qo_hbm, me_hbm, se_hbm, mo_hbm, so_hbm, out_hbm,
    gain_ref, query_ref, mix_ref, scale_ref, out_ref, entry_scr, part_scr, gain_sem, query_sem, mix_sem, scale_sem, out_sem,
):
    gain = pltpu.make_async_copy(gain_hbm, gain_ref, gain_sem)
    queries = [
        pltpu.make_async_copy(src, query_ref.at[i * G // 2 : (i + 1) * G // 2], query_sem.at[i])
        for i, src in enumerate((qe_hbm, qo_hbm))
    ]
    mixes, scales, stores = [], [], []
    for i in range(G):
        cols = slice(i % (G // 2) * GW, (i % (G // 2) + 1) * GW)
        mix, scale = (me_hbm, se_hbm) if i < G // 2 else (mo_hbm, so_hbm)
        mixes.append(pltpu.make_async_copy(mix.at[:, cols], mix_ref.at[i], mix_sem.at[i]))
        scales.append(pltpu.make_async_copy(scale.at[:, cols], scale_ref.at[i], scale_sem.at[i]))
        g = i % (G // 2) * 2 + i // (G // 2)
        cols = slice(g * GW, (g + 1) * GW)
        stores.append(pltpu.make_async_copy(out_ref.at[:, cols], out_hbm.at[:, cols], out_sem.at[i]))
    for load in (*queries, gain, *(c for pair in zip(mixes, scales) for c in pair)):
        load.start()
    bound = split2(jnp.maximum(bound_ref[...], FLOOR))
    for g in range(G):
        rows = slice(g * N, (g + 1) * N)
        entry_scr[rows, :] = root8(entry_ref[rows, :]) * dot(bound, expander(g))[:1]
    for load in (*queries, gain):
        load.wait()
    for i in range(G):
        g = i % (G // 2) * 2 + i // (G // 2)
        if i % 2 == 0:
            for load in (*mixes[i : i + 2], *scales[i : i + 2]):
                load.wait()
        slot = i % 2
        own = dot_whole(query_ref[i], entry_scr[g * N : (g + 1) * N, :])
        squares = jnp.zeros((TOK, LANES), f32)
        for k in range(GW // LANES):
            cols = slice(k * LANES, (k + 1) * LANES)
            part = mix_ref[i, :, cols].astype(f32) + scale_ref[i, :, cols].astype(f32) * own[:, cols]
            part_scr[slot, :, cols] = part
            squares = squares + part * part
        high = squares.astype(bf16)
        low = (squares - high.astype(f32)).astype(bf16)
        mean = dot(jnp.concatenate([high, low], axis=1), jnp.ones((2 * LANES, LANES), bf16)) * (1.0 / GW)
        mean = lax.rsqrt(mean + 1e-05)
        for k in range(GW // LANES):
            cols = slice(k * LANES, (k + 1) * LANES)
            at = slice(g * GW + k * LANES, g * GW + (k + 1) * LANES)
            out_ref[:, at] = (part_scr[slot, :, cols] * mean * gain_ref[:, at]).astype(bf16)
        if i % 2 == 1:
            stores[i - 1].start()
            stores[i].start()
    for store in stores:
        store.wait()


def call(kernel, outs, grid, in_specs, out_specs, scratch=(), est=None, name=None, vmem=VMEM_MIB, alias=None):
    return pl.pallas_call(
        kernel,
        out_shape=outs,
        grid_spec=pltpu.PrefetchScalarGridSpec(
            num_scalar_prefetch=0,
            grid=grid,
            in_specs=in_specs,
            out_specs=out_specs,
            scratch_shapes=scratch,
        ),
        compiler_params=pltpu.CompilerParams(vmem_limit_bytes=vmem * MIB),
        input_output_aliases=alias or {},
        cost_estimate=est,
        name=name,
    )


def struct(*shape, dtype=bf16):
    return pltpu.HBM(shape, dtype)


def near(*shape, dtype=bf16):
    return pltpu.VMEM(shape, dtype)


def far(a):
    return pltpu.with_memory_space_constraint(a, pltpu.HBM)


def kept(a):
    return pltpu.with_memory_space_constraint(a, pltpu.VMEM)


def exchange(rows):
    return lax.all_to_all(rows, "ctx", split_axis=0, concat_axis=0, tiled=True)


def twice(a):
    return jnp.concatenate([a, a], axis=-1)


def shards(
    text_values, text_gate, text_proj, text_step, tile_values, tile_gate, tile_proj, tile_step,
    tile_position, tile_count, conv_weight, conv_bias, step_bias, decay_log, skip_gain, norm_gain,
):
    device = lax.axis_index("ctx")
    scalar = pl.BlockSpec(memory_space=pltpu.SMEM)

    hbm = pl.BlockSpec(memory_space=pl.ANY)
    vmem = pl.BlockSpec(memory_space=pltpu.VMEM)
    sems = pltpu.SemaphoreType.DMA
    positions = tile_position.reshape(32, LANES)
    packed = call(
        pack_kernel,
        struct(DEVS * 8, CHUNK),
        (1,),
        [hbm] * 4,
        hbm,
        scratch=[pltpu.VMEM((32, LANES), jnp.int32), pltpu.VMEM((TILE, H), bf16), pltpu.VMEM((TILE, E), bf16),
                 pltpu.VMEM((TILE, PW), bf16), pltpu.VMEM((DEVS * 8, CHUNK), bf16), sems((4,)), sems((3,))],
        est=cost(2 * 512 * 256 * CHUNK, 3_000_000),
        name="pack",
    )(far(positions), far(tile_step), far(tile_values), far(tile_proj))
    recv = exchange(packed)
    position = tile_position.reshape(DEVS, TILE)
    ids = jnp.arange(TILE, dtype=jnp.int32)
    landing = ((position >> 8) == device) & (ids[None, :] < tile_count[:, None])
    local = jnp.where(landing, position & (TOK - 1), -1)
    at = jnp.max(local.reshape(DEVS, TILE // 2, 2), axis=1).reshape(1, 2 * DEVS)
    ends = jnp.arange(TOK - KCONV + 1, TOK)[:, None]
    rim_slot = jnp.max(jnp.where(at == ends, jnp.arange(2 * DEVS)[None, :], -1), axis=1)
    at = far(at)
    steps = far(text_step)
    gates = call(
        gate_kernel,
        struct(DEVS * 8, G_CHUNK),
        (1,),
        [whole((32, LANES)), whole((TILE, E)), hbm, hbm, hbm],
        whole((DEVS * 8, G_CHUNK)),
        est=cost(2 * 512 * 256 * G_CHUNK, 2_000_000),
        name="gates",
    )(far(positions), far(tile_gate), at, steps, rim_slot)
    gates, recv = lax.optimization_barrier((gates, recv))
    recv = kept(recv)
    recv_gate = exchange(gates)

    bias = conv_bias[None, :]

    recv_spec = whole((DEVS * 8, CHUNK))
    at_spec = whole((1, 2 * DEVS))
    rim = call(
        rim_kernel,
        struct(EDGE, RIM_W),
        (1,),
        [scalar, vmem,
         pl.BlockSpec((EDGE, E), lambda i: (TOK // EDGE - 1, 0)),
         pl.BlockSpec((EDGE, PW), lambda i: (TOK // EDGE - 1, 0))],
        whole((EDGE, RIM_W)),
        est=cost(2 * 16 * 48 * 5120, 3_000_000),
        name="rim",
    )(rim_slot, recv, far(text_values), far(text_proj))
    rim = lax.ppermute(rim, "ctx", [(i, i + 1) for i in range(DEVS - 1)])

    conv, inputs, outputs, state, cum, size, total, head_v, head_p, tail, taps, shift = call(
        place_kernel,
        (
            struct(TOK, E), struct(G // 2, TOK, LANES), struct(G // 2, TOK, LANES), near(G * N, GW, dtype=f32),
            struct(TOK, LANES, dtype=f32), struct(TOK, LANES, dtype=f32),
            near(8, LANES, dtype=f32),
            near(EDGE, E), near(EDGE, PW), near(EDGE, E, dtype=f32),
            near(KCONV, E + PW, dtype=f32), near(1, E + PW, dtype=f32),
        ),
        (1,),
        [hbm] * 9,
        [hbm, hbm, hbm, vmem, whole((TOK, LANES)), whole((TOK, LANES)), vmem, vmem, vmem, vmem, vmem, vmem],
        scratch=[pltpu.VMEM((1, 2 * DEVS), jnp.int32), pltpu.VMEM((TOK, H), bf16), pltpu.VMEM((KCONV, E + PW), f32),
                 pltpu.VMEM((1, E + PW), f32), pltpu.VMEM((1, H), f32), pltpu.VMEM((1, H), f32),
                 pltpu.VMEM((DEVS * 8, CHUNK), bf16), pltpu.VMEM((TOK, E), bf16), pltpu.VMEM((TOK, PW), bf16),
                 pltpu.VMEM((TOK, E), bf16), pltpu.VMEM((G // 2, TOK, LANES), bf16), pltpu.VMEM((G // 2, TOK, LANES), bf16),
                 pltpu.VMEM((TOK, LANES), bf16), pltpu.VMEM((TOK, LANES), f32),
                 pltpu.VMEM((GW // LANES, DEVS * 8, LANES), f32), pltpu.VMEM((TOK, LANES), bf16),
                 pltpu.VMEM((2, TOK, GW), f32), pltpu.VMEM((2, TOK, GW), f32), pltpu.VMEM((2, TOK, GW), bf16),
                 pltpu.VMEM((G // 2, LANES, TOK), bf16), sems((6,)), sems((3,)), sems((G,)), sems(()), sems((G,)), sems((2,))],
        est=cost(2 * 256 * 512 * 5120, 10_000_000, 1_300_000),
        name="place",
    )(recv, far(text_values), far(text_proj), at, steps, far(conv_weight), far(bias),
      far(step_bias[None, :]), far(decay_log[None, :]))

    send, edge, edge_p = call(
        edge_kernel,
        (struct(G * N, STATE_W), struct(EDGE, E), struct(EDGE, PW)),
        (1,),
        [vmem] * 8,
        [whole((G * N, STATE_W)), whole((EDGE, E)), whole((EDGE, PW))],
        scratch=[pltpu.VMEM((G * N, GW), f32)],
        est=cost(2 * 64 * 16 * 4096, 2_000_000, 100_000),
        name="edge",
    )(kept(rim), kept(head_v), kept(head_p), kept(taps), kept(shift), kept(tail), kept(total), kept(state))
    send, recv_gate = lax.optimization_barrier((send, recv_gate))
    states = kept(exchange(send))

    by_head = cum[:, :H].T.reshape(G, H // G, TOK)

    def rows_own(odd, more):
        per_pair = pl.BlockSpec((1, TOK, LANES), lambda i: (i, 0, 0))
        cols = pl.BlockSpec((TOK, GW), lambda i: (0, 2 * i + odd))
        own_cols = pl.BlockSpec((TOK, GW), lambda i: (0, i))
        anywhere = pl.BlockSpec(memory_space=pl.ANY)
        return call(
            functools.partial(local_kernel, odd),
            (struct(TOK, E // 2), struct(TOK, E // 2), struct(G // 2, TOK, N), near(8, LANES, dtype=f32)),
            (G // 2,),
            [pl.BlockSpec((DEVS * 8, GW), lambda i: (0, odd)), at_spec, cols, cols,
             pl.BlockSpec((EDGE, GW), lambda i: (0, 2 * i + odd)), per_pair, per_pair,
             pl.BlockSpec((EDGE, LANES), lambda i: (0, i)), pl.BlockSpec((EDGE, LANES), lambda i: (0, G // 2 + i)),
             whole((TOK, LANES)), pl.BlockSpec((1, H // G, TOK), lambda i: (2 * i + odd, 0, 0)),
             whole((TOK, LANES)), whole((1, H))] + [anywhere] * len(more),
            [own_cols, own_cols, pl.BlockSpec((1, TOK, N), lambda i: (i, 0, 0)), whole((8, LANES))],
            scratch=[pltpu.VMEM((TOK, LANES), bf16), pltpu.VMEM((TOK, LANES), f32),
                     pltpu.VMEM((GW // LANES, DEVS * 8, LANES), f32), pltpu.VMEM((TOK, GW), f32), pltpu.VMEM((TOK, GW), f32), pltpu.VMEM((SPAN, GW), f32),
                     pltpu.VMEM((TOK, GW), f32), pltpu.VMEM((TOK, GW), f32)],
            est=cost(6_000_000_000, 8_000_000, 2_000_000),
            name=f"local{odd}",
        )(recv_gate, at, far(text_gate), *map(far, (conv, edge, inputs, outputs, edge_p, edge_p, cum, by_head, size, skip_gain[None, :])), *more)

    even = rows_own(0, ())
    entries, bound = call(
        scan_kernel,
        (struct(G * N, GW), near(8, LANES, dtype=f32)),
        (1,),
        [vmem, vmem],
        [hbm, vmem],
        scratch=[pltpu.VMEM((G * N, GW), f32), pltpu.VMEM((G * N, GW), bf16), sems((4,))],
        est=cost(2 * 512 * 512 * 128, 1_200_000),
        name="scan",
    )(states, kept(even[3]))
    entry = kept(exchange(entries))
    odds = rows_own(1, (bound,))

    return call(
        final_kernel,
        struct(TOK, E),
        (1,),
        [vmem, vmem] + [hbm] * 7,
        hbm,
        scratch=[pltpu.VMEM((1, E), f32), pltpu.VMEM((G, TOK, N), bf16), pltpu.VMEM((G, TOK, GW), bf16), pltpu.VMEM((G, TOK, GW), bf16),
                 pltpu.VMEM((TOK, E), bf16), pltpu.VMEM((G * N, GW), f32), pltpu.VMEM((2, TOK, GW), f32),
                 sems(()), sems((2,)), sems((G,)), sems((G,)), sems((G,))],
        est=cost(2 * 256 * 64 * 4096, 11_000_000),
        name="final",
    )(kept(bound), entry, far(norm_gain[None, :]), *map(far, (even[2], odds[2], even[0], even[1], odds[0], odds[1])))


def solution(mesh):
    rows = P(("dp", "ctx"), None)
    specs = (rows,) * 8 + (P("dp"),) * 2 + (P(),) * 6
    return jax.shard_map(shards, mesh=mesh, in_specs=specs, out_specs=rows, check_vma=False)
```
